128 devices in a mesh: lon: 16 (over z, x_lo, core), lat: 8 (over x_hi, y).
Axes of the slice: x: 4 (x_hi: 2, x_lo: 2; x = x_hi * 2 + x_lo), y: 4, z: 4, core: 2. Of those that a mesh axis runs over, the one named last changes fastest.
Arguments:
- block_input: bfloat16 [2, 384, 384, 512], P(None, 'lat', 'lon'), may hold values from -6 to 6
- gain: float32 [512], replicated, may hold values from 0.25 to 1.75
- w_qkv: bfloat16 [512, 1536], replicated
- w_out: bfloat16 [512, 512], replicated, may hold values from -0.25 to 0.25
- w_dec: bfloat16 [512, 80], replicated, may hold values from -0.25 to 0.25
- g_points: bfloat16 [131072, 80], P(('lat', 'lon')), may hold values from -6 to 6
- slot_point: int32 [1024, 512], P(('lat', 'lon')), may hold values from 0 to 1023
- slot_cell: int32 [1024, 512], P(('lat', 'lon')), may hold values from 0 to 2303
- slot_weight: float32 [1024, 512], P(('lat', 'lon')), may hold values from 0.25 to 1
- pair_count: int32 [1024], P(('lat', 'lon')), may hold values from 128 to 512, as said below
Outputs:
- grad_x: bfloat16 [2, 384, 384, 512], P(None, 'lat', 'lon')
- grad_qkv: float32 [512, 1536], replicated
- grad_out: float32 [512, 512], replicated
- grad_dec: float32 [512, 80], replicated
- grad_gain: float32 [512], replicated
The draws below stay inside these ranges and needn't reach their ends.
Inputs may be any that keep to these rules, and one draw needn't show every extreme that they name: slot_point indexes the owner's 1024 points. slot_cell indexes the source's 2304 local cells. `pair_count`: every device sends exactly 512 live entries to at least one band.
All inputs are finite; a program needn't handle non-finite values.
Results may differ from the reference program's by a relative error of at most 0.02.
The reference program's roundings to bfloat16 on the way count: a program that leaves them out, or rounds other values in their place, can miss the bound.
Values may be sent and summed in bfloat16 or wider, within the bound.
A program may use at most 192 MiB of HBM per device.

```python
import jax
import jax.numpy as jnp
from jax import lax

D = 512
HEADS = 8
HD = 64
LEV = 2
WA = 6
WO = 12
C = 80
LAT_DEV = 48
LON_DEV = 24
G_DEV = 1024
CAP = 512
SHIFT = 6
WT = 144
TOK_DEV = 2304
NLAT = 384
NLON = 384
NPTS = 131072
N_LON = 16
N_LAT = 8


def draw_w_qkv(key, part):
    key = jax.random.fold_in(key, 7)
    weights = jax.random.normal(key, (D, 3 * D), jnp.float32) * D ** (-0.5)
    return weights.astype(jnp.bfloat16)


def draw_pair_count(key, part):
    key = jax.random.fold_in(key, 11)
    first, second = jax.random.split(key)
    devices = N_LAT * N_LON
    counts = jax.random.randint(first, (devices, N_LAT), CAP // 4, CAP + 1)
    where_full = jax.random.randint(second, (devices, 1), 0, N_LAT)
    counts = jnp.where(jnp.arange(N_LAT)[None, :] == where_full, CAP, counts)
    return counts.reshape(-1).astype(jnp.int32)


def touch_ends(drawn, rng, low, high):
    longest = drawn.shape.index(max(drawn.shape))
    spots = []
    for shift in (0, 1):
        where = [jax.random.randint(jax.random.fold_in(rng, axis), (), 0, length) for axis, length in enumerate(drawn.shape)]
        where[longest] = (where[longest] + shift) % drawn.shape[longest]
        spots.append(tuple(where))
    return drawn.at[spots[0]].set(low).at[spots[1]].set(high)


def shard_levels(key, dims, cuts, least, largest):
    def one(dim, parts):
        heights = jax.random.uniform(jax.random.fold_in(jax.random.fold_in(key, 6), dim), (parts,), jnp.float32, least / len(cuts), largest / len(cuts))
        return jnp.repeat(jnp.exp(heights), dims[dim] // parts).reshape((-1,) + (1,) * (len(dims) - dim - 1))

    level = one(*cuts[0])
    for cut in cuts[1:]:
        level = level * one(*cut)
    return level


def normal_values(key, extent, scale, reach, shards=(), dtype=jnp.bfloat16):
    result = jax.random.normal(key, extent, jnp.float32) * scale
    if len(shards) > 0:
        result = shard_levels(key, extent, shards, -0.22, 0.18) * result
    return jnp.clip(result, min=-reach, max=reach).astype(dtype)


def setup_inputs(seed: int = 0) -> dict:
    seeds = jax.random.split(jax.random.key(seed), 11)
    block_input = normal_values(seeds[0], (LEV, NLAT, NLON, D), 1.0, 6.0, ((1, 8), (2, 16)))
    gain = jnp.clip(1.0 + 0.15 * jax.random.normal(seeds[1], (D,), jnp.float32), 0.25, 1.75)
    w_qkv = draw_w_qkv(jax.random.fold_in(seeds[10], 71), 0)
    w_out = normal_values(seeds[3], (D, D), D ** -0.5, 0.25)
    w_dec = normal_values(seeds[4], (D, C), D ** -0.5, 0.25)
    g_points = normal_values(seeds[5], (NPTS, C), 1.0, 6.0, ((0, 128),))
    slot_point = touch_ends(jax.random.randint(seeds[6], (N_LAT * N_LON * N_LAT, CAP), 0, G_DEV), jax.random.fold_in(seeds[6], 1), 0, G_DEV - 1).astype(jnp.int32)
    slot_cell = touch_ends(jax.random.randint(seeds[7], (N_LAT * N_LON * N_LAT, CAP), 0, TOK_DEV), jax.random.fold_in(seeds[7], 1), 0, TOK_DEV - 1).astype(jnp.int32)
    slot_weight = jnp.clip(0.25 + 0.75 * jax.random.uniform(seeds[8], (N_LAT * N_LON * N_LAT, CAP), jnp.float32) ** shard_levels(seeds[8], (N_LAT * N_LON * N_LAT, CAP), ((0, 128),), -0.2, 0.2), 0.25, 1.0)
    pair_count = draw_pair_count(jax.random.fold_in(seeds[10], 71), 0)
    return dict(block_input=block_input, gain=gain, w_qkv=w_qkv, w_out=w_out, w_dec=w_dec, g_points=g_points, slot_point=slot_point, slot_cell=slot_cell, slot_weight=slot_weight, pair_count=pair_count)


def prod(form, left, right):
    return jnp.einsum(form, left.astype(jnp.float32), right.astype(jnp.float32))

def to_windows(tile):
    levels, lat_rows, lon_cols, width = tile.shape
    blocks = tile.reshape(levels, lat_rows // WA, WA, lon_cols // WO, WO, width).transpose(1, 3, 0, 2, 4, 5)
    return blocks.reshape(lat_rows // WA, lon_cols // WO, levels * WA * WO, width)

def from_windows(blocks):
    lat_blocks, lon_blocks, window, width = blocks.shape
    tile = blocks.reshape(lat_blocks, lon_blocks, LEV, WA, WO, width).transpose(2, 0, 3, 1, 4, 5)
    return tile.reshape(LEV, lat_blocks * WA, lon_blocks * WO, width)

def attend_forward(windows, gain, w_qkv, w_out):
    count, window, width = windows.shape
    inputs = windows.astype(jnp.float32)
    rscale = lax.rsqrt(lax.optimization_barrier(jnp.mean(inputs * inputs, -1, keepdims=True)) + 1e-06)
    normed = (inputs * rscale * gain).astype(jnp.bfloat16)
    qkv = jnp.dot(normed.reshape(count * window, width), w_qkv, preferred_element_type=jnp.float32)
    qkv = qkv.astype(jnp.bfloat16).reshape(count, window, 3, HEADS, HD)
    query, keys, values = (qkv[:, :, 0], qkv[:, :, 1], qkv[:, :, 2])
    scores = prod('wqhe,wkhe->whqk', query, keys) * HD ** (-0.5)
    probs = jax.nn.softmax(scores, -1)
    probs_b = probs.astype(jnp.bfloat16)
    attended = prod('whqk,wkhe->wqhe', probs_b, values).astype(jnp.bfloat16).reshape(count * window, width)
    hidden = (inputs.reshape(count * window, width) + jnp.dot(attended, w_out, preferred_element_type=jnp.float32)).astype(jnp.bfloat16)
    return (rscale, normed, query, keys, values, probs, probs_b, attended, hidden)

def attend_backward(windows, saved, dhid, gain, w_qkv, w_out):
    rscale, normed, query, keys, values, probs, probs_b, attended, hidden = saved
    count, window, width = windows.shape
    dhid_b = dhid.astype(jnp.bfloat16)
    grad_out = jnp.dot(attended.T, dhid_b, preferred_element_type=jnp.float32)
    datt = jnp.dot(dhid_b, w_out.T, preferred_element_type=jnp.float32).astype(jnp.bfloat16).reshape(count, window, HEADS, HD)
    dprob = prod('wqhe,wkhe->whqk', datt, values)
    dvalue = prod('whqk,wqhe->wkhe', probs_b, datt)
    dscore = probs * (dprob - lax.optimization_barrier(jnp.sum(probs * dprob, -1, keepdims=True))) * HD ** (-0.5)
    dscore_b = dscore.astype(jnp.bfloat16)
    dquery = prod('whqk,wkhe->wqhe', dscore_b, keys)
    dkey = prod('whqk,wqhe->wkhe', dscore_b, query)
    dqkv = jnp.stack([dquery, dkey, dvalue], 2).astype(jnp.bfloat16).reshape(count * window, 3 * width)
    grad_qkv = jnp.dot(normed.reshape(count * window, width).T, dqkv, preferred_element_type=jnp.float32)
    dnormed = jnp.dot(dqkv, w_qkv.T, preferred_element_type=jnp.float32)
    inputs = windows.reshape(count * window, width).astype(jnp.float32)
    rflat = rscale.reshape(count * window, 1)
    grad_gain = lax.optimization_barrier(jnp.sum(dnormed * inputs * rflat, 0))
    dscaled = dnormed * gain
    dshift = dhid + rflat * (dscaled - inputs * rflat * rflat * lax.optimization_barrier(jnp.mean(dscaled * inputs, -1, keepdims=True)))
    return (dshift, grad_qkv, grad_out, grad_gain)

def reference(block_input, gain, w_qkv, w_out, w_dec, g_points, slot_point, slot_cell, slot_weight, pair_count):
    devices = N_LAT * N_LON
    shifted = jnp.roll(block_input, -SHIFT, axis=2)
    tiles = shifted.reshape(LEV, N_LAT, LAT_DEV, N_LON, LON_DEV, D).transpose(1, 3, 0, 2, 4, 5)
    tiles = tiles.reshape(devices, LEV, LAT_DEV, LON_DEV, D)
    points = g_points.reshape(devices, G_DEV, C)
    lists = slot_point.reshape(devices, N_LAT, CAP)
    weights = slot_weight.reshape(devices, N_LAT, CAP)
    counts = pair_count.reshape(devices, N_LAT)
    live = jnp.arange(CAP)[None, None, :] < counts[:, :, None]
    picked = jax.vmap(lambda rows, index: rows[index])(points, lists)
    sent = jnp.where(live[..., None], weights[..., None] * picked.astype(jnp.float32), 0.0).astype(jnp.bfloat16)
    arrived = sent.reshape(N_LAT, N_LON, N_LAT, CAP, C).transpose(2, 1, 0, 3, 4).reshape(devices, N_LAT * CAP, C)
    cells = slot_cell.reshape(devices, N_LAT * CAP)

    def collect(rows, index):
        return jnp.zeros((TOK_DEV, C), jnp.float32).at[index].add(rows.astype(jnp.float32))
    grad_tok = jax.vmap(collect)(arrived, cells).astype(jnp.bfloat16)

    def step(carry, item):
        tile, grad_rows = item
        windows = to_windows(tile).reshape(-1, WT, D)
        saved = attend_forward(windows, gain, w_qkv, w_out)
        dhid = jnp.dot(grad_rows, w_dec.T, preferred_element_type=jnp.float32)
        dshift, g_qkv, g_out, g_gain = attend_backward(windows, saved, dhid, gain, w_qkv, w_out)
        g_dec = jnp.dot(saved[8].T, grad_rows, preferred_element_type=jnp.float32)
        back = from_windows(dshift.astype(jnp.bfloat16).reshape(LAT_DEV // WA, LON_DEV // WO, WT, D))
        total = (carry[0] + g_qkv, carry[1] + g_out, carry[2] + g_dec, carry[3] + g_gain)
        return (total, back)
    start = (jnp.zeros((D, 3 * D), jnp.float32), jnp.zeros((D, D), jnp.float32), jnp.zeros((D, C), jnp.float32), jnp.zeros((D,), jnp.float32))
    totals, backs = lax.scan(step, start, (tiles, grad_tok))
    dshift = backs.reshape(N_LAT, N_LON, LEV, LAT_DEV, LON_DEV, D).transpose(2, 0, 3, 1, 4, 5)
    dshift = dshift.reshape(LEV, NLAT, NLON, D)
    grad_x = jnp.roll(dshift, SHIFT, axis=2)
    return (grad_x, totals[0], totals[1], totals[2], totals[3])
```

```python
import jax
import jax.numpy as jnp
from jax import lax
from jax.experimental import pallas as pl
from jax.experimental.pallas import tpu as pltpu
from jax.sharding import PartitionSpec as P

D = 512
HEADS = 8
HD = 64
WA = 6
WO = 12
WT = 144
C = 80
TOK = 2304
CAP = 512
BANDS = 8
PTS = 1024
SCALE = 0.125
F32 = jnp.float32
BF16 = jnp.bfloat16
NT = (((1,), (1,)), ((), ()))
TN = (((0,), (0,)), ((), ()))


def mm(a, b):
    return jnp.dot(a, b, preferred_element_type=F32)


def dg(a, b, dims):
    return lax.dot_general(a, b, dims, preferred_element_type=F32)


def onehot(idx_row, count):
    rows = lax.broadcasted_iota(jnp.int32, (count, idx_row.shape[1]), 0)
    return jnp.where(rows == idx_row, 1.0, 0.0).astype(BF16)


MESH = pl.DeviceIdType.MESH


def spot():
    return lax.axis_index("lat"), lax.axis_index("lon")


def device(lat, lon):
    return {"lat": lat, "lon": lon}


def greet(devices):
    barrier = pltpu.get_barrier_semaphore()
    for dev in devices:
        pl.semaphore_signal(barrier, inc=1, device_id=dev, device_id_type=MESH)
    pl.semaphore_wait(barrier, len(devices))


def remote(src, dst, send, recv, dev):
    return pltpu.make_async_remote_copy(
        src_ref=src, dst_ref=dst, send_sem=send, recv_sem=recv, device_id=dev, device_id_type=MESH
    )


def sub_iota(shape):
    return lax.broadcasted_iota(jnp.int32, shape, 1)


def norm_scale(x):
    return lax.rsqrt(jnp.mean(x * x, -1, keepdims=True) + 1e-06)


def steps_of(value, width, count):
    total = jnp.zeros_like(value)
    for n in range(1, count):
        total += jnp.where(value >= n * width, 1, 0)
    return total


def own_rows(cell):
    win = steps_of(cell, WT, 16)
    t = cell - win * WT
    r = steps_of(t, WO, 12)
    lo = t - r * WO
    low = r >= WA
    turn = jnp.where(low, 4, 0)
    mixed = 96 + (r - jnp.where(low, WA, 0)) * 8

    def wrap(v):
        return jnp.where(v >= 8, v - 8, v)

    a_row = jnp.where(
        (lo >= 2) & (lo < 10), r * 8 + lo - 2,
        mixed + wrap(jnp.where(lo < 2, lo + 6, lo - 10) + turn),
    )
    b_row = jnp.where(
        lo < 6, r * 8 + lo + 2,
        jnp.where(lo < 8, r * 8 + lo - 6, mixed + wrap(lo - 6 + turn)),
    )
    half = steps_of(win, 2, 8)
    second = win - half * 2
    return second * HALF + half * WT + jnp.where(second == 0, a_row, b_row)


NB = 8
HALF = NB * WT
NG = 4
GW = NG * HD
QC = 3 * GW
ER = 640


def start(copies):
    for copy in copies:
        copy.start()
    return copies


def finish(copies):
    for copy in copies:
        copy.wait()


def total_of(buf, n):
    acc = buf[0].astype(F32)
    for i in range(1, n):
        acc = acc + buf[i].astype(F32)
    return acc.astype(BF16)


class Sum:
    def __init__(self, src, out, rows, lanes, split_lanes, bufs, sems):
        self.src, self.out = src, out
        self.buf_a, self.sum_b, self.buf_b, self.sum_c, self.buf_c = bufs
        self.sems = sems
        lat, lon = spot()
        self.lat, self.lon = lat, lon
        self.core, self.grp = lax.rem(lon, 2), lax.div(lon, 2)
        self.sib = lon + 1 - 2 * self.core
        self.rows, self.lanes, self.split_lanes = rows, lanes, split_lanes
        self.half, self.band = lanes // 2, rows // 8
        self.grps = [lax.rem(self.grp + s, 8) for s in range(1, 8)]
        self.lats = [lax.rem(lat + s, 8) for s in range(1, 8)]
        self.step_no = 0

    def lane(self, core):
        return pl.ds(pl.multiple_of(core * self.half, 128), self.half)

    def rows_of(self, grp):
        return pl.ds(pl.multiple_of(grp * self.band, 16), self.band)

    def piece(self, lat):
        if self.split_lanes:
            n = self.half // 2
            return pl.ds(0, self.band), pl.ds(pl.multiple_of(lax.rem(lat, 2) * n, 128), n)
        n = self.band // 4
        return pl.ds(pl.multiple_of(lax.rem(lat, 4) * n, 16), n), pl.ds(0, self.half)

    def whole_piece(self, lat):
        if self.split_lanes:
            n = self.half // 2
            at = self.core * self.half + lax.rem(lat, 2) * n
            return self.rows_of(self.grp), pl.ds(pl.multiple_of(at, 128), n)
        n = self.band // 4
        at = self.grp * self.band + lax.rem(lat, 4) * n
        return pl.ds(pl.multiple_of(at, 16), n), self.lane(self.core)

    def copy(self, src, dst, n, dev):
        return remote(src, dst, self.sems.at[0, n], self.sems.at[1, n], dev)

    def step(self):
        getattr(self, "step%d" % self.step_no)()
        self.step_no += 1

    def step0(self):
        src = self.src.at[:, self.lane(1 - self.core)]
        self.flying = start([self.copy(src, self.buf_a, 0, device(self.lat, self.sib))])

    def step1(self):
        finish(self.flying)
        self.sum_b[...] = (
            self.src[:, self.lane(self.core)].astype(F32) + self.buf_a[...].astype(F32)
        ).astype(BF16)
        self.flying = start([
            self.copy(
                self.sum_b.at[self.rows_of(g)], self.buf_b.at[self.grp], 1 + s,
                device(self.lat, g * 2 + self.core),
            )
            for s, g in enumerate(self.grps)
        ])
        self.buf_b[self.grp] = self.sum_b[self.rows_of(self.grp)]

    def step2(self):
        finish(self.flying)
        self.sum_c[...] = total_of(self.buf_b, 8)
        self.flying = start([
            self.copy(
                self.sum_c.at[self.piece(o)], self.buf_c.at[self.lat], 8 + s, device(o, self.lon)
            )
            for s, o in enumerate(self.lats)
        ])
        self.buf_c[self.lat] = self.sum_c[self.piece(self.lat)]

    def step3(self):
        finish(self.flying)
        here = self.whole_piece(self.lat)
        self.out[here] = total_of(self.buf_c, 8)
        own = self.out.at[here]
        count = 2 if self.split_lanes else 4
        first = self.lat - lax.rem(self.lat, count)
        peers = [first + lax.rem(self.lat + s, count) for s in range(1, count)]
        self.flying = start([
            self.copy(own, own, 15 + s, device(o, self.lon)) for s, o in enumerate(peers)
        ])

    def step4(self):
        finish(self.flying)
        own = self.out.at[self.rows_of(self.grp), self.lane(self.core)]
        self.flying = start([
            self.copy(own, own, 18 + s, device(self.lat, g * 2 + self.core))
            for s, g in enumerate(self.grps)
        ])

    def step5(self):
        finish(self.flying)
        own = self.out.at[:, self.lane(self.core)]
        self.flying = start([self.copy(own, own, 25, device(self.lat, self.sib))])

    def step6(self):
        finish(self.flying)


def fused_kernel(
    x_hbm, pts_ref, slot_ref, weight_ref, count_ref, cell_ref, gain_ref, wqkv_hbm, wout_hbm,
    wdec_ref,
    gx_hbm, arrive_ref, qa_ref, qb_ref, e_ref,
    xv, wqkv, wout, load_sem, store_sem,
    sent, arr, asend, arecv, first, halo, edge, hsems,
    xw, nw, qkv, probs, att, oh, marr, gtt, dhf, dhb, datt, hid,
    src_a, src_b, src_e,
    a0, a1, a2, a3, a4, b0, b1, b2, b3, b4, e0, e1, e2, e3, e4, sems_a, sems_b, sems_e,
):
    lat, lon = spot()
    core, grp = lax.rem(lon, 2), lax.div(lon, 2)
    west, east = lax.rem(lon + 15, 16), lax.rem(lon + 1, 16)
    others = [lax.rem(lat + s, BANDS) for s in range(1, BANDS)]
    loads = start([
        pltpu.make_async_copy(x_hbm, xv, load_sem.at[0]),
        pltpu.make_async_copy(wqkv_hbm, wqkv, load_sem.at[1]),
        pltpu.make_async_copy(wout_hbm, wout, load_sem.at[2]),
    ])
    barrier = pltpu.get_barrier_semaphore()
    peers = (
        [device(lat, lon + 1 - 2 * core)]
        + [device(lat, lax.rem(grp + s, 8) * 2 + core) for s in range(1, 8)]
        + [device(o, lon) for o in others]
        + [device(lat, west), device(lat, east)]
    )
    for dev in peers:
        pl.semaphore_signal(barrier, inc=1, device_id=dev, device_id_type=MESH)

    sum_a = Sum(src_a, qa_ref, D, QC, False, (a0, a1, a2, a3, a4), sems_a)
    sum_b = Sum(src_b, qb_ref, D, QC, False, (b0, b1, b2, b3, b4), sems_b)
    sum_e = Sum(src_e, e_ref, ER, D, True, (e0, e1, e2, e3, e4), sems_e)

    pts = jnp.concatenate([pts_ref[:, n * 256 : (n + 1) * 256] for n in range(4)], axis=0)
    lane = lax.broadcasted_iota(jnp.int32, (1, CAP), 1)

    def rows_for(d):
        point = slot_ref[pl.ds(d, 1), :]
        quarter = steps_of(point, 256, 4)
        picked = mm(pts, onehot(point - quarter * 256, 256))
        rows = picked[0:C]
        for n in range(1, 4):
            rows = jnp.where(quarter == n, picked[n * C : (n + 1) * C], rows)
        live = lane < count_ref[pl.ds(d, 1), :]
        return jnp.where(live, weight_ref[pl.ds(d, 1), :] * rows, 0.0).astype(BF16)

    for s, o in enumerate(others):
        sent[s] = rows_for(o)
    arr[lat] = rows_for(lat)
    loads[0].wait()

    @pl.loop(0, NB)
    def _(lb):
        for lev in range(2):
            rows = pl.ds(pl.multiple_of(lb * 96 + lev * 48, 16), 48)
            part = xv[lev, pl.ds(lb * WA, WA)].astype(F32)[:, 0:8]
            first[rows, :] = part.reshape(48, D).astype(BF16)

    pl.semaphore_wait(barrier, len(peers))
    in_copy = remote(first, halo, hsems.at[0], hsems.at[1], device(lat, west))
    in_copy.start()
    copies = start([
        remote(sent.at[s], arr.at[lat], asend.at[s], arecv.at[s], device(o, lon))
        for s, o in enumerate(others)
    ])

    gain = gain_ref[...]

    def put_window(rows, toks):
        xw[rows, :] = toks.astype(BF16)
        nw[rows, :] = (toks * norm_scale(toks) * gain).astype(BF16)

    def project(at):
        @pl.loop(0, 6)
        def _(c):
            cols = pl.ds(pl.multiple_of(c * 256, 256), 256)
            qkv[at : at + HALF, cols] = mm(nw[at : at + HALF, :], wqkv[:, cols]).astype(BF16)

    @pl.loop(0, NB)
    def _(lb):
        x0 = xv[0, pl.ds(lb * WA, WA)].astype(F32)
        x1 = xv[1, pl.ds(lb * WA, WA)].astype(F32)
        sub = sub_iota((WA, 8, D))
        c0 = jnp.where(sub >= 6, x0[:, 0:8], x0[:, 16:24])
        c1 = jnp.where(sub >= 6, x1[:, 0:8], x1[:, 16:24])
        mixed = jnp.where((sub < 2) | (sub >= 6), c0, pltpu.roll(c1, 4, 1))
        toks = jnp.concatenate([x0[:, 8:16], x1[:, 8:16], mixed], axis=0).reshape(WT, D)
        put_window(pl.ds(pl.multiple_of(lb * WT, WT), WT), toks)

    loads[1].wait()
    project(0)

    head = lax.broadcasted_iota(jnp.int32, (1, GW), 1) // HD
    masks = [jnp.where(head == a, 1.0, 0.0).astype(BF16) for a in range(NG)]
    picks = [head == a for a in range(NG)]

    def stack(a):
        return jnp.concatenate([a * m for m in masks], axis=0)

    def pick(o):
        out = o[0:WT]
        for a in range(1, NG):
            out = jnp.where(picks[a], o[a * WT : (a + 1) * WT], out)
        return out

    def forward(w):
        rows = pl.ds(pl.multiple_of(w * WT, WT), WT)
        for g in range(HEADS // NG):
            cols = slice(g * GW, (g + 1) * GW)
            k = qkv[rows, D + g * GW : D + (g + 1) * GW]
            v = qkv[rows, 2 * D + g * GW : 2 * D + (g + 1) * GW]
            st = dg(k, stack(qkv[rows, cols] * BF16(SCALE)), NT)
            e = jnp.exp(st - jnp.max(st, axis=0, keepdims=True))
            pb = (e * (1.0 / jnp.sum(e, axis=0, keepdims=True))).astype(BF16)
            probs[g, rows, :] = pb
            att[rows, cols] = pick(dg(pb, v, TN)).astype(BF16)

    @pl.loop(0, NB)
    def _(w):
        forward(w)

    in_copy.wait()

    @pl.loop(0, NB)
    def _(lb):
        at = pl.multiple_of(lb * 96, 16)
        h0 = halo[pl.ds(at, 48), :].astype(F32).reshape(WA, 8, D)
        h1 = halo[pl.ds(pl.multiple_of(at + 48, 16), 48), :].astype(F32).reshape(WA, 8, D)
        x0 = xv[0, pl.ds(lb * WA, WA)].astype(F32)
        x1 = xv[1, pl.ds(lb * WA, WA)].astype(F32)
        sub = sub_iota((WA, 8, D))
        w0 = jnp.where(sub < 2, h0, x0[:, 16:24])
        w1 = jnp.where(sub < 2, h1, x1[:, 16:24])
        mixed = jnp.where((sub < 2) | (sub >= 6), pltpu.roll(h1, 4, 1), h0)
        toks = jnp.concatenate([w0, w1, mixed], axis=0).reshape(WT, D)
        put_window(pl.ds(pl.multiple_of(HALF + lb * WT, WT), WT), toks)

    project(HALF)

    @pl.loop(NB, 2 * NB)
    def _(w):
        forward(w)

    row = own_rows(cell_ref[...])
    block = steps_of(row, 256, 9)
    place = row - block * 256
    for i in range(BANDS):
        oh[:, i * CAP : (i + 1) * CAP] = onehot(place[i : i + 1, :], 256)
    finish(copies)
    for i in range(BANDS):
        part = arr[i]
        for b in range(9):
            mask = jnp.where(block[i : i + 1, :] == b, 1.0, 0.0).astype(BF16)
            marr[b * C : (b + 1) * C, i * CAP : (i + 1) * CAP] = part * mask
    toks = dg(marr[...], oh[...], NT).astype(BF16)
    for b in range(9):
        gtt[:, b * 256 : (b + 1) * 256] = toks[b * C : (b + 1) * C]
    loads[2].wait()

    @pl.loop(0, 9)
    def _(b):
        rows = pl.ds(pl.multiple_of(b * 256, 256), 256)
        dh = dg(gtt[:, rows], wdec_ref[...], TN)
        dhf[rows, :] = dh
        dhb[rows, :] = dh.astype(BF16)
        datt[rows, :] = dg(dh.astype(BF16), wout[...], NT).astype(BF16)
        hid[rows, :] = (xw[rows, :].astype(F32) + mm(att[rows, :], wout[...])).astype(BF16)

    src_e[0:D, :] = dg(att[...], dhb[...], TN).astype(BF16)
    src_e[D : D + C, :] = mm(gtt[...], hid[...]).astype(BF16)
    src_e[D + C : ER, :] = jnp.zeros((ER - D - C, D), BF16)
    sum_e.step()

    def backward(w, g):
        rows = pl.ds(pl.multiple_of(w * WT, WT), WT)
        cols = slice(g * GW, (g + 1) * GW)
        kcols = slice(D + g * GW, D + (g + 1) * GW)
        vcols = slice(2 * D + g * GW, 2 * D + (g + 1) * GW)
        k = qkv[rows, kcols]
        v = qkv[rows, vcols]
        qs = stack(qkv[rows, cols] * BF16(SCALE))
        ds = stack(datt[rows, cols])
        pb = probs[g, rows, :]
        p = pb.astype(F32)
        dp = dg(v, ds, NT)
        t = jnp.sum(p * dp, axis=0, keepdims=True)
        dst = (p * (dp - t)).astype(BF16)
        dv = mm(pb, ds)
        dk = mm(dst, qs)
        dq = pick(dg(dst, k, TN)) * SCALE
        qkv[rows, cols] = dq.astype(BF16)
        qkv[rows, kcols] = dk.astype(BF16)
        qkv[rows, vcols] = dv.astype(BF16)

    def back_loop(lo, hi, g):
        @pl.loop(lo, hi)
        def _(w):
            backward(w, g)

    def weight_grad(src, g):
        for n in range(3):
            part = dg(nw[...], qkv[:, n * D + g * GW : n * D + (g + 1) * GW], TN)
            src[:, n * GW : (n + 1) * GW] = part.astype(BF16)

    back_loop(0, NB, 0)
    sum_e.step()
    back_loop(NB, 2 * NB, 0)
    sum_e.step()
    weight_grad(src_a, 0)
    sum_a.step()
    back_loop(0, NB, 1)
    sum_e.step()
    sum_a.step()
    back_loop(NB, 2 * NB, 1)
    sum_e.step()
    sum_a.step()
    weight_grad(src_b, 1)
    sum_b.step()
    sum_e.step()
    sum_a.step()

    sub = sub_iota((WA, 8, D))

    def input_grad(lb):
        ys = []
        for s in range(2):
            rows = pl.ds(pl.multiple_of(s * HALF + lb * WT, WT), WT)
            x = xw[rows, :].astype(F32)
            dn = dg(qkv[rows, :], wqkv[...], NT)
            r = norm_scale(x)
            dng = dn * gain
            mean = jnp.mean(dng * x, -1, keepdims=True)
            y = dhf[rows, :] + r * (dng - x * (r * r * mean))
            ys.append(y.reshape(18, 8, D))
        ya, yb = ys
        m0, n0 = ya[12:18], yb[12:18]
        m1, n1 = pltpu.roll(m0, 4, 1), pltpu.roll(n0, 4, 1)
        at = pl.ds(lb * WA, WA)
        xv[0, at] = jnp.concatenate([m0, ya[0:6], jnp.where(sub < 2, m0, yb[0:6])], 1).astype(BF16)
        xv[1, at] = jnp.concatenate([m1, ya[6:12], jnp.where(sub < 2, m1, yb[6:12])], 1).astype(BF16)
        g0 = jnp.where(sub < 2, yb[0:6], n0).reshape(48, D)
        g1 = jnp.where(sub < 2, yb[6:12], n1).reshape(48, D)
        here = pl.multiple_of(lb * 96, 16)
        edge[pl.ds(here, 48), :] = g0.astype(BF16)
        edge[pl.ds(pl.multiple_of(here + 48, 16), 48), :] = g1.astype(BF16)

    outs = []

    def input_loop(n, lo, hi):
        @pl.loop(lo, hi)
        def _(lb):
            input_grad(lb)

        rows = pl.ds(lo * 96, (hi - lo) * 96)
        outs.append(remote(
            edge.at[rows], arrive_ref.at[rows], hsems.at[2 + 2 * n], hsems.at[3 + 2 * n],
            device(lat, east),
        ))
        outs[-1].start()
        at = pl.ds(lo * WA, (hi - lo) * WA)
        outs.append(pltpu.make_async_copy(xv.at[:, at], gx_hbm.at[:, at], store_sem.at[n]))
        outs[-1].start()

    input_loop(0, 0, 2)
    sum_b.step()
    sum_a.step()
    sum_e.step()
    input_loop(1, 2, 5)
    sum_b.step()
    sum_a.step()
    input_loop(2, 5, 8)
    sum_b.step()
    sum_a.step()
    sum_b.step()
    sum_b.step()
    sum_b.step()
    finish(outs)


def place_kernel(
    gx_ref, arrive_ref, qa_ref, qb_ref, e_ref, wqkv_ref, gain_ref,
    out_ref, gqkv_ref, gout_ref, gdec_ref, ggain_ref,
):
    sub = sub_iota((WA, 8, D))
    for lb in range(NB):
        for lev in range(2):
            at = slice(lb * WA, (lb + 1) * WA)
            x = gx_ref[lev, at].astype(F32)
            new = arrive_ref[lb * 96 + lev * 48 : lb * 96 + lev * 48 + 48].astype(F32)
            edge = jnp.where(sub < 6, new.reshape(WA, 8, D), x[:, 0:8])
            out_ref[lev, at] = jnp.concatenate([edge, x[:, 8:24]], 1).astype(BF16)
    acc = jnp.zeros((D, 128), F32)
    for g, q_ref in enumerate((qa_ref, qb_ref)):
        for n in range(3):
            cols = slice(n * D + g * GW, n * D + (g + 1) * GW)
            part = q_ref[:, n * GW : (n + 1) * GW].astype(F32)
            gqkv_ref[:, cols] = part
            prod = part * wqkv_ref[:, cols].astype(F32)
            acc += prod[:, 0:128] + prod[:, 128:256]
    ggain_ref[...] = jnp.sum(acc.T, axis=0, keepdims=True) / gain_ref[...]
    gout_ref[...] = e_ref[0:D].astype(F32)
    gdec_ref[...] = e_ref[D : D + C].astype(F32)


VM = pl.BlockSpec(memory_space=pltpu.VMEM)
ANY = pl.BlockSpec(memory_space=pl.ANY)
SDS = jax.ShapeDtypeStruct
DMA = pltpu.SemaphoreType.DMA


def sum_bufs(rows, lanes, split_lanes):
    half, band = lanes // 2, rows // 8
    piece = (band, half // 2) if split_lanes else (band // 4, half)
    shapes = [(rows, half), (rows, half), (8, band, half), (band, half), (8,) + piece]
    return [pltpu.VMEM(s, BF16) for s in shapes]


def fused_call(x, pts_t, slots, weights, counts, cells, gain, w_qkv, w_out, w_dec_t):
    def vm(*shape, dtype=BF16):
        return pltpu.VMEM(shape, dtype)

    return pl.pallas_call(
        fused_kernel,
        out_shape=(
            SDS(x.shape, BF16), SDS((768, D), BF16), SDS((D, QC), BF16), SDS((D, QC), BF16),
            SDS((ER, D), BF16),
        ),
        in_specs=[ANY] + [VM] * 6 + [ANY, ANY, VM],
        out_specs=(ANY, VM, VM, VM, VM),
        scratch_shapes=[
            vm(2, 48, 24, D), vm(D, 3 * D), vm(D, D), DMA((3,)), DMA((3,)),
            vm(7, C, CAP), vm(BANDS, C, CAP), DMA((7,)), DMA((7,)),
            vm(768, D), vm(768, D), vm(768, D), DMA((8,)),
            vm(TOK, D), vm(TOK, D), vm(TOK, 3 * D), vm(2, TOK, NG * WT), vm(TOK, D),
            vm(256, BANDS * CAP), vm(9 * C, BANDS * CAP), vm(C, TOK), vm(TOK, D, dtype=F32),
            vm(TOK, D), vm(TOK, D), vm(TOK, D),
            vm(D, QC), vm(D, QC), vm(ER, D),
            *sum_bufs(D, QC, False), *sum_bufs(D, QC, False), *sum_bufs(ER, D, True),
            DMA((2, 26)), DMA((2, 26)), DMA((2, 26)),
        ],
        compiler_params=pltpu.CompilerParams(
            vmem_limit_bytes=62 << 20, collective_id=0, has_side_effects=True
        ),
        name="fused",
    )(x, pts_t, slots, weights, counts, cells, gain, w_qkv, w_out, w_dec_t)


def place_call(gx, arriving, qa, qb, e, w_qkv, gain):
    return pl.pallas_call(
        place_kernel,
        out_shape=(
            SDS(gx.shape, BF16), SDS((D, 3 * D), F32), SDS((D, D), F32), SDS((C, D), F32),
            SDS((1, D), F32),
        ),
        in_specs=[VM] * 7,
        out_specs=(VM,) * 5,
        compiler_params=pltpu.CompilerParams(vmem_limit_bytes=40 << 20),
        name="place",
    )(gx, arriving, qa, qb, e, w_qkv, gain)


def body(
    block_input, gain, w_qkv, w_out, w_dec, g_points, slot_point, slot_cell, slot_weight, pair_count
):
    counts = jnp.broadcast_to(pair_count[:, None], slot_point.shape)
    parts = fused_call(
        block_input, g_points.T, slot_point, slot_weight, counts, slot_cell, gain[None],
        w_qkv, w_out, w_dec.T,
    )
    grad_x, g_qkv, g_out, g_dec, g_gain = place_call(*parts, w_qkv, gain[None])
    return (grad_x, g_qkv, g_out, g_dec.T, g_gain[0])


def solution(mesh):
    placed = (
        P(None, "lat", "lon", None),
        P(),
        P(),
        P(),
        P(),
        P(("lat", "lon"), None),
        P(("lat", "lon"), None),
        P(("lat", "lon"), None),
        P(("lat", "lon"), None),
        P(("lat", "lon")),
    )
    return jax.shard_map(
        body,
        mesh=mesh,
        in_specs=placed,
        out_specs=(P(None, "lat", "lon", None), P(), P(), P(), P()),
        check_vma=False,
    )
```

```python
import jax
import jax.numpy as jnp
from jax import lax
from jax.experimental import pallas as pl
from jax.experimental.pallas import tpu as pltpu
from jax.sharding import PartitionSpec as P

D = 512
HEADS = 8
HD = 64
WA = 6
WO = 12
WT = 144
C = 80
TOK = 2304
CAP = 512
BANDS = 8
PTS = 1024
SCALE = 0.125
F32 = jnp.float32
BF16 = jnp.bfloat16
NT = (((1,), (1,)), ((), ()))
TN = (((0,), (0,)), ((), ()))


def mm(a, b):
    return jnp.dot(a, b, preferred_element_type=F32)


def dg(a, b, dims):
    return lax.dot_general(a, b, dims, preferred_element_type=F32)


def onehot(idx_row, count):
    rows = lax.broadcasted_iota(jnp.int32, (count, idx_row.shape[1]), 0)
    return jnp.where(rows == idx_row, 1.0, 0.0).astype(BF16)


MESH = pl.DeviceIdType.MESH


def spot():
    return lax.axis_index("lat"), lax.axis_index("lon")


def device(lat, lon):
    return {"lat": lat, "lon": lon}


def greet(devices):
    barrier = pltpu.get_barrier_semaphore()
    for dev in devices:
        pl.semaphore_signal(barrier, inc=1, device_id=dev, device_id_type=MESH)
    pl.semaphore_wait(barrier, len(devices))


def remote(src, dst, send, recv, dev):
    return pltpu.make_async_remote_copy(
        src_ref=src, dst_ref=dst, send_sem=send, recv_sem=recv, device_id=dev, device_id_type=MESH
    )


def sub_iota(shape):
    return lax.broadcasted_iota(jnp.int32, shape, 1)


def norm_scale(x):
    return lax.rsqrt(jnp.mean(x * x, -1, keepdims=True) + 1e-06)


def steps_of(value, width, count):
    total = jnp.zeros_like(value)
    for n in range(1, count):
        total += jnp.where(value >= n * width, 1, 0)
    return total


def own_rows(cell):
    win = steps_of(cell, WT, 16)
    t = cell - win * WT
    r = steps_of(t, WO, 12)
    lo = t - r * WO
    low = r >= WA
    turn = jnp.where(low, 4, 0)
    mixed = 96 + (r - jnp.where(low, WA, 0)) * 8

    def wrap(v):
        return jnp.where(v >= 8, v - 8, v)

    a_row = jnp.where(
        (lo >= 2) & (lo < 10), r * 8 + lo - 2,
        mixed + wrap(jnp.where(lo < 2, lo + 6, lo - 10) + turn),
    )
    b_row = jnp.where(
        lo < 6, r * 8 + lo + 2,
        jnp.where(lo < 8, r * 8 + lo - 6, mixed + wrap(lo - 6 + turn)),
    )
    half = steps_of(win, 2, 8)
    second = win - half * 2
    return second * HALF + half * WT + jnp.where(second == 0, a_row, b_row)


NB = 8
HALF = NB * WT
GROUPS = ((0, 4), (4, 2), (6, 2))
ER = 640


def start(copies):
    for copy in copies:
        copy.start()
    return copies


def finish(copies):
    for copy in copies:
        copy.wait()


def total_of(buf, n):
    acc = buf[0].astype(F32)
    for i in range(1, n):
        acc = acc + buf[i].astype(F32)
    return acc.astype(BF16)


class Sum:
    def __init__(self, src, out, plan, bufs, sems):
        self.src, self.out = src, out
        self.buf_a, self.sum_b, self.buf_b, self.sum_c, self.buf_c = bufs
        self.sems = sems
        lat, lon = spot()
        self.lat, self.lon = lat, lon
        self.core, grp = lax.rem(lon, 2), lax.div(lon, 2)
        self.sib = lon + 1 - 2 * self.core
        self.rows, self.lanes, self.by_lanes, self.rp, self.lp, self.lat_first = plan
        self.hr = self.rows if self.by_lanes else self.rows // 2
        self.hl = self.lanes // 2 if self.by_lanes else self.lanes
        self.band = self.hr // 8
        self.pr, self.pl = self.band // self.rp, self.hl // self.lp
        self.one, self.two = (lat, grp) if self.lat_first else (grp, lat)
        self.step_no = 0

    def dev_one(self, n):
        if self.lat_first:
            return device(n, self.lon)
        return device(self.lat, n * 2 + self.core)

    def dev_two(self, n):
        if self.lat_first:
            return device(self.lat, n * 2 + self.core)
        return device(n, self.lon)

    def half(self, core):
        if self.by_lanes:
            return pl.ds(0, self.hr), pl.ds(pl.multiple_of(core * self.hl, 128), self.hl)
        return pl.ds(pl.multiple_of(core * self.hr, 16), self.hr), pl.ds(0, self.hl)

    def band_of(self, n):
        return pl.ds(pl.multiple_of(n * self.band, 16), self.band)

    def piece(self, n, row=0, lane=0):
        part = lax.rem(n, self.rp * self.lp)
        row = row + lax.rem(part, self.rp) * self.pr
        lane = lane + lax.div(part, self.rp) * self.pl
        return (
            pl.ds(pl.multiple_of(row, 16), self.pr), pl.ds(pl.multiple_of(lane, 128), self.pl)
        )

    def corner(self):
        row, lane = self.one * self.band, 0
        if self.by_lanes:
            lane = self.core * self.hl
        else:
            row = row + self.core * self.hr
        return row, lane

    def copy(self, src, dst, n, dev):
        return remote(src, dst, self.sems.at[0, n], self.sems.at[1, n], dev)

    def step(self):
        getattr(self, "step%d" % self.step_no)()
        self.step_no += 1

    def step0(self):
        src = self.src.at[self.half(1 - self.core)]
        self.flying = start([self.copy(src, self.buf_a, 0, device(self.lat, self.sib))])

    def step1(self):
        finish(self.flying)
        self.sum_b[...] = (
            self.src[self.half(self.core)].astype(F32) + self.buf_a[...].astype(F32)
        ).astype(BF16)
        self.flying = start([
            self.copy(
                self.sum_b.at[self.band_of(lax.rem(self.one + s, 8))], self.buf_b.at[self.one], s,
                self.dev_one(lax.rem(self.one + s, 8)),
            )
            for s in range(1, 8)
        ])
        self.buf_b[self.one] = self.sum_b[self.band_of(self.one)]

    def step2(self):
        finish(self.flying)
        self.sum_c[...] = total_of(self.buf_b, 8)
        self.flying = start([
            self.copy(
                self.sum_c.at[self.piece(lax.rem(self.two + s, 8))], self.buf_c.at[self.two],
                7 + s, self.dev_two(lax.rem(self.two + s, 8)),
            )
            for s in range(1, 8)
        ])
        self.buf_c[self.two] = self.sum_c[self.piece(self.two)]

    def step3(self):
        finish(self.flying)
        here = self.piece(self.two, *self.corner())
        self.out[here] = total_of(self.buf_c, 8)
        own = self.out.at[here]
        count = self.rp * self.lp
        first = self.two - lax.rem(self.two, count)
        self.flying = start([
            self.copy(own, own, 14 + s, self.dev_two(first + lax.rem(self.two + s, count)))
            for s in range(1, count)
        ])

    def step4(self):
        finish(self.flying)
        row, lane = self.corner()
        own = self.out.at[
            pl.ds(pl.multiple_of(row, 16), self.band), pl.ds(pl.multiple_of(lane, 128), self.hl)
        ]
        self.flying = start([
            self.copy(own, own, 17 + s, self.dev_one(lax.rem(self.one + s, 8)))
            for s in range(1, 8)
        ])

    def step5(self):
        finish(self.flying)
        own = self.out.at[self.half(self.core)]
        self.flying = start([self.copy(own, own, 25, device(self.lat, self.sib))])

    def step6(self):
        finish(self.flying)


PLAN_E = (ER, D, True, 1, 2, True)
PLAN_4 = (D, 768, True, 4, 1, False)
PLAN_2 = (D, 384, False, 2, 1, False)


def fused_kernel(
    x_hbm, pts_ref, slot_ref, weight_ref, count_ref, cell_ref, gain_ref, wqkv_hbm, wout_hbm,
    wdec_ref,
    gx_hbm, arrive_ref, qa_ref, qb_ref, qc_ref, e_ref,
    xv, wqkv, wout, load_sem, store_sem,
    sent, arr, asend, arecv, first, halo, edge, hsems,
    xw, nw, qkv, probs_a, probs_b, probs_c, att, oh, marr, gtt, dhf, dhb, datt, hid, dnf,
    src_a, src_b, src_c, src_e,
    a0, a1, a2, a3, a4, b0, b1, b2, b3, b4, c0, c1, c2, c3, c4, e0, e1, e2, e3, e4,
    sems_a, sems_b, sems_c, sems_e,
):
    lat, lon = spot()
    core, grp = lax.rem(lon, 2), lax.div(lon, 2)
    west, east = lax.rem(lon + 15, 16), lax.rem(lon + 1, 16)
    others = [lax.rem(lat + s, BANDS) for s in range(1, BANDS)]
    loads = start([
        pltpu.make_async_copy(x_hbm, xv, load_sem.at[0]),
        pltpu.make_async_copy(wqkv_hbm, wqkv, load_sem.at[1]),
        pltpu.make_async_copy(wout_hbm, wout, load_sem.at[2]),
    ])
    barrier = pltpu.get_barrier_semaphore()
    peers = (
        [device(lat, lon + 1 - 2 * core)]
        + [device(lat, lax.rem(grp + s, 8) * 2 + core) for s in range(1, 8)]
        + [device(o, lon) for o in others]
        + [device(lat, west), device(lat, east)]
    )
    for dev in peers:
        pl.semaphore_signal(barrier, inc=1, device_id=dev, device_id_type=MESH)

    sum_a = Sum(src_a, qa_ref, PLAN_4, (a0, a1, a2, a3, a4), sems_a)
    sum_b = Sum(src_b, qb_ref, PLAN_2, (b0, b1, b2, b3, b4), sems_b)
    sum_c = Sum(src_c, qc_ref, PLAN_2, (c0, c1, c2, c3, c4), sems_c)
    sum_e = Sum(src_e, e_ref, PLAN_E, (e0, e1, e2, e3, e4), sems_e)
    probs = (probs_a, probs_b, probs_c)

    pts = jnp.concatenate([pts_ref[:, n * 256 : (n + 1) * 256] for n in range(4)], axis=0)
    lane = lax.broadcasted_iota(jnp.int32, (1, CAP), 1)

    def rows_for(d):
        point = slot_ref[pl.ds(d, 1), :]
        quarter = steps_of(point, 256, 4)
        picked = mm(pts, onehot(point - quarter * 256, 256))
        rows = picked[0:C]
        for n in range(1, 4):
            rows = jnp.where(quarter == n, picked[n * C : (n + 1) * C], rows)
        live = lane < count_ref[d]
        return jnp.where(live, weight_ref[pl.ds(d, 1), :] * rows, 0.0).astype(BF16)

    for s, o in enumerate(others):
        sent[s] = rows_for(o)
    arr[lat] = rows_for(lat)
    loads[0].wait()

    @pl.loop(0, NB)
    def _(lb):
        for lev in range(2):
            rows = pl.ds(pl.multiple_of(lb * 96 + lev * 48, 16), 48)
            part = xv[lev, pl.ds(lb * WA, WA)].astype(F32)[:, 0:8]
            first[rows, :] = part.reshape(48, D).astype(BF16)

    pl.semaphore_wait(barrier, len(peers))
    in_copy = remote(first, halo, hsems.at[0], hsems.at[1], device(lat, west))
    in_copy.start()
    copies = start([
        remote(sent.at[s], arr.at[lat], asend.at[s], arecv.at[s], device(o, lon))
        for s, o in enumerate(others)
    ])

    gain = gain_ref[...]

    def put_window(rows, toks):
        xw[rows, :] = toks.astype(BF16)
        nw[rows, :] = (toks * norm_scale(toks) * gain).astype(BF16)

    def project(at):
        @pl.loop(0, 6)
        def _(c):
            cols = pl.ds(pl.multiple_of(c * 256, 256), 256)
            qkv[at : at + HALF, cols] = mm(nw[at : at + HALF, :], wqkv[:, cols]).astype(BF16)

    @pl.loop(0, NB)
    def _(lb):
        x0 = xv[0, pl.ds(lb * WA, WA)].astype(F32)
        x1 = xv[1, pl.ds(lb * WA, WA)].astype(F32)
        sub = sub_iota((WA, 8, D))
        c0 = jnp.where(sub >= 6, x0[:, 0:8], x0[:, 16:24])
        c1 = jnp.where(sub >= 6, x1[:, 0:8], x1[:, 16:24])
        mixed = jnp.where((sub < 2) | (sub >= 6), c0, pltpu.roll(c1, 4, 1))
        toks = jnp.concatenate([x0[:, 8:16], x1[:, 8:16], mixed], axis=0).reshape(WT, D)
        put_window(pl.ds(pl.multiple_of(lb * WT, WT), WT), toks)

    loads[1].wait()
    project(0)

    masks, picks = {}, {}
    for n in (4, 2):
        head = lax.broadcasted_iota(jnp.int32, (1, n * HD), 1) // HD
        masks[n] = [jnp.where(head == a, 1.0, 0.0).astype(BF16) for a in range(n)]
        picks[n] = [head == a for a in range(n)]

    def stack(a, n):
        return jnp.concatenate([a * m for m in masks[n]], axis=0)

    def pick(o, n):
        out = o[0:WT]
        for a in range(1, n):
            out = jnp.where(picks[n][a], o[a * WT : (a + 1) * WT], out)
        return out

    def col(part, g):
        at, n = GROUPS[g]
        return slice(part * D + at * HD, part * D + (at + n) * HD)

    def window(w):
        return pl.ds(pl.multiple_of(w * WT, WT), WT)

    def forward(w):
        for some in ((0,), (1, 2)):
            todo = [(window(2 * w + i), g) for i in range(2) for g in some]
            scores = [
                dg(qkv[rows, col(1, g)], stack(qkv[rows, col(0, g)] * BF16(SCALE), GROUPS[g][1]), NT)
                for rows, g in todo
            ]
            pbs = []
            for st in scores:
                e = jnp.exp(st - jnp.max(st, axis=0, keepdims=True))
                pbs.append((e * (1.0 / jnp.sum(e, axis=0, keepdims=True))).astype(BF16))
            outs = [dg(pb, qkv[rows, col(2, g)], TN) for pb, (rows, g) in zip(pbs, todo)]
            for pb, o, (rows, g) in zip(pbs, outs, todo):
                probs[g][rows, :] = pb
                att[rows, col(0, g)] = pick(o, GROUPS[g][1]).astype(BF16)

    @pl.loop(0, NB // 2)
    def _(w):
        forward(w)

    in_copy.wait()

    @pl.loop(0, NB)
    def _(lb):
        at = pl.multiple_of(lb * 96, 16)
        h0 = halo[pl.ds(at, 48), :].astype(F32).reshape(WA, 8, D)
        h1 = halo[pl.ds(pl.multiple_of(at + 48, 16), 48), :].astype(F32).reshape(WA, 8, D)
        x0 = xv[0, pl.ds(lb * WA, WA)].astype(F32)
        x1 = xv[1, pl.ds(lb * WA, WA)].astype(F32)
        sub = sub_iota((WA, 8, D))
        w0 = jnp.where(sub < 2, h0, x0[:, 16:24])
        w1 = jnp.where(sub < 2, h1, x1[:, 16:24])
        mixed = jnp.where((sub < 2) | (sub >= 6), pltpu.roll(h1, 4, 1), h0)
        toks = jnp.concatenate([w0, w1, mixed], axis=0).reshape(WT, D)
        put_window(pl.ds(pl.multiple_of(HALF + lb * WT, WT), WT), toks)

    project(HALF)

    @pl.loop(NB // 2, NB)
    def _(w):
        forward(w)

    row = own_rows(cell_ref[...])
    block = steps_of(row, 256, 9)
    place = row - block * 256
    for i in range(BANDS):
        oh[:, i * CAP : (i + 1) * CAP] = onehot(place[i : i + 1, :], 256)
    finish(copies)
    for i in range(BANDS):
        part = arr[i]
        for b in range(9):
            mask = jnp.where(block[i : i + 1, :] == b, 1.0, 0.0).astype(BF16)
            marr[b * C : (b + 1) * C, i * CAP : (i + 1) * CAP] = part * mask
    toks = dg(marr[...], oh[...], NT).astype(BF16)
    for b in range(9):
        gtt[:, b * 256 : (b + 1) * 256] = toks[b * C : (b + 1) * C]
    loads[2].wait()

    @pl.loop(0, 3)
    def _(b):
        rows = pl.ds(pl.multiple_of(b * 768, 768), 768)
        dh = dg(gtt[:, rows], wdec_ref[...], TN)
        dhf[rows, :] = dh
        dhb[rows, :] = dh.astype(BF16)
        datt[rows, :] = dg(dh.astype(BF16), wout[...], NT).astype(BF16)
        hid[rows, :] = (xw[rows, :].astype(F32) + mm(att[rows, :], wout[...])).astype(BF16)

    src_e[0:D, :] = dg(att[...], dhb[...], TN).astype(BF16)
    src_e[D : D + C, :] = mm(gtt[...], hid[...]).astype(BF16)
    src_e[D + C : ER, :] = jnp.zeros((ER - D - C, D), BF16)
    sum_e.step()

    def backward(w, g):
        n = GROUPS[g][1]
        todo = [window(2 * w + i) for i in range(2)]
        ks = [qkv[rows, col(1, g)] for rows in todo]
        qs = [stack(qkv[rows, col(0, g)] * BF16(SCALE), n) for rows in todo]
        ds = [stack(datt[rows, col(0, g)], n) for rows in todo]
        pbs = [probs[g][rows, :] for rows in todo]
        dps = [dg(qkv[rows, col(2, g)], d, NT) for rows, d in zip(todo, ds)]
        dvs = [mm(pb, d) for pb, d in zip(pbs, ds)]
        dsts = []
        for pb, dp in zip(pbs, dps):
            p = pb.astype(F32)
            t = jnp.sum(p * dp, axis=0, keepdims=True)
            dsts.append((p * (dp - t)).astype(BF16))
        dks = [mm(dst, q) for dst, q in zip(dsts, qs)]
        dqs = [pick(dg(dst, k, TN), n) * SCALE for dst, k in zip(dsts, ks)]
        for rows, dq, dk, dv in zip(todo, dqs, dks, dvs):
            qkv[rows, col(0, g)] = dq.astype(BF16)
            qkv[rows, col(1, g)] = dk.astype(BF16)
            qkv[rows, col(2, g)] = dv.astype(BF16)

    def back_loop(lo, hi, g):
        @pl.loop(lo // 2, hi // 2)
        def _(w):
            backward(w, g)

    def weight_grad(src, g):
        width = GROUPS[g][1] * HD
        for n in range(3):
            part = dg(nw[...], qkv[:, col(n, g)], TN)
            src[:, n * width : (n + 1) * width] = part.astype(BF16)

    back_loop(0, 4, 0)
    sum_e.step()
    back_loop(4, 16, 0)
    sum_e.step()
    weight_grad(src_a, 0)
    sum_a.step()
    back_loop(0, 8, 1)
    sum_e.step()
    sum_a.step()
    back_loop(8, 16, 1)
    sum_e.step()
    weight_grad(src_b, 1)
    sum_b.step()
    back_loop(0, 8, 2)
    sum_a.step()
    sum_b.step()
    back_loop(8, 16, 2)
    sum_a.step()
    weight_grad(src_c, 2)
    sum_c.step()
    sum_e.step()
    sum_a.step()
    sum_b.step()

    sub = sub_iota((WA, 8, D))

    def project_back(at):
        for n in range(2):
            cols = slice(n * 256, (n + 1) * 256)
            dnf[:, cols] = dg(qkv[at : at + HALF, :], wqkv[cols, :], NT)

    def input_grad(at, lb):
        rows = pl.ds(pl.multiple_of(at + lb * WT, WT), WT)
        x = xw[rows, :].astype(F32)
        r = norm_scale(x)
        dng = dnf[window(lb), :] * gain
        mean = jnp.mean(dng * x, -1, keepdims=True)
        y = dhf[rows, :] + r * (dng - x * (r * r * mean))
        return y.reshape(18, 8, D)

    outs = []

    def second_windows(lo, hi, n):
        @pl.loop(lo, hi)
        def _(lb):
            y = input_grad(HALF, lb)
            mix = y[12:18]
            turned = pltpu.roll(mix, 4, 1)
            at = pl.ds(lb * WA, WA)
            for lev, m in enumerate((mix, turned)):
                main = y[lev * 6 : lev * 6 + 6]
                xv[lev, at] = jnp.concatenate([main, main, main], 1).astype(BF16)
                here = pl.ds(pl.multiple_of(lb * 96 + lev * 48, 16), 48)
                edge[here, :] = jnp.where(sub < 2, main, m).reshape(48, D).astype(BF16)

        rows = pl.ds(lo * 96, (hi - lo) * 96)
        outs.append(remote(
            edge.at[rows], arrive_ref.at[rows], hsems.at[2 + 2 * n], hsems.at[3 + 2 * n],
            device(lat, east),
        ))
        outs[-1].start()

    def first_windows(lo, hi, n):
        @pl.loop(lo, hi)
        def _(lb):
            y = input_grad(0, lb)
            mix = y[12:18]
            turned = pltpu.roll(mix, 4, 1)
            at = pl.ds(lb * WA, WA)
            for lev, m in enumerate((mix, turned)):
                main = y[lev * 6 : lev * 6 + 6]
                right = jnp.where(sub < 2, m, xv[lev, at].astype(F32)[:, 16:24])
                xv[lev, at] = jnp.concatenate([m, main, right], 1).astype(BF16)

        at = pl.ds(lo * WA, (hi - lo) * WA)
        outs.append(pltpu.make_async_copy(xv.at[:, at], gx_hbm.at[:, at], store_sem.at[n]))
        outs[-1].start()

    project_back(HALF)
    sum_c.step()
    second_windows(0, 4, 0)
    sum_b.step()
    sum_e.step()
    second_windows(4, 8, 1)
    sum_c.step()
    sum_b.step()
    project_back(0)
    sum_a.step()
    sum_c.step()
    first_windows(0, 4, 0)
    sum_c.step()
    sum_b.step()
    first_windows(4, 8, 1)
    sum_a.step()
    sum_c.step()
    sum_b.step()
    sum_c.step()
    finish(outs)


def place_kernel(
    gx_ref, arrive_ref, qa_ref, qb_ref, qc_ref, e_ref, edec_ref, wqkv_ref, gain_ref,
    out_ref, gqkv_ref, gout_ref, gdec_ref, ggain_ref,
):
    sub = sub_iota((WA, 8, D))
    for lb in range(2):
        for lev in range(2):
            at = slice(lb * WA, (lb + 1) * WA)
            x = gx_ref[lev, at].astype(F32)
            new = arrive_ref[lb * 96 + lev * 48 : lb * 96 + lev * 48 + 48].astype(F32)
            edge = jnp.where(sub < 6, new.reshape(WA, 8, D), x[:, 0:8])
            out_ref[lev, at] = jnp.concatenate([edge, x[:, 8:24]], 1).astype(BF16)
    acc = jnp.zeros((128, 128), F32)
    for (first, count), q_ref in zip(GROUPS, (qa_ref, qb_ref, qc_ref)):
        width = count * HD
        for n in range(3):
            cols = slice(n * D + first * HD, n * D + first * HD + width)
            part = q_ref[:, n * width : (n + 1) * width].astype(F32)
            gqkv_ref[:, cols] = part
            prod = part * wqkv_ref[:, cols].astype(F32)
            for k in range(0, width, 128):
                acc += prod[:, k : k + 128]
    ggain_ref[...] = jnp.sum(acc.T, axis=0, keepdims=True) / gain_ref[...]
    gout_ref[...] = e_ref[...].astype(F32)
    gdec_ref[...] = edec_ref[0:C].astype(F32)


VM = pl.BlockSpec(memory_space=pltpu.VMEM)
ANY = pl.BlockSpec(memory_space=pl.ANY)
SDS = jax.ShapeDtypeStruct
DMA = pltpu.SemaphoreType.DMA


SM = pl.BlockSpec(memory_space=pltpu.SMEM)


def sum_bufs(plan):
    rows, lanes, by_lanes, rp, lp, _ = plan
    rows, lanes = (rows, lanes // 2) if by_lanes else (rows // 2, lanes)
    band = rows // 8
    shapes = [(rows, lanes), (rows, lanes), (8, band, lanes), (band, lanes)]
    shapes.append((8, band // rp, lanes // lp))
    return [pltpu.VMEM(s, BF16) for s in shapes]


def fused_call(x, pts_t, slots, weights, counts, cells, gain, w_qkv, w_out, w_dec_t):
    def vm(*shape, dtype=BF16):
        return pltpu.VMEM(shape, dtype)

    return pl.pallas_call(
        fused_kernel,
        out_shape=(
            SDS(x.shape, BF16), SDS((768, D), BF16), SDS((D, 768), BF16), SDS((D, 384), BF16),
            SDS((D, 384), BF16), SDS((ER, D), BF16),
        ),
        in_specs=[ANY, VM, VM, VM, SM, VM, VM, ANY, ANY, VM],
        out_specs=(ANY, VM, VM, VM, VM, VM),
        scratch_shapes=[
            vm(2, 48, 24, D), vm(D, 3 * D), vm(D, D), DMA((3,)), DMA((3,)),
            vm(7, C, CAP), vm(BANDS, C, CAP), DMA((7,)), DMA((7,)),
            vm(768, D), vm(768, D), vm(768, D), DMA((8,)),
            vm(TOK, D), vm(TOK, D), vm(TOK, 3 * D),
            vm(TOK, 4 * WT), vm(TOK, 2 * WT), vm(TOK, 2 * WT), vm(TOK, D),
            vm(256, BANDS * CAP), vm(9 * C, BANDS * CAP), vm(C, TOK), vm(TOK, D, dtype=F32),
            vm(TOK, D), vm(TOK, D), vm(TOK, D), vm(HALF, D, dtype=F32),
            vm(D, 768), vm(D, 384), vm(D, 384), vm(ER, D),
            *sum_bufs(PLAN_4), *sum_bufs(PLAN_2), *sum_bufs(PLAN_2), *sum_bufs(PLAN_E),
            DMA((2, 26)), DMA((2, 26)), DMA((2, 26)), DMA((2, 26)),
        ],
        compiler_params=pltpu.CompilerParams(
            vmem_limit_bytes=62 << 20, collective_id=0, has_side_effects=True
        ),
        name="fused",
    )(x, pts_t, slots, weights, counts, cells, gain, w_qkv, w_out, w_dec_t)


def place_call(gx, arriving, qa, qb, qc, e, w_qkv, gain):
    def rows(lanes):
        return pl.BlockSpec((128, lanes), lambda i: (i, 0))

    grid_rows = pl.BlockSpec((2, 12, 24, D), lambda i: (0, i, 0, 0))
    across = pl.BlockSpec((1, 128), lambda i: (0, i))
    return pl.pallas_call(
        place_kernel,
        grid=(4,),
        out_shape=(
            SDS(gx.shape, BF16), SDS((D, 3 * D), F32), SDS((D, D), F32), SDS((C, D), F32),
            SDS((1, D), F32),
        ),
        in_specs=[
            grid_rows, pl.BlockSpec((192, D), lambda i: (i, 0)), rows(768), rows(384), rows(384),
            rows(D), pl.BlockSpec((128, D), lambda i: (4, 0)), rows(3 * D), across,
        ],
        out_specs=(grid_rows, rows(3 * D), rows(D), pl.BlockSpec((C, D), lambda i: (0, 0)), across),
        compiler_params=pltpu.CompilerParams(vmem_limit_bytes=60 << 20),
        name="place",
    )(gx, arriving, qa, qb, qc, e, e, w_qkv, gain)


def body(
    block_input, gain, w_qkv, w_out, w_dec, g_points, slot_point, slot_cell, slot_weight, pair_count
):
    parts = fused_call(
        block_input, g_points.T, slot_point, slot_weight, pair_count, slot_cell, gain[None],
        w_qkv, w_out, w_dec.T,
    )
    grad_x, g_qkv, g_out, g_dec, g_gain = place_call(*parts, w_qkv, gain[None])
    return (grad_x, g_qkv, g_out, g_dec.T, g_gain[0])


def solution(mesh):
    placed = (
        P(None, "lat", "lon", None),
        P(),
        P(),
        P(),
        P(),
        P(("lat", "lon"), None),
        P(("lat", "lon"), None),
        P(("lat", "lon"), None),
        P(("lat", "lon"), None),
        P(("lat", "lon")),
    )
    return jax.shard_map(
        body,
        mesh=mesh,
        in_specs=placed,
        out_specs=(P(None, "lat", "lon", None), P(), P(), P(), P()),
        check_vma=False,
    )
```

```python
import jax
import jax.numpy as jnp
from jax import lax
from jax.experimental import pallas as pl
from jax.experimental.pallas import tpu as pltpu
from jax.sharding import PartitionSpec as P

D = 512
HEADS = 8
HD = 64
WA = 6
WO = 12
WT = 144
C = 80
TOK = 2304
CAP = 512
BANDS = 8
PTS = 1024
SCALE = 0.125
F32 = jnp.float32
BF16 = jnp.bfloat16
NT = (((1,), (1,)), ((), ()))
TN = (((0,), (0,)), ((), ()))


def mm(a, b):
    return jnp.dot(a, b, preferred_element_type=F32)


def dg(a, b, dims):
    return lax.dot_general(a, b, dims, preferred_element_type=F32)


def onehot(idx_row, count):
    rows = lax.broadcasted_iota(jnp.int32, (count, idx_row.shape[1]), 0)
    return jnp.where(rows == idx_row, 1.0, 0.0).astype(BF16)


MESH = pl.DeviceIdType.MESH


def spot():
    return lax.axis_index("lat"), lax.axis_index("lon")


def device(lat, lon):
    return {"lat": lat, "lon": lon}


def greet(devices):
    barrier = pltpu.get_barrier_semaphore()
    for dev in devices:
        pl.semaphore_signal(barrier, inc=1, device_id=dev, device_id_type=MESH)
    pl.semaphore_wait(barrier, len(devices))


def remote(src, dst, send, recv, dev):
    return pltpu.make_async_remote_copy(
        src_ref=src, dst_ref=dst, send_sem=send, recv_sem=recv, device_id=dev, device_id_type=MESH
    )


def sub_iota(shape):
    return lax.broadcasted_iota(jnp.int32, shape, 1)


def norm_scale(x):
    return lax.rsqrt(jnp.mean(x * x, -1, keepdims=True) + 1e-06)


def steps_of(value, width, count):
    total = jnp.zeros_like(value)
    for n in range(1, count):
        total += jnp.where(value >= n * width, 1, 0)
    return total


def own_rows(cell):
    win = steps_of(cell, WT, 16)
    t = cell - win * WT
    r = steps_of(t, WO, 12)
    lo = t - r * WO
    low = r >= WA
    turn = jnp.where(low, 4, 0)
    mixed = 96 + (r - jnp.where(low, WA, 0)) * 8

    def wrap(v):
        return jnp.where(v >= 8, v - 8, v)

    a_row = jnp.where(
        (lo >= 2) & (lo < 10), r * 8 + lo - 2,
        mixed + wrap(jnp.where(lo < 2, lo + 6, lo - 10) + turn),
    )
    b_row = jnp.where(
        lo < 6, r * 8 + lo + 2,
        jnp.where(lo < 8, r * 8 + lo - 6, mixed + wrap(lo - 6 + turn)),
    )
    half = steps_of(win, 2, 8)
    second = win - half * 2
    return second * HALF + half * WT + jnp.where(second == 0, a_row, b_row)


NB = 8
HALF = NB * WT
GROUPS = ((0, 4), (4, 2), (6, 2))
ER = 640


def start(copies):
    for copy in copies:
        copy.start()
    return copies


def finish(copies):
    for copy in copies:
        copy.wait()


def total_of(buf, n):
    acc = buf[0].astype(F32)
    for i in range(1, n):
        acc = acc + buf[i].astype(F32)
    return acc.astype(BF16)


class Sum:
    def __init__(self, src, out, plan, bufs, sems):
        self.src, self.out = src, out
        self.buf_a, self.sum_b, self.buf_b, self.sum_c, self.buf_c = bufs
        self.sems = sems
        lat, lon = spot()
        self.lat, self.lon = lat, lon
        self.core, grp = lax.rem(lon, 2), lax.div(lon, 2)
        self.sib = lon + 1 - 2 * self.core
        self.rows, self.lanes, self.by_lanes, self.rp, self.lp, self.lat_first = plan
        self.hr = self.rows if self.by_lanes else self.rows // 2
        self.hl = self.lanes // 2 if self.by_lanes else self.lanes
        self.band = self.hr // 8
        self.pr, self.pl = self.band // self.rp, self.hl // self.lp
        self.one, self.two = (lat, grp) if self.lat_first else (grp, lat)
        self.step_no = 0

    def dev_one(self, n):
        if self.lat_first:
            return device(n, self.lon)
        return device(self.lat, n * 2 + self.core)

    def dev_two(self, n):
        if self.lat_first:
            return device(self.lat, n * 2 + self.core)
        return device(n, self.lon)

    def half(self, core):
        if self.by_lanes:
            return pl.ds(0, self.hr), pl.ds(pl.multiple_of(core * self.hl, 128), self.hl)
        return pl.ds(pl.multiple_of(core * self.hr, 16), self.hr), pl.ds(0, self.hl)

    def band_of(self, n):
        return pl.ds(pl.multiple_of(n * self.band, 16), self.band)

    def piece(self, n, row=0, lane=0):
        part = lax.rem(n, self.rp * self.lp)
        row = row + lax.rem(part, self.rp) * self.pr
        lane = lane + lax.div(part, self.rp) * self.pl
        return (
            pl.ds(pl.multiple_of(row, 16), self.pr), pl.ds(pl.multiple_of(lane, 128), self.pl)
        )

    def corner(self):
        row, lane = self.one * self.band, 0
        if self.by_lanes:
            lane = self.core * self.hl
        else:
            row = row + self.core * self.hr
        return row, lane

    def copy(self, src, dst, n, dev):
        return remote(src, dst, self.sems.at[0, n], self.sems.at[1, n], dev)

    def step(self):
        getattr(self, "step%d" % self.step_no)()
        self.step_no += 1

    def step0(self):
        src = self.src.at[self.half(1 - self.core)]
        self.flying = start([self.copy(src, self.buf_a, 0, device(self.lat, self.sib))])

    def step1(self):
        finish(self.flying)
        self.sum_b[...] = (
            self.src[self.half(self.core)].astype(F32) + self.buf_a[...].astype(F32)
        ).astype(BF16)
        self.flying = start([
            self.copy(
                self.sum_b.at[self.band_of(lax.rem(self.one + s, 8))], self.buf_b.at[self.one], s,
                self.dev_one(lax.rem(self.one + s, 8)),
            )
            for s in range(1, 8)
        ])
        self.buf_b[self.one] = self.sum_b[self.band_of(self.one)]

    def step2(self):
        finish(self.flying)
        self.sum_c[...] = total_of(self.buf_b, 8)
        self.flying = start([
            self.copy(
                self.sum_c.at[self.piece(lax.rem(self.two + s, 8))], self.buf_c.at[self.two],
                7 + s, self.dev_two(lax.rem(self.two + s, 8)),
            )
            for s in range(1, 8)
        ])
        self.buf_c[self.two] = self.sum_c[self.piece(self.two)]

    def step3(self):
        finish(self.flying)
        here = self.piece(self.two, *self.corner())
        self.out[here] = total_of(self.buf_c, 8)
        own = self.out.at[here]
        count = self.rp * self.lp
        first = self.two - lax.rem(self.two, count)
        self.flying = start([
            self.copy(own, own, 14 + s, self.dev_two(first + lax.rem(self.two + s, count)))
            for s in range(1, count)
        ])

    def step4(self):
        finish(self.flying)
        row, lane = self.corner()
        own = self.out.at[
            pl.ds(pl.multiple_of(row, 16), self.band), pl.ds(pl.multiple_of(lane, 128), self.hl)
        ]
        self.flying = start([
            self.copy(own, own, 17 + s, self.dev_one(lax.rem(self.one + s, 8)))
            for s in range(1, 8)
        ])

    def step5(self):
        finish(self.flying)
        own = self.out.at[self.half(self.core)]
        self.flying = start([self.copy(own, own, 25, device(self.lat, self.sib))])

    def step6(self):
        finish(self.flying)


PLAN_E = (ER, D, True, 1, 2, True)
PLAN_4 = (D, 768, True, 4, 1, False)
PLAN_2 = (D, 384, False, 2, 1, False)


def fused_kernel(
    x_hbm, pts_ref, slot_ref, weight_ref, count_ref, cell_ref, gain_ref, wqkv_hbm, wout_hbm,
    wdec_ref,
    gx_hbm, arrive_ref, qa_ref, qb_ref, qc_ref, e_ref,
    xv, wqkv, wout, load_sem, store_sem,
    sent, arr, asend, arecv, first, halo, edge, hsems,
    xw, nw, qkv, probs_a, probs_b, probs_c, att, oh, marr, gtt, dhf, dhb, datt, hid, dnf,
    src_a, src_b, src_c, src_e,
    a0, a1, a2, a3, a4, b0, b1, b2, b3, b4, c0, c1, c2, c3, c4, e0, e1, e2, e3, e4,
    sems_a, sems_b, sems_c, sems_e,
):
    lat, lon = spot()
    core, grp = lax.rem(lon, 2), lax.div(lon, 2)
    west, east = lax.rem(lon + 15, 16), lax.rem(lon + 1, 16)
    others = [lax.rem(lat + s, BANDS) for s in range(1, BANDS)]
    loads = start([
        pltpu.make_async_copy(x_hbm, xv, load_sem.at[0]),
        pltpu.make_async_copy(wqkv_hbm, wqkv, load_sem.at[1]),
        pltpu.make_async_copy(wout_hbm, wout, load_sem.at[2]),
    ])
    barrier = pltpu.get_barrier_semaphore()
    peers = (
        [device(lat, lon + 1 - 2 * core)]
        + [device(lat, lax.rem(grp + s, 8) * 2 + core) for s in range(1, 8)]
        + [device(o, lon) for o in others]
        + [device(lat, west), device(lat, east)]
    )
    for dev in peers:
        pl.semaphore_signal(barrier, inc=1, device_id=dev, device_id_type=MESH)

    sum_a = Sum(src_a, qa_ref, PLAN_4, (a0, a1, a2, a3, a4), sems_a)
    sum_b = Sum(src_b, qb_ref, PLAN_2, (b0, b1, b2, b3, b4), sems_b)
    sum_c = Sum(src_c, qc_ref, PLAN_2, (c0, c1, c2, c3, c4), sems_c)
    sum_e = Sum(src_e, e_ref, PLAN_E, (e0, e1, e2, e3, e4), sems_e)
    probs = (probs_a, probs_b, probs_c)

    pts = jnp.concatenate([pts_ref[:, n * 256 : (n + 1) * 256] for n in range(4)], axis=0)
    lane = lax.broadcasted_iota(jnp.int32, (1, CAP), 1)

    def rows_for(d):
        point = slot_ref[pl.ds(d, 1), :]
        quarter = steps_of(point, 256, 4)
        picked = mm(pts, onehot(point - quarter * 256, 256))
        rows = picked[0:C]
        for n in range(1, 4):
            rows = jnp.where(quarter == n, picked[n * C : (n + 1) * C], rows)
        live = lane < count_ref[d]
        return jnp.where(live, weight_ref[pl.ds(d, 1), :] * rows, 0.0).astype(BF16)

    for s, o in enumerate(others):
        sent[s] = rows_for(o)
    arr[lat] = rows_for(lat)
    loads[0].wait()

    @pl.loop(0, NB)
    def _(lb):
        for lev in range(2):
            rows = pl.ds(pl.multiple_of(lb * 96 + lev * 48, 16), 48)
            part = xv[lev, pl.ds(lb * WA, WA)].astype(F32)[:, 0:8]
            first[rows, :] = part.reshape(48, D).astype(BF16)

    pl.semaphore_wait(barrier, len(peers))
    in_copy = remote(first, halo, hsems.at[0], hsems.at[1], device(lat, west))
    in_copy.start()
    copies = start([
        remote(sent.at[s], arr.at[lat], asend.at[s], arecv.at[s], device(o, lon))
        for s, o in enumerate(others)
    ])

    gain = gain_ref[...]

    def put_window(rows, toks):
        xw[rows, :] = toks.astype(BF16)
        nw[rows, :] = (toks * norm_scale(toks) * gain).astype(BF16)

    def project(at):
        @pl.loop(0, 6)
        def _(c):
            cols = pl.ds(pl.multiple_of(c * 256, 256), 256)
            qkv[at : at + HALF, cols] = mm(nw[at : at + HALF, :], wqkv[:, cols]).astype(BF16)

    @pl.loop(0, NB)
    def _(lb):
        x0 = xv[0, pl.ds(lb * WA, WA)].astype(F32)
        x1 = xv[1, pl.ds(lb * WA, WA)].astype(F32)
        sub = sub_iota((WA, 8, D))
        c0 = jnp.where(sub >= 6, x0[:, 0:8], x0[:, 16:24])
        c1 = jnp.where(sub >= 6, x1[:, 0:8], x1[:, 16:24])
        mixed = jnp.where((sub < 2) | (sub >= 6), c0, pltpu.roll(c1, 4, 1))
        toks = jnp.concatenate([x0[:, 8:16], x1[:, 8:16], mixed], axis=0).reshape(WT, D)
        put_window(pl.ds(pl.multiple_of(lb * WT, WT), WT), toks)

    loads[1].wait()
    project(0)

    masks, picks = {}, {}
    for n in (4, 2):
        head = lax.broadcasted_iota(jnp.int32, (1, n * HD), 1) // HD
        masks[n] = [jnp.where(head == a, 1.0, 0.0).astype(BF16) for a in range(n)]
        picks[n] = [head == a for a in range(n)]

    def stack(a, n):
        return jnp.concatenate([a * m for m in masks[n]], axis=0)

    def pick(o, n):
        out = o[0:WT]
        for a in range(1, n):
            out = jnp.where(picks[n][a], o[a * WT : (a + 1) * WT], out)
        return out

    def col(part, g):
        at, n = GROUPS[g]
        return slice(part * D + at * HD, part * D + (at + n) * HD)

    def window(w):
        return pl.ds(pl.multiple_of(w * WT, WT), WT)

    def forward(w, some):
        todo = [(window(2 * w + i), g) for i in range(2) for g in some]
        scores = [
            dg(qkv[rows, col(1, g)], stack(qkv[rows, col(0, g)] * BF16(SCALE), GROUPS[g][1]), NT)
            for rows, g in todo
        ]
        pbs = []
        for st in scores:
            e = jnp.exp(st - jnp.max(st, axis=0, keepdims=True))
            pbs.append((e * (1.0 / jnp.sum(e, axis=0, keepdims=True))).astype(BF16))
        outs = [dg(pb, qkv[rows, col(2, g)], TN) for pb, (rows, g) in zip(pbs, todo)]
        for pb, o, (rows, g) in zip(pbs, outs, todo):
            probs[g][rows, :] = pb
            att[rows, col(0, g)] = pick(o, GROUPS[g][1]).astype(BF16)

    def forward_loop(lo, hi, some):
        @pl.loop(lo // 2, hi // 2)
        def _(w):
            forward(w, some)

    forward_loop(0, NB, (0,))

    in_copy.wait()

    @pl.loop(0, NB)
    def _(lb):
        at = pl.multiple_of(lb * 96, 16)
        h0 = halo[pl.ds(at, 48), :].astype(F32).reshape(WA, 8, D)
        h1 = halo[pl.ds(pl.multiple_of(at + 48, 16), 48), :].astype(F32).reshape(WA, 8, D)
        x0 = xv[0, pl.ds(lb * WA, WA)].astype(F32)
        x1 = xv[1, pl.ds(lb * WA, WA)].astype(F32)
        sub = sub_iota((WA, 8, D))
        w0 = jnp.where(sub < 2, h0, x0[:, 16:24])
        w1 = jnp.where(sub < 2, h1, x1[:, 16:24])
        mixed = jnp.where((sub < 2) | (sub >= 6), pltpu.roll(h1, 4, 1), h0)
        toks = jnp.concatenate([w0, w1, mixed], axis=0).reshape(WT, D)
        put_window(pl.ds(pl.multiple_of(HALF + lb * WT, WT), WT), toks)

    project(HALF)

    forward_loop(NB, 2 * NB, (0,))

    row = own_rows(cell_ref[...])
    block = steps_of(row, 256, 9)
    place = row - block * 256
    for i in range(BANDS):
        oh[:, i * CAP : (i + 1) * CAP] = onehot(place[i : i + 1, :], 256)
    finish(copies)
    for i in range(BANDS):
        part = arr[i]
        for b in range(9):
            mask = jnp.where(block[i : i + 1, :] == b, 1.0, 0.0).astype(BF16)
            marr[b * C : (b + 1) * C, i * CAP : (i + 1) * CAP] = part * mask
    toks = dg(marr[...], oh[...], NT).astype(BF16)
    for b in range(9):
        gtt[:, b * 256 : (b + 1) * 256] = toks[b * C : (b + 1) * C]
    loads[2].wait()

    @pl.loop(0, 3)
    def _(b):
        rows = pl.ds(pl.multiple_of(b * 768, 768), 768)
        dh = dg(gtt[:, rows], wdec_ref[...], TN)
        dhf[rows, :] = dh
        dhb[rows, :] = dh.astype(BF16)
        datt[rows, :] = dg(dh.astype(BF16), wout[...], NT).astype(BF16)

    def hidden_grads():
        @pl.loop(0, 3)
        def _(b):
            rows = pl.ds(pl.multiple_of(b * 768, 768), 768)
            hid[rows, :] = (xw[rows, :].astype(F32) + mm(att[rows, :], wout[...])).astype(BF16)

        src_e[0:D, :] = dg(att[...], dhb[...], TN).astype(BF16)
        src_e[D : D + C, :] = mm(gtt[...], hid[...]).astype(BF16)
        src_e[D + C : ER, :] = jnp.zeros((ER - D - C, D), BF16)

    def backward(w, g):
        n = GROUPS[g][1]
        todo = [window(2 * w + i) for i in range(2)]
        ks = [qkv[rows, col(1, g)] for rows in todo]
        qs = [stack(qkv[rows, col(0, g)] * BF16(SCALE), n) for rows in todo]
        ds = [stack(datt[rows, col(0, g)], n) for rows in todo]
        pbs = [probs[g][rows, :] for rows in todo]
        dps = [dg(qkv[rows, col(2, g)], d, NT) for rows, d in zip(todo, ds)]
        dvs = [mm(pb, d) for pb, d in zip(pbs, ds)]
        dsts = []
        for pb, dp in zip(pbs, dps):
            p = pb.astype(F32)
            t = jnp.sum(p * dp, axis=0, keepdims=True)
            dsts.append((p * (dp - t)).astype(BF16))
        dks = [mm(dst, q) for dst, q in zip(dsts, qs)]
        dqs = [pick(dg(dst, k, TN), n) * SCALE for dst, k in zip(dsts, ks)]
        for rows, dq, dk, dv in zip(todo, dqs, dks, dvs):
            qkv[rows, col(0, g)] = dq.astype(BF16)
            qkv[rows, col(1, g)] = dk.astype(BF16)
            qkv[rows, col(2, g)] = dv.astype(BF16)

    def back_loop(lo, hi, g):
        @pl.loop(lo // 2, hi // 2)
        def _(w):
            backward(w, g)

    def weight_grad(src, g):
        width = GROUPS[g][1] * HD
        for n in range(3):
            part = dg(nw[...], qkv[:, col(n, g)], TN)
            src[:, n * width : (n + 1) * width] = part.astype(BF16)

    back_loop(0, 16, 0)
    weight_grad(src_a, 0)
    sum_a.step()
    forward_loop(0, 8, (1, 2))
    sum_a.step()
    forward_loop(8, 16, (1, 2))
    hidden_grads()
    sum_e.step()
    sum_a.step()
    back_loop(0, 16, 1)
    sum_e.step()
    sum_a.step()
    weight_grad(src_b, 1)
    sum_b.step()
    back_loop(0, 8, 2)
    sum_a.step()
    back_loop(8, 16, 2)
    sum_b.step()
    weight_grad(src_c, 2)
    sum_c.step()
    sum_e.step()

    sub = sub_iota((WA, 8, D))

    def project_back(at):
        for n in range(2):
            cols = slice(n * 256, (n + 1) * 256)
            dnf[:, cols] = dg(qkv[at : at + HALF, :], wqkv[cols, :], NT)

    def input_grad(at, lb):
        rows = pl.ds(pl.multiple_of(at + lb * WT, WT), WT)
        x = xw[rows, :].astype(F32)
        r = norm_scale(x)
        dng = dnf[window(lb), :] * gain
        mean = jnp.mean(dng * x, -1, keepdims=True)
        y = dhf[rows, :] + r * (dng - x * (r * r * mean))
        return y.reshape(18, 8, D)

    outs = []

    def second_windows(lo, hi, n):
        @pl.loop(lo, hi)
        def _(lb):
            y = input_grad(HALF, lb)
            mix = y[12:18]
            turned = pltpu.roll(mix, 4, 1)
            at = pl.ds(lb * WA, WA)
            for lev, m in enumerate((mix, turned)):
                main = y[lev * 6 : lev * 6 + 6]
                xv[lev, at] = jnp.concatenate([main, main, main], 1).astype(BF16)
                here = pl.ds(pl.multiple_of(lb * 96 + lev * 48, 16), 48)
                edge[here, :] = jnp.where(sub < 2, main, m).reshape(48, D).astype(BF16)

        rows = pl.ds(lo * 96, (hi - lo) * 96)
        outs.append(remote(
            edge.at[rows], arrive_ref.at[rows], hsems.at[2 + 2 * n], hsems.at[3 + 2 * n],
            device(lat, east),
        ))
        outs[-1].start()

    def first_windows(lo, hi, n):
        @pl.loop(lo, hi)
        def _(lb):
            y = input_grad(0, lb)
            mix = y[12:18]
            turned = pltpu.roll(mix, 4, 1)
            at = pl.ds(lb * WA, WA)
            for lev, m in enumerate((mix, turned)):
                main = y[lev * 6 : lev * 6 + 6]
                right = jnp.where(sub < 2, m, xv[lev, at].astype(F32)[:, 16:24])
                xv[lev, at] = jnp.concatenate([m, main, right], 1).astype(BF16)

        at = pl.ds(lo * WA, (hi - lo) * WA)
        outs.append(pltpu.make_async_copy(xv.at[:, at], gx_hbm.at[:, at], store_sem.at[n]))
        outs[-1].start()

    project_back(HALF)
    second_windows(0, 4, 0)
    sum_c.step()
    sum_e.step()
    sum_a.step()
    second_windows(4, 8, 1)
    sum_b.step()
    project_back(0)
    sum_e.step()
    sum_a.step()
    first_windows(0, 4, 0)
    sum_b.step()
    first_windows(4, 8, 1)
    sum_c.step()
    sum_b.step()
    sum_c.step()
    sum_e.step()
    sum_c.step()
    sum_b.step()
    sum_c.step()
    sum_e.step()
    sum_b.step()
    sum_c.step()
    finish(outs)


def place_kernel(
    gx_ref, arrive_ref, qa_ref, qb_ref, qc_ref, e_ref, edec_ref, wqkv_ref, gain_ref,
    out_ref, gqkv_ref, gout_ref, gdec_ref, ggain_ref, gains,
):
    sub = sub_iota((WA, 8, D))
    for lev in range(2):
        x = gx_ref[lev].astype(F32)
        new = arrive_ref[lev * 48 : lev * 48 + 48].astype(F32)
        edge = jnp.where(sub < 6, new.reshape(WA, 8, D), x[:, 0:8])
        out_ref[lev] = jnp.concatenate([edge, x[:, 8:24]], 1).astype(BF16)
    acc = jnp.zeros((64, 128), F32)
    for (first, count), q_ref in zip(GROUPS, (qa_ref, qb_ref, qc_ref)):
        width = count * HD
        for n in range(3):
            cols = slice(n * D + first * HD, n * D + first * HD + width)
            part = q_ref[:, n * width : (n + 1) * width].astype(F32)
            gqkv_ref[:, cols] = part
            prod = part * wqkv_ref[:, cols].astype(F32)
            for k in range(0, width, 128):
                acc += prod[:, k : k + 128]
    step = pl.program_id(0)
    gains[pl.ds(pl.multiple_of(step * 64, 64), 64), :] = acc

    @pl.when(step == 7)
    def _():
        ggain_ref[...] = jnp.sum(gains[...].T, axis=0, keepdims=True) / gain_ref[...]

    gout_ref[...] = e_ref[...].astype(F32)
    gdec_ref[...] = edec_ref[0:C].astype(F32)


VM = pl.BlockSpec(memory_space=pltpu.VMEM)
ANY = pl.BlockSpec(memory_space=pl.ANY)
SDS = jax.ShapeDtypeStruct
DMA = pltpu.SemaphoreType.DMA


SM = pl.BlockSpec(memory_space=pltpu.SMEM)


def sum_bufs(plan):
    rows, lanes, by_lanes, rp, lp, _ = plan
    rows, lanes = (rows, lanes // 2) if by_lanes else (rows // 2, lanes)
    band = rows // 8
    shapes = [(rows, lanes), (rows, lanes), (8, band, lanes), (band, lanes)]
    shapes.append((8, band // rp, lanes // lp))
    return [pltpu.VMEM(s, BF16) for s in shapes]


def fused_call(x, pts_t, slots, weights, counts, cells, gain, w_qkv, w_out, w_dec_t):
    def vm(*shape, dtype=BF16):
        return pltpu.VMEM(shape, dtype)

    return pl.pallas_call(
        fused_kernel,
        out_shape=(
            SDS(x.shape, BF16), SDS((768, D), BF16), SDS((D, 768), BF16), SDS((D, 384), BF16),
            SDS((D, 384), BF16), SDS((ER, D), BF16),
        ),
        in_specs=[ANY, VM, VM, VM, SM, VM, VM, ANY, ANY, VM],
        out_specs=(ANY, VM, VM, VM, VM, VM),
        scratch_shapes=[
            vm(2, 48, 24, D), vm(D, 3 * D), vm(D, D), DMA((3,)), DMA((3,)),
            vm(7, C, CAP), vm(BANDS, C, CAP), DMA((7,)), DMA((7,)),
            vm(768, D), vm(768, D), vm(768, D), DMA((8,)),
            vm(TOK, D), vm(TOK, D), vm(TOK, 3 * D),
            vm(TOK, 4 * WT), vm(TOK, 2 * WT), vm(TOK, 2 * WT), vm(TOK, D),
            vm(256, BANDS * CAP), vm(9 * C, BANDS * CAP), vm(C, TOK), vm(TOK, D, dtype=F32),
            vm(TOK, D), vm(TOK, D), vm(TOK, D), vm(HALF, D, dtype=F32),
            vm(D, 768), vm(D, 384), vm(D, 384), vm(ER, D),
            *sum_bufs(PLAN_4), *sum_bufs(PLAN_2), *sum_bufs(PLAN_2), *sum_bufs(PLAN_E),
            DMA((2, 26)), DMA((2, 26)), DMA((2, 26)), DMA((2, 26)),
        ],
        compiler_params=pltpu.CompilerParams(
            vmem_limit_bytes=62 << 20, collective_id=0, has_side_effects=True
        ),
        name="fused",
    )(x, pts_t, slots, weights, counts, cells, gain, w_qkv, w_out, w_dec_t)


def place_call(gx, arriving, qa, qb, qc, e, w_qkv, gain):
    def rows(lanes):
        return pl.BlockSpec((64, lanes), lambda i: (i, 0))

    grid_rows = pl.BlockSpec((2, WA, 24, D), lambda i: (0, i, 0, 0))
    across = pl.BlockSpec((1, D), lambda i: (0, 0))
    return pl.pallas_call(
        place_kernel,
        grid=(8,),
        out_shape=(
            SDS(gx.shape, BF16), SDS((D, 3 * D), F32), SDS((D, D), F32), SDS((C, D), F32),
            SDS((1, D), F32),
        ),
        in_specs=[
            grid_rows, pl.BlockSpec((96, D), lambda i: (i, 0)), rows(768), rows(384), rows(384),
            rows(D), pl.BlockSpec((128, D), lambda i: (4, 0)), rows(3 * D), across,
        ],
        out_specs=(grid_rows, rows(3 * D), rows(D), pl.BlockSpec((C, D), lambda i: (0, 0)), across),
        scratch_shapes=[pltpu.VMEM((D, 128), F32)],
        compiler_params=pltpu.CompilerParams(vmem_limit_bytes=60 << 20),
        name="place",
    )(gx, arriving, qa, qb, qc, e, e, w_qkv, gain)


def body(
    block_input, gain, w_qkv, w_out, w_dec, g_points, slot_point, slot_cell, slot_weight, pair_count
):
    parts = fused_call(
        block_input, g_points.T, slot_point, slot_weight, pair_count, slot_cell, gain[None],
        w_qkv, w_out, w_dec.T,
    )
    grad_x, g_qkv, g_out, g_dec, g_gain = place_call(*parts, w_qkv, gain[None])
    return (grad_x, g_qkv, g_out, g_dec.T, g_gain[0])


def solution(mesh):
    placed = (
        P(None, "lat", "lon", None),
        P(),
        P(),
        P(),
        P(),
        P(("lat", "lon"), None),
        P(("lat", "lon"), None),
        P(("lat", "lon"), None),
        P(("lat", "lon"), None),
        P(("lat", "lon")),
    )
    return jax.shard_map(
        body,
        mesh=mesh,
        in_specs=placed,
        out_specs=(P(None, "lat", "lon", None), P(), P(), P(), P()),
        check_vma=False,
    )
```

```python
import jax
import jax.numpy as jnp
from jax import lax
from jax.experimental import pallas as pl
from jax.experimental.pallas import tpu as pltpu
from jax.sharding import PartitionSpec as P

D = 512
HEADS = 8
HD = 64
WA = 6
WO = 12
WT = 144
C = 80
TOK = 2304
CAP = 512
BANDS = 8
PTS = 1024
SCALE = 0.125
F32 = jnp.float32
BF16 = jnp.bfloat16
NT = (((1,), (1,)), ((), ()))
TN = (((0,), (0,)), ((), ()))


def mm(a, b):
    return jnp.dot(a, b, preferred_element_type=F32)


def dg(a, b, dims):
    return lax.dot_general(a, b, dims, preferred_element_type=F32)


def onehot(idx_row, count):
    rows = lax.broadcasted_iota(jnp.int32, (count, idx_row.shape[1]), 0)
    return jnp.where(rows == idx_row, 1.0, 0.0).astype(BF16)


MESH = pl.DeviceIdType.MESH


def spot():
    return lax.axis_index("lat"), lax.axis_index("lon")


def device(lat, lon):
    return {"lat": lat, "lon": lon}


def greet(devices):
    barrier = pltpu.get_barrier_semaphore()
    for dev in devices:
        pl.semaphore_signal(barrier, inc=1, device_id=dev, device_id_type=MESH)
    pl.semaphore_wait(barrier, len(devices))


def remote(src, dst, send, recv, dev):
    return pltpu.make_async_remote_copy(
        src_ref=src, dst_ref=dst, send_sem=send, recv_sem=recv, device_id=dev, device_id_type=MESH
    )


def sub_iota(shape):
    return lax.broadcasted_iota(jnp.int32, shape, 1)


def norm_scale(x):
    return lax.rsqrt(jnp.mean(x * x, -1, keepdims=True) + 1e-06)


def steps_of(value, width, count):
    total = jnp.zeros_like(value)
    for n in range(1, count):
        total += jnp.where(value >= n * width, 1, 0)
    return total


def own_rows(cell):
    win = steps_of(cell, WT, 16)
    t = cell - win * WT
    r = steps_of(t, WO, 12)
    lo = t - r * WO
    low = r >= WA
    turn = jnp.where(low, 4, 0)
    mixed = 96 + (r - jnp.where(low, WA, 0)) * 8

    def wrap(v):
        return jnp.where(v >= 8, v - 8, v)

    a_row = jnp.where(
        (lo >= 2) & (lo < 10), r * 8 + lo - 2,
        mixed + wrap(jnp.where(lo < 2, lo + 6, lo - 10) + turn),
    )
    b_row = jnp.where(
        lo < 6, r * 8 + lo + 2,
        jnp.where(lo < 8, r * 8 + lo - 6, mixed + wrap(lo - 6 + turn)),
    )
    half = steps_of(win, 2, 8)
    second = win - half * 2
    return second * HALF + half * WT + jnp.where(second == 0, a_row, b_row)


NB = 8
HALF = NB * WT
GROUPS = ((0, 4), (4, 2), (6, 2))
ER = 640


def start(copies):
    for copy in copies:
        copy.start()
    return copies


def finish(copies):
    for copy in copies:
        copy.wait()


def total_of(buf, n):
    acc = buf[0].astype(F32)
    for i in range(1, n):
        acc = acc + buf[i].astype(F32)
    return acc.astype(BF16)


class Sum:
    def __init__(self, src, out, plan, bufs, sems):
        self.src, self.out = src, out
        self.buf_a, self.sum_b, self.buf_b, self.sum_c, self.buf_c, self.buf_d = bufs
        self.sems = sems
        lat, lon = spot()
        self.lat, self.lon = lat, lon
        self.core = lax.rem(lon, 2)
        self.z, self.y = lax.div(lon, 4), lax.rem(lat, 4)
        self.xlo, self.xhi = lax.rem(lax.div(lon, 2), 2), lax.div(lat, 4)
        self.x = self.xhi * 2 + self.xlo
        self.sib = lon + 1 - 2 * self.core
        self.rows, self.lanes, self.by_lanes, self.rp, self.lp, self.y_first = plan
        self.hr = self.rows if self.by_lanes else self.rows // 2
        self.hl = self.lanes // 2 if self.by_lanes else self.lanes
        self.band = self.hr // 4
        self.pr, self.pl = self.band // self.rp, self.hl // self.lp
        self.one, self.two = (self.y, self.z) if self.y_first else (self.z, self.y)
        self.step_no = 0

    def at_z(self, n):
        return device(self.lat, n * 4 + lax.rem(self.lon, 4))

    def at_y(self, n):
        return device(self.xhi * 4 + n, self.lon)

    def at_x(self, n):
        return device(
            lax.div(n, 2) * 4 + self.y, self.z * 4 + lax.rem(n, 2) * 2 + self.core
        )

    def dev_one(self, n):
        return self.at_y(n) if self.y_first else self.at_z(n)

    def dev_two(self, n):
        return self.at_z(n) if self.y_first else self.at_y(n)

    def half(self, core):
        if self.by_lanes:
            return pl.ds(0, self.hr), pl.ds(pl.multiple_of(core * self.hl, 128), self.hl)
        return pl.ds(pl.multiple_of(core * self.hr, 16), self.hr), pl.ds(0, self.hl)

    def band_of(self, n):
        return pl.ds(pl.multiple_of(n * self.band, 16), self.band)

    def piece(self, n, row=0, lane=0):
        row = row + lax.rem(n, self.rp) * self.pr
        lane = lane + lax.div(n, self.rp) * self.pl
        return (
            pl.ds(pl.multiple_of(row, 16), self.pr), pl.ds(pl.multiple_of(lane, 128), self.pl)
        )

    def corner(self):
        row, lane = self.one * self.band, 0
        if self.by_lanes:
            lane = self.core * self.hl
        else:
            row = row + self.core * self.hr
        return row, lane

    def copy(self, src, dst, n, dev):
        return remote(src, dst, self.sems.at[0, n], self.sems.at[1, n], dev)

    def step(self):
        getattr(self, "step%d" % self.step_no)()
        self.step_no += 1

    def step0(self):
        src = self.src.at[self.half(1 - self.core)]
        self.flying = start([self.copy(src, self.buf_a, 0, device(self.lat, self.sib))])

    def step1(self):
        finish(self.flying)
        self.sum_b[...] = (
            self.src[self.half(self.core)].astype(F32) + self.buf_a[...].astype(F32)
        ).astype(BF16)
        peers = [lax.rem(self.one + s, 4) for s in range(1, 4)]
        self.flying = start([
            self.copy(self.sum_b.at[self.band_of(o)], self.buf_b.at[self.one], 1 + s, self.dev_one(o))
            for s, o in enumerate(peers)
        ])
        self.buf_b[self.one] = self.sum_b[self.band_of(self.one)]

    def step2(self):
        finish(self.flying)
        self.sum_c[...] = total_of(self.buf_b, 4)
        peers = [lax.rem(self.two + s, 4) for s in range(1, 4)]
        self.flying = start([
            self.copy(self.sum_c.at[self.piece(o)], self.buf_c.at[self.two], 4 + s, self.dev_two(o))
            for s, o in enumerate(peers)
        ])
        self.buf_c[self.two] = self.sum_c[self.piece(self.two)]

    def step3(self):
        finish(self.flying)
        self.buf_d[self.x] = total_of(self.buf_c, 4)
        own = self.buf_d.at[self.x]
        self.flying = start([
            self.copy(own, own, 7 + s, self.at_x(lax.rem(self.x + 1 + s, 4))) for s in range(3)
        ])

    def step4(self):
        finish(self.flying)
        here = self.piece(self.two, *self.corner())
        self.out[here] = total_of(self.buf_d, 4)
        own = self.out.at[here]
        self.flying = start([
            self.copy(own, own, 10 + s, self.dev_two(lax.rem(self.two + 1 + s, 4)))
            for s in range(3)
        ])

    def step5(self):
        finish(self.flying)
        row, lane = self.corner()
        own = self.out.at[
            pl.ds(pl.multiple_of(row, 16), self.band), pl.ds(pl.multiple_of(lane, 128), self.hl)
        ]
        self.flying = start([
            self.copy(own, own, 13 + s, self.dev_one(lax.rem(self.one + 1 + s, 4)))
            for s in range(3)
        ])

    def step6(self):
        finish(self.flying)
        own = self.out.at[self.half(self.core)]
        self.flying = start([self.copy(own, own, 16, device(self.lat, self.sib))])

    def step7(self):
        finish(self.flying)


PLAN_E = (ER, D, True, 2, 2, True)
PLAN_4 = (D, 768, True, 4, 1, False)
PLAN_2 = (D, 384, False, 4, 1, False)
PLAN_2Y = (D, 384, False, 4, 1, True)


def fused_kernel(
    x_hbm, pts_ref, slot_ref, weight_ref, count_ref, cell_ref, gain_ref, wqkv_hbm, wout_hbm,
    wdec_ref,
    gx_hbm, arrive_ref, qa_ref, qb_ref, qc_ref, e_ref,
    xv, wqkv, wout, load_sem, store_sem,
    sent, arr, asend, arecv, first, halo, edge, hsems,
    xw, nw, qkv, probs_a, probs_b, probs_c, att, oh, marr, gtt, dhf, dhb, datt, hid, dnf,
    src_a, src_b, src_c, src_e,
    a0, a1, a2, a3, a4, a5, b0, b1, b2, b3, b4, b5, c0, c1, c2, c3, c4, c5, e0, e1, e2, e3, e4, e5,
    sems_a, sems_b, sems_c, sems_e,
):
    lat, lon = spot()
    core = lax.rem(lon, 2)
    flip = lon + 2 - 4 * lax.rem(lax.div(lon, 2), 2)
    west, east = lax.rem(lon + 15, 16), lax.rem(lon + 1, 16)
    others = [lax.rem(lat + s, BANDS) for s in range(1, BANDS)]
    loads = start([
        pltpu.make_async_copy(x_hbm, xv, load_sem.at[0]),
        pltpu.make_async_copy(wqkv_hbm, wqkv, load_sem.at[1]),
        pltpu.make_async_copy(wout_hbm, wout, load_sem.at[2]),
    ])
    barrier = pltpu.get_barrier_semaphore()
    peers = (
        [device(lat, lon + 1 - 2 * core)]
        + [device(lat, lax.rem(lon + 4 * s, 16)) for s in range(1, 4)]
        + [device(o, flip) for o in (lat, lax.rem(lat + 4, BANDS))]
        + [device(o, lon) for o in others]
        + [device(lat, west), device(lat, east)]
    )
    for dev in peers:
        pl.semaphore_signal(barrier, inc=1, device_id=dev, device_id_type=MESH)

    sum_a = Sum(src_a, qa_ref, PLAN_4, (a0, a1, a2, a3, a4, a5), sems_a)
    sum_b = Sum(src_b, qb_ref, PLAN_2, (b0, b1, b2, b3, b4, b5), sems_b)
    sum_c = Sum(src_c, qc_ref, PLAN_2Y, (c0, c1, c2, c3, c4, c5), sems_c)
    sum_e = Sum(src_e, e_ref, PLAN_E, (e0, e1, e2, e3, e4, e5), sems_e)
    probs = (probs_a, probs_b, probs_c)

    pts = jnp.concatenate([pts_ref[:, n * 256 : (n + 1) * 256] for n in range(4)], axis=0)
    lane = lax.broadcasted_iota(jnp.int32, (1, CAP), 1)

    def rows_for(d):
        point = slot_ref[pl.ds(d, 1), :]
        quarter = steps_of(point, 256, 4)
        picked = mm(pts, onehot(point - quarter * 256, 256))
        rows = picked[0:C]
        for n in range(1, 4):
            rows = jnp.where(quarter == n, picked[n * C : (n + 1) * C], rows)
        live = lane < count_ref[d]
        return jnp.where(live, weight_ref[pl.ds(d, 1), :] * rows, 0.0).astype(BF16)

    loads[0].wait()

    @pl.loop(0, NB)
    def _(lb):
        for lev in range(2):
            rows = pl.ds(pl.multiple_of(lb * 96 + lev * 48, 16), 48)
            part = xv[lev, pl.ds(lb * WA, WA)].astype(F32)[:, 0:8]
            first[rows, :] = part.reshape(48, D).astype(BF16)

    pl.semaphore_wait(barrier, len(peers))
    in_copy = remote(first, halo, hsems.at[0], hsems.at[1], device(lat, west))
    in_copy.start()
    copies = []
    for s, o in enumerate(others):
        sent[s] = rows_for(o)
        copies += start([remote(sent.at[s], arr.at[lat], asend.at[s], arecv.at[s], device(o, lon))])
    arr[lat] = rows_for(lat)

    gain = gain_ref[...]

    def put_window(rows, toks):
        xw[rows, :] = toks.astype(BF16)
        nw[rows, :] = (toks * norm_scale(toks) * gain).astype(BF16)

    def project(at):
        @pl.loop(0, 6)
        def _(c):
            cols = pl.ds(pl.multiple_of(c * 256, 256), 256)
            qkv[at : at + HALF, cols] = mm(nw[at : at + HALF, :], wqkv[:, cols]).astype(BF16)

    @pl.loop(0, NB)
    def _(lb):
        x0 = xv[0, pl.ds(lb * WA, WA)].astype(F32)
        x1 = xv[1, pl.ds(lb * WA, WA)].astype(F32)
        sub = sub_iota((WA, 8, D))
        c0 = jnp.where(sub >= 6, x0[:, 0:8], x0[:, 16:24])
        c1 = jnp.where(sub >= 6, x1[:, 0:8], x1[:, 16:24])
        mixed = jnp.where((sub < 2) | (sub >= 6), c0, pltpu.roll(c1, 4, 1))
        toks = jnp.concatenate([x0[:, 8:16], x1[:, 8:16], mixed], axis=0).reshape(WT, D)
        put_window(pl.ds(pl.multiple_of(lb * WT, WT), WT), toks)

    loads[1].wait()
    project(0)

    masks, picks = {}, {}
    for n in (4, 2):
        head = lax.broadcasted_iota(jnp.int32, (1, n * HD), 1) // HD
        masks[n] = [jnp.where(head == a, 1.0, 0.0).astype(BF16) for a in range(n)]
        picks[n] = [head == a for a in range(n)]

    def stack(a, n):
        return jnp.concatenate([a * m for m in masks[n]], axis=0)

    def pick(o, n):
        out = o[0:WT]
        for a in range(1, n):
            out = jnp.where(picks[n][a], o[a * WT : (a + 1) * WT], out)
        return out

    def col(part, g):
        at, n = GROUPS[g]
        return slice(part * D + at * HD, part * D + (at + n) * HD)

    def window(w):
        return pl.ds(pl.multiple_of(w * WT, WT), WT)

    def forward(w, some):
        todo = [(window(2 * w + i), g) for i in range(2) for g in some]
        scores = [
            dg(qkv[rows, col(1, g)], stack(qkv[rows, col(0, g)] * BF16(SCALE), GROUPS[g][1]), NT)
            for rows, g in todo
        ]
        pbs = []
        for st in scores:
            e = jnp.exp(st - jnp.max(st, axis=0, keepdims=True))
            pbs.append((e * (1.0 / jnp.sum(e, axis=0, keepdims=True))).astype(BF16))
        outs = [dg(pb, qkv[rows, col(2, g)], TN) for pb, (rows, g) in zip(pbs, todo)]
        for pb, o, (rows, g) in zip(pbs, outs, todo):
            probs[g][rows, :] = pb
            att[rows, col(0, g)] = pick(o, GROUPS[g][1]).astype(BF16)

    def forward_loop(lo, hi, some):
        @pl.loop(lo // 2, hi // 2)
        def _(w):
            forward(w, some)

    forward_loop(0, NB, (0,))
    forward_loop(0, NB, (1, 2))
    in_copy.wait()

    @pl.loop(0, NB)
    def _(lb):
        at = pl.multiple_of(lb * 96, 16)
        h0 = halo[pl.ds(at, 48), :].astype(F32).reshape(WA, 8, D)
        h1 = halo[pl.ds(pl.multiple_of(at + 48, 16), 48), :].astype(F32).reshape(WA, 8, D)
        x0 = xv[0, pl.ds(lb * WA, WA)].astype(F32)
        x1 = xv[1, pl.ds(lb * WA, WA)].astype(F32)
        sub = sub_iota((WA, 8, D))
        w0 = jnp.where(sub < 2, h0, x0[:, 16:24])
        w1 = jnp.where(sub < 2, h1, x1[:, 16:24])
        mixed = jnp.where((sub < 2) | (sub >= 6), pltpu.roll(h1, 4, 1), h0)
        toks = jnp.concatenate([w0, w1, mixed], axis=0).reshape(WT, D)
        put_window(pl.ds(pl.multiple_of(HALF + lb * WT, WT), WT), toks)

    project(HALF)

    forward_loop(NB, 2 * NB, (0,))

    row = own_rows(cell_ref[...])
    block = steps_of(row, 256, 9)
    place = row - block * 256
    for i in range(BANDS):
        oh[:, i * CAP : (i + 1) * CAP] = onehot(place[i : i + 1, :], 256)
    finish(copies)
    for i in range(BANDS):
        part = arr[i]
        for b in range(9):
            mask = jnp.where(block[i : i + 1, :] == b, 1.0, 0.0).astype(BF16)
            marr[b * C : (b + 1) * C, i * CAP : (i + 1) * CAP] = part * mask
    toks = dg(marr[...], oh[...], NT).astype(BF16)
    for b in range(9):
        gtt[:, b * 256 : (b + 1) * 256] = toks[b * C : (b + 1) * C]
    loads[2].wait()

    @pl.loop(0, 3)
    def _(b):
        rows = pl.ds(pl.multiple_of(b * 768, 768), 768)
        dh = dg(gtt[:, rows], wdec_ref[...], TN)
        dhf[rows, :] = dh
        dhb[rows, :] = dh.astype(BF16)
        datt[rows, :] = dg(dh.astype(BF16), wout[...], NT).astype(BF16)

    def hidden_grads():
        @pl.loop(0, 3)
        def _(b):
            rows = pl.ds(pl.multiple_of(b * 768, 768), 768)
            hid[rows, :] = (xw[rows, :].astype(F32) + mm(att[rows, :], wout[...])).astype(BF16)

        src_e[0:D, :] = dg(att[...], dhb[...], TN).astype(BF16)
        src_e[D : D + C, :] = mm(gtt[...], hid[...]).astype(BF16)
        src_e[D + C : ER, :] = jnp.zeros((ER - D - C, D), BF16)

    def backward(w, g):
        n = GROUPS[g][1]
        todo = [window(2 * w + i) for i in range(2)]
        ks = [qkv[rows, col(1, g)] for rows in todo]
        qs = [stack(qkv[rows, col(0, g)] * BF16(SCALE), n) for rows in todo]
        ds = [stack(datt[rows, col(0, g)], n) for rows in todo]
        pbs = [probs[g][rows, :] for rows in todo]
        dps = [dg(qkv[rows, col(2, g)], d, NT) for rows, d in zip(todo, ds)]
        dvs = [mm(pb, d) for pb, d in zip(pbs, ds)]
        dsts = []
        for pb, dp in zip(pbs, dps):
            p = pb.astype(F32)
            t = jnp.sum(p * dp, axis=0, keepdims=True)
            dsts.append((p * (dp - t)).astype(BF16))
        dks = [mm(dst, q) for dst, q in zip(dsts, qs)]
        dqs = [pick(dg(dst, k, TN), n) * SCALE for dst, k in zip(dsts, ks)]
        for rows, dq, dk, dv in zip(todo, dqs, dks, dvs):
            qkv[rows, col(0, g)] = dq.astype(BF16)
            qkv[rows, col(1, g)] = dk.astype(BF16)
            qkv[rows, col(2, g)] = dv.astype(BF16)

    def back_loop(lo, hi, g):
        @pl.loop(lo // 2, hi // 2)
        def _(w):
            backward(w, g)

    def weight_grad(src, g):
        width = GROUPS[g][1] * HD
        for n in range(3):
            part = dg(nw[...], qkv[:, col(n, g)], TN)
            src[:, n * width : (n + 1) * width] = part.astype(BF16)

    back_loop(0, 16, 0)
    weight_grad(src_a, 0)
    sum_a.step()
    forward_loop(8, 16, (1, 2))
    sum_a.step()
    hidden_grads()
    sum_e.step()
    back_loop(0, 8, 1)
    sum_a.step()
    sum_e.step()
    back_loop(8, 16, 1)
    sum_a.step()
    weight_grad(src_b, 1)
    sum_b.step()
    sum_e.step()
    back_loop(0, 8, 2)
    sum_a.step()
    sum_b.step()
    sum_e.step()
    back_loop(8, 16, 2)
    sum_a.step()
    sum_e.step()
    weight_grad(src_c, 2)
    sum_c.step()
    sum_b.step()

    sub = sub_iota((WA, 8, D))

    def project_back(at):
        for n in range(2):
            cols = slice(n * 256, (n + 1) * 256)
            dnf[:, cols] = dg(qkv[at : at + HALF, :], wqkv[cols, :], NT)

    def input_grad(at, lb):
        rows = pl.ds(pl.multiple_of(at + lb * WT, WT), WT)
        x = xw[rows, :].astype(F32)
        r = norm_scale(x)
        dng = dnf[window(lb), :] * gain
        mean = jnp.mean(dng * x, -1, keepdims=True)
        y = dhf[rows, :] + r * (dng - x * (r * r * mean))
        return y.reshape(18, 8, D)

    outs = []

    def second_windows(lo, hi, n):
        @pl.loop(lo, hi)
        def _(lb):
            y = input_grad(HALF, lb)
            mix = y[12:18]
            turned = pltpu.roll(mix, 4, 1)
            at = pl.ds(lb * WA, WA)
            for lev, m in enumerate((mix, turned)):
                main = y[lev * 6 : lev * 6 + 6]
                xv[lev, at] = jnp.concatenate([main, main, main], 1).astype(BF16)
                here = pl.ds(pl.multiple_of(lb * 96 + lev * 48, 16), 48)
                edge[here, :] = jnp.where(sub < 2, main, m).reshape(48, D).astype(BF16)

        rows = pl.ds(lo * 96, (hi - lo) * 96)
        outs.append(remote(
            edge.at[rows], arrive_ref.at[rows], hsems.at[2 + 2 * n], hsems.at[3 + 2 * n],
            device(lat, east),
        ))
        outs[-1].start()

    def first_windows(lo, hi, n):
        @pl.loop(lo, hi)
        def _(lb):
            y = input_grad(0, lb)
            mix = y[12:18]
            turned = pltpu.roll(mix, 4, 1)
            at = pl.ds(lb * WA, WA)
            for lev, m in enumerate((mix, turned)):
                main = y[lev * 6 : lev * 6 + 6]
                right = jnp.where(sub < 2, m, xv[lev, at].astype(F32)[:, 16:24])
                xv[lev, at] = jnp.concatenate([m, main, right], 1).astype(BF16)

        at = pl.ds(lo * WA, (hi - lo) * WA)
        outs.append(pltpu.make_async_copy(xv.at[:, at], gx_hbm.at[:, at], store_sem.at[n]))
        outs[-1].start()

    project_back(HALF)
    sum_a.step()
    sum_b.step()
    sum_e.step()
    second_windows(0, 4, 0)
    sum_c.step()
    sum_b.step()
    second_windows(4, 8, 1)
    sum_c.step()
    sum_b.step()
    sum_e.step()
    project_back(0)
    sum_c.step()
    sum_b.step()
    sum_a.step()
    first_windows(0, 4, 0)
    sum_c.step()
    sum_e.step()
    first_windows(4, 8, 1)
    sum_c.step()
    sum_b.step()
    sum_c.step()
    sum_c.step()
    finish(outs)


def place_kernel(
    gx_ref, arrive_ref, qa_ref, qb_ref, qc_ref, e_ref, edec_ref, wqkv_ref, gain_ref,
    out_ref, gqkv_ref, gout_ref, gdec_ref, ggain_ref, gains,
):
    sub = sub_iota((WA, 8, D))
    for lb in range(2):
        for lev in range(2):
            at = slice(lb * WA, (lb + 1) * WA)
            x = gx_ref[lev, at].astype(F32)
            new = arrive_ref[lb * 96 + lev * 48 : lb * 96 + lev * 48 + 48].astype(F32)
            edge = jnp.where(sub < 6, new.reshape(WA, 8, D), x[:, 0:8])
            out_ref[lev, at] = jnp.concatenate([edge, x[:, 8:24]], 1).astype(BF16)
    acc = jnp.zeros((128, 128), F32)
    for (first, count), q_ref in zip(GROUPS, (qa_ref, qb_ref, qc_ref)):
        width = count * HD
        for n in range(3):
            cols = slice(n * D + first * HD, n * D + first * HD + width)
            part = q_ref[:, n * width : (n + 1) * width].astype(F32)
            gqkv_ref[:, cols] = part
            prod = part * wqkv_ref[:, cols].astype(F32)
            for k in range(0, width, 128):
                acc += prod[:, k : k + 128]
    step = pl.program_id(0)
    gains[pl.ds(pl.multiple_of(step * 128, 128), 128), :] = acc

    @pl.when(step == 3)
    def _():
        ggain_ref[...] = jnp.sum(gains[...].T, axis=0, keepdims=True) / gain_ref[...]

    gout_ref[...] = e_ref[...].astype(F32)
    gdec_ref[...] = edec_ref[0:C].astype(F32)


VM = pl.BlockSpec(memory_space=pltpu.VMEM)
ANY = pl.BlockSpec(memory_space=pl.ANY)
SDS = jax.ShapeDtypeStruct
DMA = pltpu.SemaphoreType.DMA


SM = pl.BlockSpec(memory_space=pltpu.SMEM)


def sum_bufs(plan):
    rows, lanes, by_lanes, rp, lp, _ = plan
    rows, lanes = (rows, lanes // 2) if by_lanes else (rows // 2, lanes)
    band = rows // 4
    shapes = [(rows, lanes), (rows, lanes), (4, band, lanes), (band, lanes)]
    shapes += [(4, band // rp, lanes // lp)] * 2
    return [pltpu.VMEM(s, BF16) for s in shapes]


def fused_call(x, pts_t, slots, weights, counts, cells, gain, w_qkv, w_out, w_dec_t):
    def vm(*shape, dtype=BF16):
        return pltpu.VMEM(shape, dtype)

    return pl.pallas_call(
        fused_kernel,
        out_shape=(
            SDS(x.shape, BF16), SDS((768, D), BF16), SDS((D, 768), BF16), SDS((D, 384), BF16),
            SDS((D, 384), BF16), SDS((ER, D), BF16),
        ),
        in_specs=[ANY, VM, VM, VM, SM, VM, VM, ANY, ANY, VM],
        out_specs=(ANY, VM, VM, VM, VM, VM),
        scratch_shapes=[
            vm(2, 48, 24, D), vm(D, 3 * D), vm(D, D), DMA((3,)), DMA((3,)),
            vm(7, C, CAP), vm(BANDS, C, CAP), DMA((7,)), DMA((7,)),
            vm(768, D), vm(768, D), vm(768, D), DMA((8,)),
            vm(TOK, D), vm(TOK, D), vm(TOK, 3 * D),
            vm(TOK, 4 * WT), vm(TOK, 2 * WT), vm(TOK, 2 * WT), vm(TOK, D),
            vm(256, BANDS * CAP), vm(9 * C, BANDS * CAP), vm(C, TOK), vm(TOK, D, dtype=F32),
            vm(TOK, D), vm(TOK, D), vm(TOK, D), vm(HALF, D, dtype=F32),
            vm(D, 768), vm(D, 384), vm(D, 384), vm(ER, D),
            *sum_bufs(PLAN_4), *sum_bufs(PLAN_2), *sum_bufs(PLAN_2), *sum_bufs(PLAN_E),
            DMA((2, 17)), DMA((2, 17)), DMA((2, 17)), DMA((2, 17)),
        ],
        compiler_params=pltpu.CompilerParams(
            vmem_limit_bytes=62 << 20, collective_id=0, has_side_effects=True
        ),
        name="fused",
    )(x, pts_t, slots, weights, counts, cells, gain, w_qkv, w_out, w_dec_t)


def place_call(gx, arriving, qa, qb, qc, e, w_qkv, gain):
    def rows(lanes):
        return pl.BlockSpec((128, lanes), lambda i: (i, 0))

    grid_rows = pl.BlockSpec((2, 12, 24, D), lambda i: (0, i, 0, 0))
    across = pl.BlockSpec((1, D), lambda i: (0, 0))
    return pl.pallas_call(
        place_kernel,
        grid=(4,),
        out_shape=(
            SDS(gx.shape, BF16), SDS((D, 3 * D), F32), SDS((D, D), F32), SDS((C, D), F32),
            SDS((1, D), F32),
        ),
        in_specs=[
            grid_rows, pl.BlockSpec((192, D), lambda i: (i, 0)), rows(768), rows(384), rows(384),
            rows(D), pl.BlockSpec((128, D), lambda i: (4, 0)), rows(3 * D), across,
        ],
        out_specs=(grid_rows, rows(3 * D), rows(D), pl.BlockSpec((C, D), lambda i: (0, 0)), across),
        scratch_shapes=[pltpu.VMEM((D, 128), F32)],
        compiler_params=pltpu.CompilerParams(vmem_limit_bytes=60 << 20),
        name="place",
    )(gx, arriving, qa, qb, qc, e, e, w_qkv, gain)


def body(
    block_input, gain, w_qkv, w_out, w_dec, g_points, slot_point, slot_cell, slot_weight, pair_count
):
    parts = fused_call(
        block_input, g_points.T, slot_point, slot_weight, pair_count, slot_cell, gain[None],
        w_qkv, w_out, w_dec.T,
    )
    grad_x, g_qkv, g_out, g_dec, g_gain = place_call(*parts, w_qkv, gain[None])
    return (grad_x, g_qkv, g_out, g_dec.T, g_gain[0])


def solution(mesh):
    placed = (
        P(None, "lat", "lon", None),
        P(),
        P(),
        P(),
        P(),
        P(("lat", "lon"), None),
        P(("lat", "lon"), None),
        P(("lat", "lon"), None),
        P(("lat", "lon"), None),
        P(("lat", "lon")),
    )
    return jax.shard_map(
        body,
        mesh=mesh,
        in_specs=placed,
        out_specs=(P(None, "lat", "lon", None), P(), P(), P(), P()),
        check_vma=False,
    )
```

```python
import jax
import jax.numpy as jnp
from jax import lax
from jax.experimental import pallas as pl
from jax.experimental.pallas import tpu as pltpu
from jax.sharding import PartitionSpec as P

D = 512
HEADS = 8
HD = 64
WA = 6
WO = 12
WT = 144
C = 80
TOK = 2304
CAP = 512
BANDS = 8
PTS = 1024
SCALE = 0.125
F32 = jnp.float32
BF16 = jnp.bfloat16
NT = (((1,), (1,)), ((), ()))
TN = (((0,), (0,)), ((), ()))


def mm(a, b):
    return jnp.dot(a, b, preferred_element_type=F32)


def dg(a, b, dims):
    return lax.dot_general(a, b, dims, preferred_element_type=F32)


def onehot(idx_row, count):
    rows = lax.broadcasted_iota(jnp.int32, (count, idx_row.shape[1]), 0)
    return jnp.where(rows == idx_row, 1.0, 0.0).astype(BF16)


MESH = pl.DeviceIdType.MESH


def spot():
    return lax.axis_index("lat"), lax.axis_index("lon")


def device(lat, lon):
    return {"lat": lat, "lon": lon}


def greet(devices):
    barrier = pltpu.get_barrier_semaphore()
    for dev in devices:
        pl.semaphore_signal(barrier, inc=1, device_id=dev, device_id_type=MESH)
    pl.semaphore_wait(barrier, len(devices))


def remote(src, dst, send, recv, dev):
    return pltpu.make_async_remote_copy(
        src_ref=src, dst_ref=dst, send_sem=send, recv_sem=recv, device_id=dev, device_id_type=MESH
    )


def sub_iota(shape):
    return lax.broadcasted_iota(jnp.int32, shape, 1)


def norm_scale(x):
    return lax.rsqrt(jnp.mean(x * x, -1, keepdims=True) + 1e-06)


def steps_of(value, width, count):
    total = jnp.zeros_like(value)
    for n in range(1, count):
        total += jnp.where(value >= n * width, 1, 0)
    return total


def own_rows(cell):
    win = steps_of(cell, WT, 16)
    t = cell - win * WT
    r = steps_of(t, WO, 12)
    lo = t - r * WO
    low = r >= WA
    turn = jnp.where(low, 4, 0)
    mixed = 96 + (r - jnp.where(low, WA, 0)) * 8

    def wrap(v):
        return jnp.where(v >= 8, v - 8, v)

    a_row = jnp.where(
        (lo >= 2) & (lo < 10), r * 8 + lo - 2,
        mixed + wrap(jnp.where(lo < 2, lo + 6, lo - 10) + turn),
    )
    b_row = jnp.where(
        lo < 6, r * 8 + lo + 2,
        jnp.where(lo < 8, r * 8 + lo - 6, mixed + wrap(lo - 6 + turn)),
    )
    half = steps_of(win, 2, 8)
    second = win - half * 2
    return second * HALF + half * WT + jnp.where(second == 0, a_row, b_row)


NB = 8
HALF = NB * WT
GROUPS = ((0, 4), (4, 2), (6, 2))
ER = 640


def start(copies):
    for copy in copies:
        copy.start()
    return copies


def finish(copies):
    for copy in copies:
        copy.wait()


def total_of(buf, n):
    acc = buf[0].astype(F32)
    for i in range(1, n):
        acc = acc + buf[i].astype(F32)
    return acc.astype(BF16)


class Sum:
    def __init__(self, src, out, plan, bufs, sems):
        self.src, self.out = src, out
        self.buf_a, self.sum_b, self.buf_b, self.sum_c, self.buf_c, self.buf_d = bufs
        self.sems = sems
        lat, lon = spot()
        self.lat, self.lon = lat, lon
        self.core = lax.rem(lon, 2)
        self.z, self.y = lax.div(lon, 4), lax.rem(lat, 4)
        self.xlo, self.xhi = lax.rem(lax.div(lon, 2), 2), lax.div(lat, 4)
        self.x = self.xhi * 2 + self.xlo
        self.sib = lon + 1 - 2 * self.core
        self.rows, self.lanes, self.by_lanes, self.rp, self.lp, self.y_first = plan
        self.hr = self.rows if self.by_lanes else self.rows // 2
        self.hl = self.lanes // 2 if self.by_lanes else self.lanes
        self.band = self.hr // 4
        self.pr, self.pl = self.band // self.rp, self.hl // self.lp
        self.one, self.two = (self.y, self.z) if self.y_first else (self.z, self.y)
        self.step_no = 0

    def at_z(self, n):
        return device(self.lat, n * 4 + lax.rem(self.lon, 4))

    def at_y(self, n):
        return device(self.xhi * 4 + n, self.lon)

    def at_x(self, n):
        return device(
            lax.div(n, 2) * 4 + self.y, self.z * 4 + lax.rem(n, 2) * 2 + self.core
        )

    def dev_one(self, n):
        return self.at_y(n) if self.y_first else self.at_z(n)

    def dev_two(self, n):
        return self.at_z(n) if self.y_first else self.at_y(n)

    def half(self, core):
        if self.by_lanes:
            return pl.ds(0, self.hr), pl.ds(pl.multiple_of(core * self.hl, 128), self.hl)
        return pl.ds(pl.multiple_of(core * self.hr, 16), self.hr), pl.ds(0, self.hl)

    def band_of(self, n):
        return pl.ds(pl.multiple_of(n * self.band, 16), self.band)

    def piece(self, n, row=0, lane=0):
        row = row + lax.rem(n, self.rp) * self.pr
        lane = lane + lax.div(n, self.rp) * self.pl
        return (
            pl.ds(pl.multiple_of(row, 16), self.pr), pl.ds(pl.multiple_of(lane, 128), self.pl)
        )

    def corner(self):
        row, lane = self.one * self.band, 0
        if self.by_lanes:
            lane = self.core * self.hl
        else:
            row = row + self.core * self.hr
        return row, lane

    def copy(self, src, dst, n, dev):
        return remote(src, dst, self.sems.at[0, n], self.sems.at[1, n], dev)

    def step(self):
        getattr(self, "step%d" % self.step_no)()
        self.step_no += 1

    def step0(self):
        src = self.src.at[self.half(1 - self.core)]
        self.flying = start([self.copy(src, self.buf_a, 0, device(self.lat, self.sib))])

    def step1(self):
        finish(self.flying)
        self.sum_b[...] = (
            self.src[self.half(self.core)].astype(F32) + self.buf_a[...].astype(F32)
        ).astype(BF16)
        peers = [lax.rem(self.one + s, 4) for s in range(1, 4)]
        self.flying = start([
            self.copy(self.sum_b.at[self.band_of(o)], self.buf_b.at[self.one], 1 + s, self.dev_one(o))
            for s, o in enumerate(peers)
        ])
        self.buf_b[self.one] = self.sum_b[self.band_of(self.one)]

    def step2(self):
        finish(self.flying)
        self.sum_c[...] = total_of(self.buf_b, 4)
        peers = [lax.rem(self.two + s, 4) for s in range(1, 4)]
        self.flying = start([
            self.copy(self.sum_c.at[self.piece(o)], self.buf_c.at[self.two], 4 + s, self.dev_two(o))
            for s, o in enumerate(peers)
        ])
        self.buf_c[self.two] = self.sum_c[self.piece(self.two)]

    def step3(self):
        finish(self.flying)
        self.buf_d[self.x] = total_of(self.buf_c, 4)
        own = self.buf_d.at[self.x]
        self.flying = start([
            self.copy(own, own, 7 + s, self.at_x(lax.rem(self.x + 1 + s, 4))) for s in range(3)
        ])

    def step4(self):
        finish(self.flying)
        here = self.piece(self.two, *self.corner())
        self.out[here] = total_of(self.buf_d, 4)
        own = self.out.at[here]
        self.flying = start([
            self.copy(own, own, 10 + s, self.dev_two(lax.rem(self.two + 1 + s, 4)))
            for s in range(3)
        ])

    def step5(self):
        finish(self.flying)
        row, lane = self.corner()
        own = self.out.at[
            pl.ds(pl.multiple_of(row, 16), self.band), pl.ds(pl.multiple_of(lane, 128), self.hl)
        ]
        self.flying = start([
            self.copy(own, own, 13 + s, self.dev_one(lax.rem(self.one + 1 + s, 4)))
            for s in range(3)
        ])

    def step6(self):
        finish(self.flying)
        own = self.out.at[self.half(self.core)]
        self.flying = start([self.copy(own, own, 16, device(self.lat, self.sib))])

    def step7(self):
        finish(self.flying)


PLAN_E = (ER, D, True, 2, 2, True)
PLAN_4 = (D, 768, True, 4, 1, False)
PLAN_2 = (D, 384, False, 4, 1, False)
PLAN_2Y = (D, 384, False, 4, 1, True)


def fused_kernel(
    x_hbm, pts_ref, slot_ref, weight_ref, count_ref, cell_ref, gain_ref, wqkv_hbm, wout_hbm,
    wdec_ref,
    gx_hbm, arrive_ref, qa_ref, qb_ref, qc_ref, e_ref,
    xv, wqkv, wout, load_sem, store_sem,
    sent, arr, asend, arecv, first, halo, edge, hsems,
    xw, nw, qkv, probs_a, probs_b, probs_c, att, oh, marr, gtt, dhf, dhb, datt, hid, dnf,
    src_a, src_b, src_c, src_e,
    a0, a1, a2, a3, a4, a5, b0, b1, b2, b3, b4, b5, c0, c1, c2, c3, c4, c5, e0, e1, e2, e3, e4, e5,
    sems_a, sems_b, sems_c, sems_e,
):
    lat, lon = spot()
    core = lax.rem(lon, 2)
    flip = lon + 2 - 4 * lax.rem(lax.div(lon, 2), 2)
    west, east = lax.rem(lon + 15, 16), lax.rem(lon + 1, 16)
    others = [lax.rem(lat + s, BANDS) for s in range(1, BANDS)]
    loads = start([
        pltpu.make_async_copy(x_hbm, xv, load_sem.at[0]),
        pltpu.make_async_copy(wqkv_hbm, wqkv, load_sem.at[1]),
        pltpu.make_async_copy(wout_hbm, wout, load_sem.at[2]),
    ])
    barrier = pltpu.get_barrier_semaphore()
    peers = (
        [device(lat, lon + 1 - 2 * core)]
        + [device(lat, lax.rem(lon + 4 * s, 16)) for s in range(1, 4)]
        + [device(o, flip) for o in (lat, lax.rem(lat + 4, BANDS))]
        + [device(o, lon) for o in others]
        + [device(lat, west), device(lat, east)]
    )
    for dev in peers:
        pl.semaphore_signal(barrier, inc=1, device_id=dev, device_id_type=MESH)

    sum_a = Sum(src_a, qa_ref, PLAN_4, (a0, a1, a2, a3, a4, a5), sems_a)
    sum_b = Sum(src_b, qb_ref, PLAN_2, (b0, b1, b2, b3, b4, b5), sems_b)
    sum_c = Sum(src_c, qc_ref, PLAN_2Y, (c0, c1, c2, c3, c4, c5), sems_c)
    sum_e = Sum(src_e, e_ref, PLAN_E, (e0, e1, e2, e3, e4, e5), sems_e)
    probs = (probs_a, probs_b, probs_c)

    pts = jnp.concatenate([pts_ref[:, n * 256 : (n + 1) * 256] for n in range(4)], axis=0)
    lane = lax.broadcasted_iota(jnp.int32, (1, CAP), 1)

    def rows_for(d):
        point = slot_ref[pl.ds(d, 1), :]
        quarter = steps_of(point, 256, 4)
        picked = mm(pts, onehot(point - quarter * 256, 256))
        rows = picked[0:C]
        for n in range(1, 4):
            rows = jnp.where(quarter == n, picked[n * C : (n + 1) * C], rows)
        live = lane < count_ref[d]
        return jnp.where(live, weight_ref[pl.ds(d, 1), :] * rows, 0.0).astype(BF16)

    loads[0].wait()

    @pl.loop(0, NB)
    def _(lb):
        for lev in range(2):
            rows = pl.ds(pl.multiple_of(lb * 96 + lev * 48, 16), 48)
            part = xv[lev, pl.ds(lb * WA, WA)].astype(F32)[:, 0:8]
            first[rows, :] = part.reshape(48, D).astype(BF16)

    pl.semaphore_wait(barrier, len(peers))
    in_copy = remote(first, halo, hsems.at[0], hsems.at[1], device(lat, west))
    in_copy.start()
    copies = []
    for s, o in enumerate(others):
        sent[s] = rows_for(o)
        copies += start([remote(sent.at[s], arr.at[lat], asend.at[s], arecv.at[s], device(o, lon))])
    arr[lat] = rows_for(lat)

    gain = gain_ref[...]

    def put_window(rows, toks):
        xw[rows, :] = toks.astype(BF16)
        nw[rows, :] = (toks * norm_scale(toks) * gain).astype(BF16)

    def project(at):
        @pl.loop(0, 6)
        def _(c):
            cols = pl.ds(pl.multiple_of(c * 256, 256), 256)
            qkv[at : at + HALF, cols] = mm(nw[at : at + HALF, :], wqkv[:, cols]).astype(BF16)

    @pl.loop(0, NB)
    def _(lb):
        x0 = xv[0, pl.ds(lb * WA, WA)].astype(F32)
        x1 = xv[1, pl.ds(lb * WA, WA)].astype(F32)
        sub = sub_iota((WA, 8, D))
        c0 = jnp.where(sub >= 6, x0[:, 0:8], x0[:, 16:24])
        c1 = jnp.where(sub >= 6, x1[:, 0:8], x1[:, 16:24])
        mixed = jnp.where((sub < 2) | (sub >= 6), c0, pltpu.roll(c1, 4, 1))
        toks = jnp.concatenate([x0[:, 8:16], x1[:, 8:16], mixed], axis=0).reshape(WT, D)
        put_window(pl.ds(pl.multiple_of(lb * WT, WT), WT), toks)

    loads[1].wait()
    project(0)

    masks, picks = {}, {}
    for n in (4, 2):
        head = lax.broadcasted_iota(jnp.int32, (1, n * HD), 1) // HD
        masks[n] = [jnp.where(head == a, 1.0, 0.0).astype(BF16) for a in range(n)]
        picks[n] = [head == a for a in range(n)]

    def stack(a, n):
        return jnp.concatenate([a * m for m in masks[n]], axis=0)

    def pick(o, n):
        out = o[0:WT]
        for a in range(1, n):
            out = jnp.where(picks[n][a], o[a * WT : (a + 1) * WT], out)
        return out

    def col(part, g):
        at, n = GROUPS[g]
        return slice(part * D + at * HD, part * D + (at + n) * HD)

    def window(w):
        return pl.ds(pl.multiple_of(w * WT, WT), WT)

    def forward(w, some):
        todo = [(window(2 * w + i), g) for i in range(2) for g in some]
        scores = [
            dg(qkv[rows, col(1, g)], stack(qkv[rows, col(0, g)] * BF16(SCALE), GROUPS[g][1]), NT)
            for rows, g in todo
        ]
        pbs = []
        for st in scores:
            e = jnp.exp(st - jnp.max(st, axis=0, keepdims=True))
            pbs.append((e * (1.0 / jnp.sum(e, axis=0, keepdims=True))).astype(BF16))
        outs = [dg(pb, qkv[rows, col(2, g)], TN) for pb, (rows, g) in zip(pbs, todo)]
        for pb, o, (rows, g) in zip(pbs, outs, todo):
            probs[g][rows, :] = pb
            att[rows, col(0, g)] = pick(o, GROUPS[g][1]).astype(BF16)

    def forward_loop(lo, hi, some):
        @pl.loop(lo // 2, hi // 2)
        def _(w):
            forward(w, some)

    forward_loop(0, 8, (0,))
    forward_loop(0, 8, (1, 2))
    in_copy.wait()

    @pl.loop(0, NB)
    def _(lb):
        at = pl.multiple_of(lb * 96, 16)
        h0 = halo[pl.ds(at, 48), :].astype(F32).reshape(WA, 8, D)
        h1 = halo[pl.ds(pl.multiple_of(at + 48, 16), 48), :].astype(F32).reshape(WA, 8, D)
        x0 = xv[0, pl.ds(lb * WA, WA)].astype(F32)
        x1 = xv[1, pl.ds(lb * WA, WA)].astype(F32)
        sub = sub_iota((WA, 8, D))
        w0 = jnp.where(sub < 2, h0, x0[:, 16:24])
        w1 = jnp.where(sub < 2, h1, x1[:, 16:24])
        mixed = jnp.where((sub < 2) | (sub >= 6), pltpu.roll(h1, 4, 1), h0)
        toks = jnp.concatenate([w0, w1, mixed], axis=0).reshape(WT, D)
        put_window(pl.ds(pl.multiple_of(HALF + lb * WT, WT), WT), toks)

    project(HALF)

    forward_loop(8, 16, (0,))
    forward_loop(8, 16, (1, 2))

    row = own_rows(cell_ref[...])
    block = steps_of(row, 256, 9)
    place = row - block * 256
    for i in range(BANDS):
        oh[:, i * CAP : (i + 1) * CAP] = onehot(place[i : i + 1, :], 256)
    finish(copies)
    for i in range(BANDS):
        part = arr[i]
        for b in range(9):
            mask = jnp.where(block[i : i + 1, :] == b, 1.0, 0.0).astype(BF16)
            marr[b * C : (b + 1) * C, i * CAP : (i + 1) * CAP] = part * mask
    toks = dg(marr[...], oh[...], NT).astype(BF16)
    for b in range(9):
        gtt[:, b * 256 : (b + 1) * 256] = toks[b * C : (b + 1) * C]
    loads[2].wait()

    @pl.loop(0, 3)
    def _(b):
        rows = pl.ds(pl.multiple_of(b * 768, 768), 768)
        dh = dg(gtt[:, rows], wdec_ref[...], TN)
        dhf[rows, :] = dh
        dhb[rows, :] = dh.astype(BF16)
        datt[rows, :] = dg(dh.astype(BF16), wout[...], NT).astype(BF16)

    def hidden_grads():
        @pl.loop(0, 3)
        def _(b):
            rows = pl.ds(pl.multiple_of(b * 768, 768), 768)
            hid[rows, :] = (xw[rows, :].astype(F32) + mm(att[rows, :], wout[...])).astype(BF16)

        src_e[0:D, :] = dg(att[...], dhb[...], TN).astype(BF16)
        src_e[D : D + C, :] = mm(gtt[...], hid[...]).astype(BF16)
        src_e[D + C : ER, :] = jnp.zeros((ER - D - C, D), BF16)

    def backward(w, g):
        n = GROUPS[g][1]
        todo = [window(2 * w + i) for i in range(2)]
        ks = [qkv[rows, col(1, g)] for rows in todo]
        qs = [stack(qkv[rows, col(0, g)] * BF16(SCALE), n) for rows in todo]
        ds = [stack(datt[rows, col(0, g)], n) for rows in todo]
        pbs = [probs[g][rows, :] for rows in todo]
        dps = [dg(qkv[rows, col(2, g)], d, NT) for rows, d in zip(todo, ds)]
        dvs = [mm(pb, d) for pb, d in zip(pbs, ds)]
        dsts = []
        for pb, dp in zip(pbs, dps):
            p = pb.astype(F32)
            t = jnp.sum(p * dp, axis=0, keepdims=True)
            dsts.append((p * (dp - t)).astype(BF16))
        dks = [mm(dst, q) for dst, q in zip(dsts, qs)]
        dqs = [pick(dg(dst, k, TN), n) * SCALE for dst, k in zip(dsts, ks)]
        for rows, dq, dk, dv in zip(todo, dqs, dks, dvs):
            qkv[rows, col(0, g)] = dq.astype(BF16)
            qkv[rows, col(1, g)] = dk.astype(BF16)
            qkv[rows, col(2, g)] = dv.astype(BF16)

    def back_loop(lo, hi, g):
        @pl.loop(lo // 2, hi // 2)
        def _(w):
            backward(w, g)

    def weight_grad(src, g):
        width = GROUPS[g][1] * HD
        for n in range(3):
            part = dg(nw[...], qkv[:, col(n, g)], TN)
            src[:, n * width : (n + 1) * width] = part.astype(BF16)

    hidden_grads()
    sum_e.step()
    back_loop(0, 8, 0)
    sum_e.step()
    back_loop(8, 16, 0)
    sum_e.step()
    weight_grad(src_a, 0)
    sum_a.step()
    back_loop(0, 8, 1)
    sum_e.step()
    back_loop(8, 16, 1)
    sum_a.step()
    sum_e.step()
    weight_grad(src_b, 1)
    sum_b.step()
    back_loop(0, 16, 2)
    sum_a.step()
    sum_e.step()
    weight_grad(src_c, 2)
    sum_c.step()
    sum_b.step()

    sub = sub_iota((WA, 8, D))

    def project_back(at):
        for n in range(2):
            cols = slice(n * 256, (n + 1) * 256)
            dnf[:, cols] = dg(qkv[at : at + HALF, :], wqkv[cols, :], NT)

    def input_grad(at, lb):
        rows = pl.ds(pl.multiple_of(at + lb * WT, WT), WT)
        x = xw[rows, :].astype(F32)
        r = norm_scale(x)
        dng = dnf[window(lb), :] * gain
        mean = jnp.mean(dng * x, -1, keepdims=True)
        y = dhf[rows, :] + r * (dng - x * (r * r * mean))
        return y.reshape(18, 8, D)

    outs = []

    def second_windows(lo, hi, n):
        @pl.loop(lo, hi)
        def _(lb):
            y = input_grad(HALF, lb)
            mix = y[12:18]
            turned = pltpu.roll(mix, 4, 1)
            at = pl.ds(lb * WA, WA)
            for lev, m in enumerate((mix, turned)):
                main = y[lev * 6 : lev * 6 + 6]
                xv[lev, at] = jnp.concatenate([main, main, main], 1).astype(BF16)
                here = pl.ds(pl.multiple_of(lb * 96 + lev * 48, 16), 48)
                edge[here, :] = jnp.where(sub < 2, main, m).reshape(48, D).astype(BF16)

        rows = pl.ds(lo * 96, (hi - lo) * 96)
        outs.append(remote(
            edge.at[rows], arrive_ref.at[rows], hsems.at[2 + 2 * n], hsems.at[3 + 2 * n],
            device(lat, east),
        ))
        outs[-1].start()

    def first_windows(lo, hi, n):
        @pl.loop(lo, hi)
        def _(lb):
            y = input_grad(0, lb)
            mix = y[12:18]
            turned = pltpu.roll(mix, 4, 1)
            at = pl.ds(lb * WA, WA)
            for lev, m in enumerate((mix, turned)):
                main = y[lev * 6 : lev * 6 + 6]
                right = jnp.where(sub < 2, m, xv[lev, at].astype(F32)[:, 16:24])
                xv[lev, at] = jnp.concatenate([m, main, right], 1).astype(BF16)

        at = pl.ds(lo * WA, (hi - lo) * WA)
        outs.append(pltpu.make_async_copy(xv.at[:, at], gx_hbm.at[:, at], store_sem.at[n]))
        outs[-1].start()

    project_back(HALF)
    sum_a.step()
    sum_e.step()
    second_windows(0, 4, 0)
    sum_c.step()
    second_windows(4, 8, 1)
    sum_b.step()
    sum_a.step()
    project_back(0)
    sum_e.step()
    first_windows(0, 4, 0)
    sum_c.step()
    sum_b.step()
    first_windows(4, 8, 1)
    sum_a.step()
    sum_c.step()
    sum_b.step()
    sum_c.step()
    sum_b.step()
    sum_a.step()
    sum_c.step()
    sum_b.step()
    sum_c.step()
    sum_a.step()
    sum_b.step()
    sum_c.step()
    finish(outs)


def place_kernel(
    gx_ref, arrive_ref, qa_ref, qb_ref, qc_ref, e_ref, edec_ref, wqkv_ref, gain_ref,
    out_ref, gqkv_ref, gout_ref, gdec_ref, ggain_ref, gains,
):
    sub = sub_iota((WA, 8, D))
    for lb in range(2):
        for lev in range(2):
            at = slice(lb * WA, (lb + 1) * WA)
            x = gx_ref[lev, at].astype(F32)
            new = arrive_ref[lb * 96 + lev * 48 : lb * 96 + lev * 48 + 48].astype(F32)
            edge = jnp.where(sub < 6, new.reshape(WA, 8, D), x[:, 0:8])
            out_ref[lev, at] = jnp.concatenate([edge, x[:, 8:24]], 1).astype(BF16)
    acc = jnp.zeros((128, 128), F32)
    for (first, count), q_ref in zip(GROUPS, (qa_ref, qb_ref, qc_ref)):
        width = count * HD
        for n in range(3):
            cols = slice(n * D + first * HD, n * D + first * HD + width)
            part = q_ref[:, n * width : (n + 1) * width].astype(F32)
            gqkv_ref[:, cols] = part
            prod = part * wqkv_ref[:, cols].astype(F32)
            for k in range(0, width, 128):
                acc += prod[:, k : k + 128]
    step = pl.program_id(0)
    gains[pl.ds(pl.multiple_of(step * 128, 128), 128), :] = acc

    @pl.when(step == 3)
    def _():
        ggain_ref[...] = jnp.sum(gains[...].T, axis=0, keepdims=True) / gain_ref[...]

    gout_ref[...] = e_ref[...].astype(F32)
    gdec_ref[...] = edec_ref[0:C].astype(F32)


VM = pl.BlockSpec(memory_space=pltpu.VMEM)
ANY = pl.BlockSpec(memory_space=pl.ANY)
SDS = jax.ShapeDtypeStruct
DMA = pltpu.SemaphoreType.DMA


SM = pl.BlockSpec(memory_space=pltpu.SMEM)


def sum_bufs(plan):
    rows, lanes, by_lanes, rp, lp, _ = plan
    rows, lanes = (rows, lanes // 2) if by_lanes else (rows // 2, lanes)
    band = rows // 4
    shapes = [(rows, lanes), (rows, lanes), (4, band, lanes), (band, lanes)]
    shapes += [(4, band // rp, lanes // lp)] * 2
    return [pltpu.VMEM(s, BF16) for s in shapes]


def fused_call(x, pts_t, slots, weights, counts, cells, gain, w_qkv, w_out, w_dec_t):
    def vm(*shape, dtype=BF16):
        return pltpu.VMEM(shape, dtype)

    return pl.pallas_call(
        fused_kernel,
        out_shape=(
            SDS(x.shape, BF16), SDS((768, D), BF16), SDS((D, 768), BF16), SDS((D, 384), BF16),
            SDS((D, 384), BF16), SDS((ER, D), BF16),
        ),
        in_specs=[ANY, VM, VM, VM, SM, VM, VM, ANY, ANY, VM],
        out_specs=(ANY, VM, VM, VM, VM, VM),
        scratch_shapes=[
            vm(2, 48, 24, D), vm(D, 3 * D), vm(D, D), DMA((3,)), DMA((3,)),
            vm(7, C, CAP), vm(BANDS, C, CAP), DMA((7,)), DMA((7,)),
            vm(768, D), vm(768, D), vm(768, D), DMA((8,)),
            vm(TOK, D), vm(TOK, D), vm(TOK, 3 * D),
            vm(TOK, 4 * WT), vm(TOK, 2 * WT), vm(TOK, 2 * WT), vm(TOK, D),
            vm(256, BANDS * CAP), vm(9 * C, BANDS * CAP), vm(C, TOK), vm(TOK, D, dtype=F32),
            vm(TOK, D), vm(TOK, D), vm(TOK, D), vm(HALF, D, dtype=F32),
            vm(D, 768), vm(D, 384), vm(D, 384), vm(ER, D),
            *sum_bufs(PLAN_4), *sum_bufs(PLAN_2), *sum_bufs(PLAN_2), *sum_bufs(PLAN_E),
            DMA((2, 17)), DMA((2, 17)), DMA((2, 17)), DMA((2, 17)),
        ],
        compiler_params=pltpu.CompilerParams(
            vmem_limit_bytes=62 << 20, collective_id=0, has_side_effects=True
        ),
        name="fused",
    )(x, pts_t, slots, weights, counts, cells, gain, w_qkv, w_out, w_dec_t)


def place_call(gx, arriving, qa, qb, qc, e, w_qkv, gain):
    def rows(lanes):
        return pl.BlockSpec((128, lanes), lambda i: (i, 0))

    grid_rows = pl.BlockSpec((2, 12, 24, D), lambda i: (0, i, 0, 0))
    across = pl.BlockSpec((1, D), lambda i: (0, 0))
    return pl.pallas_call(
        place_kernel,
        grid=(4,),
        out_shape=(
            SDS(gx.shape, BF16), SDS((D, 3 * D), F32), SDS((D, D), F32), SDS((C, D), F32),
            SDS((1, D), F32),
        ),
        in_specs=[
            grid_rows, pl.BlockSpec((192, D), lambda i: (i, 0)), rows(768), rows(384), rows(384),
            rows(D), pl.BlockSpec((128, D), lambda i: (4, 0)), rows(3 * D), across,
        ],
        out_specs=(grid_rows, rows(3 * D), rows(D), pl.BlockSpec((C, D), lambda i: (0, 0)), across),
        scratch_shapes=[pltpu.VMEM((D, 128), F32)],
        compiler_params=pltpu.CompilerParams(vmem_limit_bytes=60 << 20),
        name="place",
    )(gx, arriving, qa, qb, qc, e, e, w_qkv, gain)


def body(
    block_input, gain, w_qkv, w_out, w_dec, g_points, slot_point, slot_cell, slot_weight, pair_count
):
    parts = fused_call(
        block_input, g_points.T, slot_point, slot_weight, pair_count, slot_cell, gain[None],
        w_qkv, w_out, w_dec.T,
    )
    grad_x, g_qkv, g_out, g_dec, g_gain = place_call(*parts, w_qkv, gain[None])
    return (grad_x, g_qkv, g_out, g_dec.T, g_gain[0])


def solution(mesh):
    placed = (
        P(None, "lat", "lon", None),
        P(),
        P(),
        P(),
        P(),
        P(("lat", "lon"), None),
        P(("lat", "lon"), None),
        P(("lat", "lon"), None),
        P(("lat", "lon"), None),
        P(("lat", "lon")),
    )
    return jax.shard_map(
        body,
        mesh=mesh,
        in_specs=placed,
        out_specs=(P(None, "lat", "lon", None), P(), P(), P(), P()),
        check_vma=False,
    )
```

```python
import jax
import jax.numpy as jnp
from jax import lax
from jax.experimental import pallas as pl
from jax.experimental.pallas import tpu as pltpu
from jax.sharding import PartitionSpec as P

D = 512
HEADS = 8
HD = 64
WA = 6
WO = 12
WT = 144
C = 80
TOK = 2304
CAP = 512
BANDS = 8
PTS = 1024
SCALE = 0.125
F32 = jnp.float32
BF16 = jnp.bfloat16
NT = (((1,), (1,)), ((), ()))
TN = (((0,), (0,)), ((), ()))


def mm(a, b):
    return jnp.dot(a, b, preferred_element_type=F32)


def dg(a, b, dims):
    return lax.dot_general(a, b, dims, preferred_element_type=F32)


def onehot(idx_row, count):
    rows = lax.broadcasted_iota(jnp.int32, (count, idx_row.shape[1]), 0)
    return jnp.where(rows == idx_row, 1.0, 0.0).astype(BF16)


MESH = pl.DeviceIdType.MESH


def spot():
    return lax.axis_index("lat"), lax.axis_index("lon")


def device(lat, lon):
    return {"lat": lat, "lon": lon}


def greet(devices):
    barrier = pltpu.get_barrier_semaphore()
    for dev in devices:
        pl.semaphore_signal(barrier, inc=1, device_id=dev, device_id_type=MESH)
    pl.semaphore_wait(barrier, len(devices))


def remote(src, dst, send, recv, dev):
    return pltpu.make_async_remote_copy(
        src_ref=src, dst_ref=dst, send_sem=send, recv_sem=recv, device_id=dev, device_id_type=MESH
    )


def sub_iota(shape):
    return lax.broadcasted_iota(jnp.int32, shape, 1)


def norm_scale(x):
    return lax.rsqrt(jnp.mean(x * x, -1, keepdims=True) + 1e-06)


def steps_of(value, width, count):
    total = jnp.zeros_like(value)
    for n in range(1, count):
        total += jnp.where(value >= n * width, 1, 0)
    return total


def own_rows(cell):
    win = steps_of(cell, WT, 16)
    t = cell - win * WT
    r = steps_of(t, WO, 12)
    lo = t - r * WO
    low = r >= WA
    turn = jnp.where(low, 4, 0)
    mixed = 96 + (r - jnp.where(low, WA, 0)) * 8

    def wrap(v):
        return jnp.where(v >= 8, v - 8, v)

    a_row = jnp.where(
        (lo >= 2) & (lo < 10), r * 8 + lo - 2,
        mixed + wrap(jnp.where(lo < 2, lo + 6, lo - 10) + turn),
    )
    b_row = jnp.where(
        lo < 6, r * 8 + lo + 2,
        jnp.where(lo < 8, r * 8 + lo - 6, mixed + wrap(lo - 6 + turn)),
    )
    half = steps_of(win, 2, 8)
    second = win - half * 2
    return second * HALF + half * WT + jnp.where(second == 0, a_row, b_row)


NB = 8
HALF = NB * WT
GROUPS = ((0, 4), (4, 4))
ER = 640


def start(copies):
    for copy in copies:
        copy.start()
    return copies


def finish(copies):
    for copy in copies:
        copy.wait()


def total_of(buf, n):
    acc = buf[0].astype(F32)
    for i in range(1, n):
        acc = acc + buf[i].astype(F32)
    return acc.astype(BF16)


class Sum:
    def __init__(self, src, out, plan, bufs, sems):
        self.src, self.out = src, out
        self.buf_a, self.sum_b, self.buf_b, self.sum_c, self.buf_c, self.buf_d = bufs
        self.sems = sems
        lat, lon = spot()
        self.lat, self.lon = lat, lon
        self.core = lax.rem(lon, 2)
        self.z, self.y = lax.div(lon, 4), lax.rem(lat, 4)
        self.xlo, self.xhi = lax.rem(lax.div(lon, 2), 2), lax.div(lat, 4)
        self.x = self.xhi * 2 + self.xlo
        self.sib = lon + 1 - 2 * self.core
        self.rows, self.lanes, self.by_lanes, self.rp, self.lp, self.y_first = plan
        self.hr = self.rows if self.by_lanes else self.rows // 2
        self.hl = self.lanes // 2 if self.by_lanes else self.lanes
        self.band = self.hr // 4
        self.pr, self.pl = self.band // self.rp, self.hl // self.lp
        self.one, self.two = (self.y, self.z) if self.y_first else (self.z, self.y)
        self.step_no = 0

    def at_z(self, n):
        return device(self.lat, n * 4 + lax.rem(self.lon, 4))

    def at_y(self, n):
        return device(self.xhi * 4 + n, self.lon)

    def at_x(self, n):
        return device(
            lax.div(n, 2) * 4 + self.y, self.z * 4 + lax.rem(n, 2) * 2 + self.core
        )

    def dev_one(self, n):
        return self.at_y(n) if self.y_first else self.at_z(n)

    def dev_two(self, n):
        return self.at_z(n) if self.y_first else self.at_y(n)

    def half(self, core):
        if self.by_lanes:
            return pl.ds(0, self.hr), pl.ds(pl.multiple_of(core * self.hl, 128), self.hl)
        return pl.ds(pl.multiple_of(core * self.hr, 16), self.hr), pl.ds(0, self.hl)

    def band_of(self, n):
        return pl.ds(pl.multiple_of(n * self.band, 16), self.band)

    def piece(self, n, row=0, lane=0):
        row = row + lax.rem(n, self.rp) * self.pr
        lane = lane + lax.div(n, self.rp) * self.pl
        return (
            pl.ds(pl.multiple_of(row, 16), self.pr), pl.ds(pl.multiple_of(lane, 128), self.pl)
        )

    def corner(self):
        row, lane = self.one * self.band, 0
        if self.by_lanes:
            lane = self.core * self.hl
        else:
            row = row + self.core * self.hr
        return row, lane

    def copy(self, src, dst, n, dev):
        return remote(src, dst, self.sems.at[0, n], self.sems.at[1, n], dev)

    def step(self):
        getattr(self, "step%d" % self.step_no)()
        self.step_no += 1

    def step0(self):
        src = self.src.at[self.half(1 - self.core)]
        self.flying = start([self.copy(src, self.buf_a, 0, device(self.lat, self.sib))])

    def step1(self):
        finish(self.flying)
        self.sum_b[...] = (
            self.src[self.half(self.core)].astype(F32) + self.buf_a[...].astype(F32)
        ).astype(BF16)
        peers = [lax.rem(self.one + s, 4) for s in range(1, 4)]
        self.flying = start([
            self.copy(self.sum_b.at[self.band_of(o)], self.buf_b.at[self.one], 1 + s, self.dev_one(o))
            for s, o in enumerate(peers)
        ])
        self.buf_b[self.one] = self.sum_b[self.band_of(self.one)]

    def step2(self):
        finish(self.flying)
        self.sum_c[...] = total_of(self.buf_b, 4)
        peers = [lax.rem(self.two + s, 4) for s in range(1, 4)]
        self.flying = start([
            self.copy(self.sum_c.at[self.piece(o)], self.buf_c.at[self.two], 4 + s, self.dev_two(o))
            for s, o in enumerate(peers)
        ])
        self.buf_c[self.two] = self.sum_c[self.piece(self.two)]

    def step3(self):
        finish(self.flying)
        self.buf_d[self.x] = total_of(self.buf_c, 4)
        own = self.buf_d.at[self.x]
        self.flying = start([
            self.copy(own, own, 7 + s, self.at_x(lax.rem(self.x + 1 + s, 4))) for s in range(3)
        ])

    def step4(self):
        finish(self.flying)
        here = self.piece(self.two, *self.corner())
        self.out[here] = total_of(self.buf_d, 4)
        own = self.out.at[here]
        self.flying = start([
            self.copy(own, own, 10 + s, self.dev_two(lax.rem(self.two + 1 + s, 4)))
            for s in range(3)
        ])

    def step5(self):
        finish(self.flying)
        row, lane = self.corner()
        own = self.out.at[
            pl.ds(pl.multiple_of(row, 16), self.band), pl.ds(pl.multiple_of(lane, 128), self.hl)
        ]
        self.flying = start([
            self.copy(own, own, 13 + s, self.dev_one(lax.rem(self.one + 1 + s, 4)))
            for s in range(3)
        ])

    def step6(self):
        finish(self.flying)
        own = self.out.at[self.half(self.core)]
        self.flying = start([self.copy(own, own, 16, device(self.lat, self.sib))])

    def step7(self):
        finish(self.flying)


PLAN_E = (ER, D, True, 2, 2, True)
PLAN_4 = (D, 768, True, 4, 1, False)
PLAN_4Y = (D, 768, True, 4, 1, True)


def fused_kernel(
    x_hbm, pts_ref, slot_ref, weight_ref, count_ref, cell_ref, gain_ref, wqkv_hbm, wout_hbm,
    wdec_ref,
    gx_hbm, arrive_ref, qa_ref, qb_ref, e_ref,
    xv, wqkv, wout, load_sem, store_sem,
    sent, arr, asend, arecv, first, halo, edge, hsems,
    xw, nw, qkv, probs_a, probs_b, att, oh, marr, gtt, dhf, dhb, datt, hid, dnf,
    src_a, src_b, src_e,
    a0, a1, a2, a3, a4, a5, b0, b1, b2, b3, b4, b5, e0, e1, e2, e3, e4, e5,
    sems_a, sems_b, sems_e,
):
    lat, lon = spot()
    core = lax.rem(lon, 2)
    flip = lon + 2 - 4 * lax.rem(lax.div(lon, 2), 2)
    west, east = lax.rem(lon + 15, 16), lax.rem(lon + 1, 16)
    others = [lax.rem(lat + s, BANDS) for s in range(1, BANDS)]
    loads = start([
        pltpu.make_async_copy(x_hbm, xv, load_sem.at[0]),
        pltpu.make_async_copy(wqkv_hbm, wqkv, load_sem.at[1]),
        pltpu.make_async_copy(wout_hbm, wout, load_sem.at[2]),
    ])
    barrier = pltpu.get_barrier_semaphore()
    peers = (
        [device(lat, lon + 1 - 2 * core)]
        + [device(lat, lax.rem(lon + 4 * s, 16)) for s in range(1, 4)]
        + [device(o, flip) for o in (lat, lax.rem(lat + 4, BANDS))]
        + [device(o, lon) for o in others]
        + [device(lat, west), device(lat, east)]
    )
    for dev in peers:
        pl.semaphore_signal(barrier, inc=1, device_id=dev, device_id_type=MESH)

    sum_a = Sum(src_a, qa_ref, PLAN_4, (a0, a1, a2, a3, a4, a5), sems_a)
    sum_b = Sum(src_b, qb_ref, PLAN_4Y, (b0, b1, b2, b3, b4, b5), sems_b)
    sum_e = Sum(src_e, e_ref, PLAN_E, (e0, e1, e2, e3, e4, e5), sems_e)
    probs = (probs_a, probs_b)

    pts = jnp.concatenate([pts_ref[:, n * 256 : (n + 1) * 256] for n in range(4)], axis=0)
    lane = lax.broadcasted_iota(jnp.int32, (1, CAP), 1)

    def rows_for(d):
        point = slot_ref[pl.ds(d, 1), :]
        quarter = steps_of(point, 256, 4)
        picked = mm(pts, onehot(point - quarter * 256, 256))
        rows = picked[0:C]
        for n in range(1, 4):
            rows = jnp.where(quarter == n, picked[n * C : (n + 1) * C], rows)
        live = lane < count_ref[d]
        return jnp.where(live, weight_ref[pl.ds(d, 1), :] * rows, 0.0).astype(BF16)

    loads[0].wait()

    @pl.loop(0, NB)
    def _(lb):
        for lev in range(2):
            rows = pl.ds(pl.multiple_of(lb * 96 + lev * 48, 16), 48)
            part = xv[lev, pl.ds(lb * WA, WA)].astype(F32)[:, 0:8]
            first[rows, :] = part.reshape(48, D).astype(BF16)

    pl.semaphore_wait(barrier, len(peers))
    in_copy = remote(first, halo, hsems.at[0], hsems.at[1], device(lat, west))
    in_copy.start()
    copies = []
    for s, o in enumerate(others):
        sent[s] = rows_for(o)
        copies += start([remote(sent.at[s], arr.at[lat], asend.at[s], arecv.at[s], device(o, lon))])
    arr[lat] = rows_for(lat)

    gain = gain_ref[...]

    def put_window(rows, toks):
        xw[rows, :] = toks.astype(BF16)
        nw[rows, :] = (toks * norm_scale(toks) * gain).astype(BF16)

    def project(at):
        @pl.loop(0, 6)
        def _(c):
            cols = pl.ds(pl.multiple_of(c * 256, 256), 256)
            qkv[at : at + HALF, cols] = mm(nw[at : at + HALF, :], wqkv[:, cols]).astype(BF16)

    @pl.loop(0, NB)
    def _(lb):
        x0 = xv[0, pl.ds(lb * WA, WA)].astype(F32)
        x1 = xv[1, pl.ds(lb * WA, WA)].astype(F32)
        sub = sub_iota((WA, 8, D))
        c0 = jnp.where(sub >= 6, x0[:, 0:8], x0[:, 16:24])
        c1 = jnp.where(sub >= 6, x1[:, 0:8], x1[:, 16:24])
        mixed = jnp.where((sub < 2) | (sub >= 6), c0, pltpu.roll(c1, 4, 1))
        toks = jnp.concatenate([x0[:, 8:16], x1[:, 8:16], mixed], axis=0).reshape(WT, D)
        put_window(pl.ds(pl.multiple_of(lb * WT, WT), WT), toks)

    loads[1].wait()
    project(0)

    masks, picks = {}, {}
    for n in (4,):
        head = lax.broadcasted_iota(jnp.int32, (1, n * HD), 1) // HD
        masks[n] = [jnp.where(head == a, 1.0, 0.0).astype(BF16) for a in range(n)]
        picks[n] = [head == a for a in range(n)]

    def stack(a, n):
        return jnp.concatenate([a * m for m in masks[n]], axis=0)

    def pick(o, n):
        out = o[0:WT]
        for a in range(1, n):
            out = jnp.where(picks[n][a], o[a * WT : (a + 1) * WT], out)
        return out

    def col(part, g):
        at, n = GROUPS[g]
        return slice(part * D + at * HD, part * D + (at + n) * HD)

    def window(w):
        return pl.ds(pl.multiple_of(w * WT, WT), WT)

    def forward(w, some):
        todo = [(window(2 * w + i), g) for i in range(2) for g in some]
        scores = [
            dg(qkv[rows, col(1, g)], stack(qkv[rows, col(0, g)] * BF16(SCALE), GROUPS[g][1]), NT)
            for rows, g in todo
        ]
        pbs = []
        for st in scores:
            e = jnp.exp(st - jnp.max(st, axis=0, keepdims=True))
            pbs.append((e * (1.0 / jnp.sum(e, axis=0, keepdims=True))).astype(BF16))
        outs = [dg(pb, qkv[rows, col(2, g)], TN) for pb, (rows, g) in zip(pbs, todo)]
        for pb, o, (rows, g) in zip(pbs, outs, todo):
            probs[g][rows, :] = pb
            att[rows, col(0, g)] = pick(o, GROUPS[g][1]).astype(BF16)

    def forward_loop(lo, hi, some):
        @pl.loop(lo // 2, hi // 2)
        def _(w):
            forward(w, some)

    forward_loop(0, 8, (0,))
    forward_loop(0, 8, (1,))
    in_copy.wait()

    @pl.loop(0, NB)
    def _(lb):
        at = pl.multiple_of(lb * 96, 16)
        h0 = halo[pl.ds(at, 48), :].astype(F32).reshape(WA, 8, D)
        h1 = halo[pl.ds(pl.multiple_of(at + 48, 16), 48), :].astype(F32).reshape(WA, 8, D)
        x0 = xv[0, pl.ds(lb * WA, WA)].astype(F32)
        x1 = xv[1, pl.ds(lb * WA, WA)].astype(F32)
        sub = sub_iota((WA, 8, D))
        w0 = jnp.where(sub < 2, h0, x0[:, 16:24])
        w1 = jnp.where(sub < 2, h1, x1[:, 16:24])
        mixed = jnp.where((sub < 2) | (sub >= 6), pltpu.roll(h1, 4, 1), h0)
        toks = jnp.concatenate([w0, w1, mixed], axis=0).reshape(WT, D)
        put_window(pl.ds(pl.multiple_of(HALF + lb * WT, WT), WT), toks)

    project(HALF)

    forward_loop(8, 16, (0,))
    forward_loop(8, 16, (1,))

    row = own_rows(cell_ref[...])
    block = steps_of(row, 256, 9)
    place = row - block * 256
    for i in range(BANDS):
        oh[:, i * CAP : (i + 1) * CAP] = onehot(place[i : i + 1, :], 256)
    finish(copies)
    for i in range(BANDS):
        part = arr[i]
        for b in range(9):
            mask = jnp.where(block[i : i + 1, :] == b, 1.0, 0.0).astype(BF16)
            marr[b * C : (b + 1) * C, i * CAP : (i + 1) * CAP] = part * mask
    toks = dg(marr[...], oh[...], NT).astype(BF16)
    for b in range(9):
        gtt[:, b * 256 : (b + 1) * 256] = toks[b * C : (b + 1) * C]
    loads[2].wait()

    @pl.loop(0, 3)
    def _(b):
        rows = pl.ds(pl.multiple_of(b * 768, 768), 768)
        dh = dg(gtt[:, rows], wdec_ref[...], TN)
        dhf[rows, :] = dh
        dhb[rows, :] = dh.astype(BF16)
        datt[rows, :] = dg(dh.astype(BF16), wout[...], NT).astype(BF16)

    def hidden_grads():
        @pl.loop(0, 3)
        def _(b):
            rows = pl.ds(pl.multiple_of(b * 768, 768), 768)
            hid[rows, :] = (xw[rows, :].astype(F32) + mm(att[rows, :], wout[...])).astype(BF16)

        src_e[0:D, :] = dg(att[...], dhb[...], TN).astype(BF16)
        src_e[D : D + C, :] = mm(gtt[...], hid[...]).astype(BF16)
        src_e[D + C : ER, :] = jnp.zeros((ER - D - C, D), BF16)

    def backward(w, g):
        n = GROUPS[g][1]
        todo = [window(2 * w + i) for i in range(2)]
        ks = [qkv[rows, col(1, g)] for rows in todo]
        qs = [stack(qkv[rows, col(0, g)] * BF16(SCALE), n) for rows in todo]
        ds = [stack(datt[rows, col(0, g)], n) for rows in todo]
        pbs = [probs[g][rows, :] for rows in todo]
        dps = [dg(qkv[rows, col(2, g)], d, NT) for rows, d in zip(todo, ds)]
        dvs = [mm(pb, d) for pb, d in zip(pbs, ds)]
        dsts = []
        for pb, dp in zip(pbs, dps):
            p = pb.astype(F32)
            t = jnp.sum(p * dp, axis=0, keepdims=True)
            dsts.append((p * (dp - t)).astype(BF16))
        dks = [mm(dst, q) for dst, q in zip(dsts, qs)]
        dqs = [pick(dg(dst, k, TN), n) * SCALE for dst, k in zip(dsts, ks)]
        for rows, dq, dk, dv in zip(todo, dqs, dks, dvs):
            qkv[rows, col(0, g)] = dq.astype(BF16)
            qkv[rows, col(1, g)] = dk.astype(BF16)
            qkv[rows, col(2, g)] = dv.astype(BF16)

    def back_loop(lo, hi, g):
        @pl.loop(lo // 2, hi // 2)
        def _(w):
            backward(w, g)

    def weight_grad(src, g):
        width = GROUPS[g][1] * HD
        for n in range(3):
            part = dg(nw[...], qkv[:, col(n, g)], TN)
            src[:, n * width : (n + 1) * width] = part.astype(BF16)

    hidden_grads()
    sum_e.step()
    back_loop(0, 8, 0)
    sum_e.step()
    back_loop(8, 16, 0)
    sum_e.step()
    weight_grad(src_a, 0)
    sum_a.step()
    back_loop(0, 8, 1)
    sum_e.step()
    sum_a.step()
    back_loop(8, 16, 1)
    sum_e.step()
    sum_a.step()
    weight_grad(src_b, 1)
    sum_b.step()

    sub = sub_iota((WA, 8, D))

    def project_back(at):
        for n in range(2):
            cols = slice(n * 256, (n + 1) * 256)
            dnf[:, cols] = dg(qkv[at : at + HALF, :], wqkv[cols, :], NT)

    def input_grad(at, lb):
        rows = pl.ds(pl.multiple_of(at + lb * WT, WT), WT)
        x = xw[rows, :].astype(F32)
        r = norm_scale(x)
        dng = dnf[window(lb), :] * gain
        mean = jnp.mean(dng * x, -1, keepdims=True)
        y = dhf[rows, :] + r * (dng - x * (r * r * mean))
        return y.reshape(18, 8, D)

    outs = []

    def second_windows(lo, hi, n):
        @pl.loop(lo, hi)
        def _(lb):
            y = input_grad(HALF, lb)
            mix = y[12:18]
            turned = pltpu.roll(mix, 4, 1)
            at = pl.ds(lb * WA, WA)
            for lev, m in enumerate((mix, turned)):
                main = y[lev * 6 : lev * 6 + 6]
                xv[lev, at] = jnp.concatenate([main, main, main], 1).astype(BF16)
                here = pl.ds(pl.multiple_of(lb * 96 + lev * 48, 16), 48)
                edge[here, :] = jnp.where(sub < 2, main, m).reshape(48, D).astype(BF16)

        rows = pl.ds(lo * 96, (hi - lo) * 96)
        outs.append(remote(
            edge.at[rows], arrive_ref.at[rows], hsems.at[2 + 2 * n], hsems.at[3 + 2 * n],
            device(lat, east),
        ))
        outs[-1].start()

    def first_windows(lo, hi, n):
        @pl.loop(lo, hi)
        def _(lb):
            y = input_grad(0, lb)
            mix = y[12:18]
            turned = pltpu.roll(mix, 4, 1)
            at = pl.ds(lb * WA, WA)
            for lev, m in enumerate((mix, turned)):
                main = y[lev * 6 : lev * 6 + 6]
                right = jnp.where(sub < 2, m, xv[lev, at].astype(F32)[:, 16:24])
                xv[lev, at] = jnp.concatenate([m, main, right], 1).astype(BF16)

        at = pl.ds(lo * WA, (hi - lo) * WA)
        outs.append(pltpu.make_async_copy(xv.at[:, at], gx_hbm.at[:, at], store_sem.at[n]))
        outs[-1].start()

    project_back(HALF)
    sum_b.step()
    sum_e.step()
    sum_a.step()
    second_windows(0, 4, 0)
    second_windows(4, 8, 1)
    sum_a.step()
    sum_e.step()
    project_back(0)
    sum_b.step()
    sum_a.step()
    first_windows(0, 4, 0)
    first_windows(4, 8, 1)
    sum_b.step()
    sum_e.step()
    sum_b.step()
    sum_a.step()
    sum_b.step()
    sum_b.step()
    sum_a.step()
    sum_b.step()
    finish(outs)


def place_kernel(
    gx_ref, arrive_ref, qa_ref, qb_ref, e_ref, edec_ref, wqkv_ref, gain_ref,
    out_ref, gqkv_ref, gout_ref, gdec_ref, ggain_ref, gains,
):
    sub = sub_iota((WA, 8, D))
    for lb in range(2):
        for lev in range(2):
            at = slice(lb * WA, (lb + 1) * WA)
            x = gx_ref[lev, at].astype(F32)
            new = arrive_ref[lb * 96 + lev * 48 : lb * 96 + lev * 48 + 48].astype(F32)
            edge = jnp.where(sub < 6, new.reshape(WA, 8, D), x[:, 0:8])
            out_ref[lev, at] = jnp.concatenate([edge, x[:, 8:24]], 1).astype(BF16)
    acc = jnp.zeros((128, 128), F32)
    for (first, count), q_ref in zip(GROUPS, (qa_ref, qb_ref)):
        width = count * HD
        for n in range(3):
            cols = slice(n * D + first * HD, n * D + first * HD + width)
            part = q_ref[:, n * width : (n + 1) * width].astype(F32)
            gqkv_ref[:, cols] = part
            prod = part * wqkv_ref[:, cols].astype(F32)
            for k in range(0, width, 128):
                acc += prod[:, k : k + 128]
    step = pl.program_id(0)
    gains[pl.ds(pl.multiple_of(step * 128, 128), 128), :] = acc

    @pl.when(step == 3)
    def _():
        ggain_ref[...] = jnp.sum(gains[...].T, axis=0, keepdims=True) / gain_ref[...]

    gout_ref[...] = e_ref[...].astype(F32)
    gdec_ref[...] = edec_ref[0:C].astype(F32)


VM = pl.BlockSpec(memory_space=pltpu.VMEM)
ANY = pl.BlockSpec(memory_space=pl.ANY)
SDS = jax.ShapeDtypeStruct
DMA = pltpu.SemaphoreType.DMA


SM = pl.BlockSpec(memory_space=pltpu.SMEM)


def sum_bufs(plan):
    rows, lanes, by_lanes, rp, lp, _ = plan
    rows, lanes = (rows, lanes // 2) if by_lanes else (rows // 2, lanes)
    band = rows // 4
    shapes = [(rows, lanes), (rows, lanes), (4, band, lanes), (band, lanes)]
    shapes += [(4, band // rp, lanes // lp)] * 2
    return [pltpu.VMEM(s, BF16) for s in shapes]


def fused_call(x, pts_t, slots, weights, counts, cells, gain, w_qkv, w_out, w_dec_t):
    def vm(*shape, dtype=BF16):
        return pltpu.VMEM(shape, dtype)

    return pl.pallas_call(
        fused_kernel,
        out_shape=(
            SDS(x.shape, BF16), SDS((768, D), BF16), SDS((D, 768), BF16), SDS((D, 768), BF16),
            SDS((ER, D), BF16),
        ),
        in_specs=[ANY, VM, VM, VM, SM, VM, VM, ANY, ANY, VM],
        out_specs=(ANY, VM, VM, VM, VM),
        scratch_shapes=[
            vm(2, 48, 24, D), vm(D, 3 * D), vm(D, D), DMA((3,)), DMA((3,)),
            vm(7, C, CAP), vm(BANDS, C, CAP), DMA((7,)), DMA((7,)),
            vm(768, D), vm(768, D), vm(768, D), DMA((8,)),
            vm(TOK, D), vm(TOK, D), vm(TOK, 3 * D),
            vm(TOK, 4 * WT), vm(TOK, 4 * WT), vm(TOK, D),
            vm(256, BANDS * CAP), vm(9 * C, BANDS * CAP), vm(C, TOK), vm(TOK, D, dtype=F32),
            vm(TOK, D), vm(TOK, D), vm(TOK, D), vm(HALF, D, dtype=F32),
            vm(D, 768), vm(D, 768), vm(ER, D),
            *sum_bufs(PLAN_4), *sum_bufs(PLAN_4Y), *sum_bufs(PLAN_E),
            DMA((2, 17)), DMA((2, 17)), DMA((2, 17)),
        ],
        compiler_params=pltpu.CompilerParams(
            vmem_limit_bytes=62 << 20, collective_id=0, has_side_effects=True
        ),
        name="fused",
    )(x, pts_t, slots, weights, counts, cells, gain, w_qkv, w_out, w_dec_t)


def place_call(gx, arriving, qa, qb, e, w_qkv, gain):
    def rows(lanes):
        return pl.BlockSpec((128, lanes), lambda i: (i, 0))

    grid_rows = pl.BlockSpec((2, 12, 24, D), lambda i: (0, i, 0, 0))
    across = pl.BlockSpec((1, D), lambda i: (0, 0))
    return pl.pallas_call(
        place_kernel,
        grid=(4,),
        out_shape=(
            SDS(gx.shape, BF16), SDS((D, 3 * D), F32), SDS((D, D), F32), SDS((C, D), F32),
            SDS((1, D), F32),
        ),
        in_specs=[
            grid_rows, pl.BlockSpec((192, D), lambda i: (i, 0)), rows(768), rows(768),
            rows(D), pl.BlockSpec((128, D), lambda i: (4, 0)), rows(3 * D), across,
        ],
        out_specs=(grid_rows, rows(3 * D), rows(D), pl.BlockSpec((C, D), lambda i: (0, 0)), across),
        scratch_shapes=[pltpu.VMEM((D, 128), F32)],
        compiler_params=pltpu.CompilerParams(vmem_limit_bytes=60 << 20),
        name="place",
    )(gx, arriving, qa, qb, e, e, w_qkv, gain)


def body(
    block_input, gain, w_qkv, w_out, w_dec, g_points, slot_point, slot_cell, slot_weight, pair_count
):
    parts = fused_call(
        block_input, g_points.T, slot_point, slot_weight, pair_count, slot_cell, gain[None],
        w_qkv, w_out, w_dec.T,
    )
    grad_x, g_qkv, g_out, g_dec, g_gain = place_call(*parts, w_qkv, gain[None])
    return (grad_x, g_qkv, g_out, g_dec.T, g_gain[0])


def solution(mesh):
    placed = (
        P(None, "lat", "lon", None),
        P(),
        P(),
        P(),
        P(),
        P(("lat", "lon"), None),
        P(("lat", "lon"), None),
        P(("lat", "lon"), None),
        P(("lat", "lon"), None),
        P(("lat", "lon")),
    )
    return jax.shard_map(
        body,
        mesh=mesh,
        in_specs=placed,
        out_specs=(P(None, "lat", "lon", None), P(), P(), P(), P()),
        check_vma=False,
    )
```

```python
import jax
import jax.numpy as jnp
from jax import lax
from jax.experimental import pallas as pl
from jax.experimental.pallas import tpu as pltpu
from jax.sharding import PartitionSpec as P

D = 512
HEADS = 8
HD = 64
WA = 6
WO = 12
WT = 144
C = 80
TOK = 2304
CAP = 512
BANDS = 8
PTS = 1024
SCALE = 0.125
F32 = jnp.float32
BF16 = jnp.bfloat16
NT = (((1,), (1,)), ((), ()))
TN = (((0,), (0,)), ((), ()))


def mm(a, b):
    return jnp.dot(a, b, preferred_element_type=F32)


def dg(a, b, dims):
    return lax.dot_general(a, b, dims, preferred_element_type=F32)


def onehot(idx_row, count):
    rows = lax.broadcasted_iota(jnp.int32, (count, idx_row.shape[1]), 0)
    return jnp.where(rows == idx_row, 1.0, 0.0).astype(BF16)


MESH = pl.DeviceIdType.MESH


def spot():
    return lax.axis_index("lat"), lax.axis_index("lon")


def device(lat, lon):
    return {"lat": lat, "lon": lon}


def greet(devices):
    barrier = pltpu.get_barrier_semaphore()
    for dev in devices:
        pl.semaphore_signal(barrier, inc=1, device_id=dev, device_id_type=MESH)
    pl.semaphore_wait(barrier, len(devices))


def remote(src, dst, send, recv, dev):
    return pltpu.make_async_remote_copy(
        src_ref=src, dst_ref=dst, send_sem=send, recv_sem=recv, device_id=dev, device_id_type=MESH
    )


def sub_iota(shape):
    return lax.broadcasted_iota(jnp.int32, shape, 1)


def norm_scale(x):
    return lax.rsqrt(jnp.mean(x * x, -1, keepdims=True) + 1e-06)


def steps_of(value, width, count):
    total = jnp.zeros_like(value)
    for n in range(1, count):
        total += jnp.where(value >= n * width, 1, 0)
    return total


def own_rows(cell):
    win = steps_of(cell, WT, 16)
    t = cell - win * WT
    r = steps_of(t, WO, 12)
    lo = t - r * WO
    low = r >= WA
    turn = jnp.where(low, 4, 0)
    mixed = 96 + (r - jnp.where(low, WA, 0)) * 8

    def wrap(v):
        return jnp.where(v >= 8, v - 8, v)

    a_row = jnp.where(
        (lo >= 2) & (lo < 10), r * 8 + lo - 2,
        mixed + wrap(jnp.where(lo < 2, lo + 6, lo - 10) + turn),
    )
    b_row = jnp.where(
        lo < 6, r * 8 + lo + 2,
        jnp.where(lo < 8, r * 8 + lo - 6, mixed + wrap(lo - 6 + turn)),
    )
    half = steps_of(win, 2, 8)
    second = win - half * 2
    return second * HALF + half * WT + jnp.where(second == 0, a_row, b_row)


NB = 8
HALF = NB * WT
GROUPS = ((0, 4), (4, 2), (6, 2))
ER = 640


def start(copies):
    for copy in copies:
        copy.start()
    return copies


def finish(copies):
    for copy in copies:
        copy.wait()


def total_of(buf, n):
    acc = buf[0].astype(F32)
    for i in range(1, n):
        acc = acc + buf[i].astype(F32)
    return acc.astype(BF16)


class Sum:
    def __init__(self, src, out, plan, bufs, sems):
        self.src, self.out = src, out
        self.buf_a, self.sum_b, self.buf_b, self.sum_c, self.buf_c = bufs
        self.sems = sems
        lat, lon = spot()
        self.lat, self.lon = lat, lon
        self.core, grp = lax.rem(lon, 2), lax.div(lon, 2)
        self.sib = lon + 1 - 2 * self.core
        self.rows, self.lanes, self.by_lanes, self.rp, self.lp, self.lat_first = plan
        self.hr = self.rows if self.by_lanes else self.rows // 2
        self.hl = self.lanes // 2 if self.by_lanes else self.lanes
        self.band = self.hr // 8
        self.pr, self.pl = self.band // self.rp, self.hl // self.lp
        self.one, self.two = (lat, grp) if self.lat_first else (grp, lat)
        self.step_no = 0

    def dev_one(self, n):
        if self.lat_first:
            return device(n, self.lon)
        return device(self.lat, n * 2 + self.core)

    def dev_two(self, n):
        if self.lat_first:
            return device(self.lat, n * 2 + self.core)
        return device(n, self.lon)

    def half(self, core):
        if self.by_lanes:
            return pl.ds(0, self.hr), pl.ds(pl.multiple_of(core * self.hl, 128), self.hl)
        return pl.ds(pl.multiple_of(core * self.hr, 16), self.hr), pl.ds(0, self.hl)

    def band_of(self, n):
        return pl.ds(pl.multiple_of(n * self.band, 16), self.band)

    def piece(self, n, row=0, lane=0):
        part = lax.rem(n, self.rp * self.lp)
        row = row + lax.rem(part, self.rp) * self.pr
        lane = lane + lax.div(part, self.rp) * self.pl
        return (
            pl.ds(pl.multiple_of(row, 16), self.pr), pl.ds(pl.multiple_of(lane, 128), self.pl)
        )

    def corner(self):
        row, lane = self.one * self.band, 0
        if self.by_lanes:
            lane = self.core * self.hl
        else:
            row = row + self.core * self.hr
        return row, lane

    def copy(self, src, dst, n, dev):
        return remote(src, dst, self.sems.at[0, n], self.sems.at[1, n], dev)

    def step(self):
        getattr(self, "step%d" % self.step_no)()
        self.step_no += 1

    def step0(self):
        src = self.src.at[self.half(1 - self.core)]
        self.flying = start([self.copy(src, self.buf_a, 0, device(self.lat, self.sib))])

    def step1(self):
        finish(self.flying)
        self.sum_b[...] = (
            self.src[self.half(self.core)].astype(F32) + self.buf_a[...].astype(F32)
        ).astype(BF16)
        self.flying = start([
            self.copy(
                self.sum_b.at[self.band_of(lax.rem(self.one + s, 8))], self.buf_b.at[self.one], s,
                self.dev_one(lax.rem(self.one + s, 8)),
            )
            for s in range(1, 8)
        ])
        self.buf_b[self.one] = self.sum_b[self.band_of(self.one)]

    def step2(self):
        finish(self.flying)
        self.sum_c[...] = total_of(self.buf_b, 8)
        self.flying = start([
            self.copy(
                self.sum_c.at[self.piece(lax.rem(self.two + s, 8))], self.buf_c.at[self.two],
                7 + s, self.dev_two(lax.rem(self.two + s, 8)),
            )
            for s in range(1, 8)
        ])
        self.buf_c[self.two] = self.sum_c[self.piece(self.two)]

    def step3(self):
        finish(self.flying)
        here = self.piece(self.two, *self.corner())
        self.out[here] = total_of(self.buf_c, 8)
        own = self.out.at[here]
        count = self.rp * self.lp
        first = self.two - lax.rem(self.two, count)
        self.flying = start([
            self.copy(own, own, 14 + s, self.dev_two(first + lax.rem(self.two + s, count)))
            for s in range(1, count)
        ])

    def step4(self):
        finish(self.flying)
        row, lane = self.corner()
        own = self.out.at[
            pl.ds(pl.multiple_of(row, 16), self.band), pl.ds(pl.multiple_of(lane, 128), self.hl)
        ]
        self.flying = start([
            self.copy(own, own, 17 + s, self.dev_one(lax.rem(self.one + s, 8)))
            for s in range(1, 8)
        ])

    def step5(self):
        finish(self.flying)
        own = self.out.at[self.half(self.core)]
        self.flying = start([self.copy(own, own, 25, device(self.lat, self.sib))])

    def step6(self):
        finish(self.flying)


PLAN_E = (ER, D, True, 1, 2, True)
PLAN_4 = (D, 768, True, 4, 1, False)
PLAN_2 = (D, 384, False, 2, 1, False)


def fused_kernel(
    x_hbm, pts_ref, slot_ref, weight_ref, count_ref, cell_ref, gain_ref, wqkv_hbm, wout_hbm,
    wdec_ref,
    gx_hbm, arrive_ref, qa_ref, qb_ref, qc_ref, e_ref,
    xv, wqkv, wout, load_sem, store_sem,
    sent, arr, asend, arecv, first, halo, edge, hsems,
    xw, nw, qkv, probs_a, probs_b, probs_c, att, oh, marr, gtt, dhf, dhb, datt, hid, dnf,
    src_a, src_b, src_c, src_e,
    a0, a1, a2, a3, a4, b0, b1, b2, b3, b4, c0, c1, c2, c3, c4, e0, e1, e2, e3, e4,
    sems_a, sems_b, sems_c, sems_e,
):
    lat, lon = spot()
    core, grp = lax.rem(lon, 2), lax.div(lon, 2)
    west, east = lax.rem(lon + 15, 16), lax.rem(lon + 1, 16)
    others = [lax.rem(lat + s, BANDS) for s in range(1, BANDS)]
    loads = start([
        pltpu.make_async_copy(x_hbm, xv, load_sem.at[0]),
        pltpu.make_async_copy(wqkv_hbm, wqkv, load_sem.at[1]),
        pltpu.make_async_copy(wout_hbm, wout, load_sem.at[2]),
    ])
    barrier = pltpu.get_barrier_semaphore()
    peers = (
        [device(lat, lon + 1 - 2 * core)]
        + [device(lat, lax.rem(grp + s, 8) * 2 + core) for s in range(1, 8)]
        + [device(o, lon) for o in others]
        + [device(lat, west), device(lat, east)]
    )
    for dev in peers:
        pl.semaphore_signal(barrier, inc=1, device_id=dev, device_id_type=MESH)

    sum_a = Sum(src_a, qa_ref, PLAN_4, (a0, a1, a2, a3, a4), sems_a)
    sum_b = Sum(src_b, qb_ref, PLAN_2, (b0, b1, b2, b3, b4), sems_b)
    sum_c = Sum(src_c, qc_ref, PLAN_2, (c0, c1, c2, c3, c4), sems_c)
    sum_e = Sum(src_e, e_ref, PLAN_E, (e0, e1, e2, e3, e4), sems_e)
    probs = (probs_a, probs_b, probs_c)

    pts = jnp.concatenate([pts_ref[:, n * 256 : (n + 1) * 256] for n in range(4)], axis=0)
    lane = lax.broadcasted_iota(jnp.int32, (1, CAP), 1)

    def rows_for(d):
        point = slot_ref[pl.ds(d, 1), :]
        quarter = steps_of(point, 256, 4)
        picked = mm(pts, onehot(point - quarter * 256, 256))
        rows = picked[0:C]
        for n in range(1, 4):
            rows = jnp.where(quarter == n, picked[n * C : (n + 1) * C], rows)
        live = lane < count_ref[d]
        return jnp.where(live, weight_ref[pl.ds(d, 1), :] * rows, 0.0).astype(BF16)

    loads[0].wait()

    @pl.loop(0, NB)
    def _(lb):
        for lev in range(2):
            rows = pl.ds(pl.multiple_of(lb * 96 + lev * 48, 16), 48)
            part = xv[lev, pl.ds(lb * WA, WA)].astype(F32)[:, 0:8]
            first[rows, :] = part.reshape(48, D).astype(BF16)

    pl.semaphore_wait(barrier, len(peers))
    in_copy = remote(first, halo, hsems.at[0], hsems.at[1], device(lat, west))
    in_copy.start()
    copies = []
    for s, o in enumerate(others):
        sent[s] = rows_for(o)
        copies += start([remote(sent.at[s], arr.at[lat], asend.at[s], arecv.at[s], device(o, lon))])
    arr[lat] = rows_for(lat)

    gain = gain_ref[...]

    def put_window(rows, toks):
        xw[rows, :] = toks.astype(BF16)
        nw[rows, :] = (toks * norm_scale(toks) * gain).astype(BF16)

    def project(at):
        @pl.loop(0, 6)
        def _(c):
            cols = pl.ds(pl.multiple_of(c * 256, 256), 256)
            qkv[at : at + HALF, cols] = mm(nw[at : at + HALF, :], wqkv[:, cols]).astype(BF16)

    @pl.loop(0, NB)
    def _(lb):
        x0 = xv[0, pl.ds(lb * WA, WA)].astype(F32)
        x1 = xv[1, pl.ds(lb * WA, WA)].astype(F32)
        sub = sub_iota((WA, 8, D))
        c0 = jnp.where(sub >= 6, x0[:, 0:8], x0[:, 16:24])
        c1 = jnp.where(sub >= 6, x1[:, 0:8], x1[:, 16:24])
        mixed = jnp.where((sub < 2) | (sub >= 6), c0, pltpu.roll(c1, 4, 1))
        toks = jnp.concatenate([x0[:, 8:16], x1[:, 8:16], mixed], axis=0).reshape(WT, D)
        put_window(pl.ds(pl.multiple_of(lb * WT, WT), WT), toks)

    loads[1].wait()
    project(0)

    masks, picks = {}, {}
    for n in (4, 2):
        head = lax.broadcasted_iota(jnp.int32, (1, n * HD), 1) // HD
        masks[n] = [jnp.where(head == a, 1.0, 0.0).astype(BF16) for a in range(n)]
        picks[n] = [head == a for a in range(n)]

    def stack(a, n):
        return jnp.concatenate([a * m for m in masks[n]], axis=0)

    def pick(o, n):
        out = o[0:WT]
        for a in range(1, n):
            out = jnp.where(picks[n][a], o[a * WT : (a + 1) * WT], out)
        return out

    def col(part, g):
        at, n = GROUPS[g]
        return slice(part * D + at * HD, part * D + (at + n) * HD)

    def window(w):
        return pl.ds(pl.multiple_of(w * WT, WT), WT)

    def forward(w):
        for some in ((0,), (1, 2)):
            todo = [(window(2 * w + i), g) for i in range(2) for g in some]
            scores = [
                dg(qkv[rows, col(1, g)], stack(qkv[rows, col(0, g)] * BF16(SCALE), GROUPS[g][1]), NT)
                for rows, g in todo
            ]
            pbs = []
            for st in scores:
                e = jnp.exp(st - jnp.max(st, axis=0, keepdims=True))
                pbs.append((e * (1.0 / jnp.sum(e, axis=0, keepdims=True))).astype(BF16))
            outs = [dg(pb, qkv[rows, col(2, g)], TN) for pb, (rows, g) in zip(pbs, todo)]
            for pb, o, (rows, g) in zip(pbs, outs, todo):
                probs[g][rows, :] = pb
                att[rows, col(0, g)] = pick(o, GROUPS[g][1]).astype(BF16)

    @pl.loop(0, NB // 2)
    def _(w):
        forward(w)

    row = own_rows(cell_ref[...])
    block = steps_of(row, 256, 9)
    place = row - block * 256
    for i in range(BANDS):
        oh[:, i * CAP : (i + 1) * CAP] = onehot(place[i : i + 1, :], 256)
    in_copy.wait()

    @pl.loop(0, NB)
    def _(lb):
        at = pl.multiple_of(lb * 96, 16)
        h0 = halo[pl.ds(at, 48), :].astype(F32).reshape(WA, 8, D)
        h1 = halo[pl.ds(pl.multiple_of(at + 48, 16), 48), :].astype(F32).reshape(WA, 8, D)
        x0 = xv[0, pl.ds(lb * WA, WA)].astype(F32)
        x1 = xv[1, pl.ds(lb * WA, WA)].astype(F32)
        sub = sub_iota((WA, 8, D))
        w0 = jnp.where(sub < 2, h0, x0[:, 16:24])
        w1 = jnp.where(sub < 2, h1, x1[:, 16:24])
        mixed = jnp.where((sub < 2) | (sub >= 6), pltpu.roll(h1, 4, 1), h0)
        toks = jnp.concatenate([w0, w1, mixed], axis=0).reshape(WT, D)
        put_window(pl.ds(pl.multiple_of(HALF + lb * WT, WT), WT), toks)

    project(HALF)

    @pl.loop(NB // 2, NB)
    def _(w):
        forward(w)

    finish(copies)
    for i in range(BANDS):
        part = arr[i]
        for b in range(9):
            mask = jnp.where(block[i : i + 1, :] == b, 1.0, 0.0).astype(BF16)
            marr[b * C : (b + 1) * C, i * CAP : (i + 1) * CAP] = part * mask
    toks = dg(marr[...], oh[...], NT).astype(BF16)
    for b in range(9):
        gtt[:, b * 256 : (b + 1) * 256] = toks[b * C : (b + 1) * C]
    loads[2].wait()

    @pl.loop(0, 3)
    def _(b):
        rows = pl.ds(pl.multiple_of(b * 768, 768), 768)
        dh = dg(gtt[:, rows], wdec_ref[...], TN)
        dhf[rows, :] = dh
        dhb[rows, :] = dh.astype(BF16)
        datt[rows, :] = dg(dh.astype(BF16), wout[...], NT).astype(BF16)
        hid[rows, :] = (xw[rows, :].astype(F32) + mm(att[rows, :], wout[...])).astype(BF16)

    src_e[0:D, :] = dg(att[...], dhb[...], TN).astype(BF16)
    src_e[D : D + C, :] = mm(gtt[...], hid[...]).astype(BF16)
    src_e[D + C : ER, :] = jnp.zeros((ER - D - C, D), BF16)
    sum_e.step()

    def backward(w, g):
        n = GROUPS[g][1]
        todo = [window(2 * w + i) for i in range(2)]
        ks = [qkv[rows, col(1, g)] for rows in todo]
        qs = [stack(qkv[rows, col(0, g)] * BF16(SCALE), n) for rows in todo]
        ds = [stack(datt[rows, col(0, g)], n) for rows in todo]
        pbs = [probs[g][rows, :] for rows in todo]
        dps = [dg(qkv[rows, col(2, g)], d, NT) for rows, d in zip(todo, ds)]
        dvs = [mm(pb, d) for pb, d in zip(pbs, ds)]
        dsts = []
        for pb, dp in zip(pbs, dps):
            p = pb.astype(F32)
            t = jnp.sum(p * dp, axis=0, keepdims=True)
            dsts.append((p * (dp - t)).astype(BF16))
        dks = [mm(dst, q) for dst, q in zip(dsts, qs)]
        dqs = [pick(dg(dst, k, TN), n) * SCALE for dst, k in zip(dsts, ks)]
        for rows, dq, dk, dv in zip(todo, dqs, dks, dvs):
            qkv[rows, col(0, g)] = dq.astype(BF16)
            qkv[rows, col(1, g)] = dk.astype(BF16)
            qkv[rows, col(2, g)] = dv.astype(BF16)

    def back_loop(lo, hi, g):
        @pl.loop(lo // 2, hi // 2)
        def _(w):
            backward(w, g)

    def weight_grad(src, g):
        width = GROUPS[g][1] * HD
        for n in range(3):
            part = dg(nw[...], qkv[:, col(n, g)], TN)
            src[:, n * width : (n + 1) * width] = part.astype(BF16)

    back_loop(0, 4, 0)
    sum_e.step()
    back_loop(4, 16, 0)
    sum_e.step()
    weight_grad(src_a, 0)
    sum_a.step()
    back_loop(0, 8, 1)
    sum_e.step()
    sum_a.step()
    back_loop(8, 16, 1)
    sum_e.step()
    weight_grad(src_b, 1)
    sum_b.step()
    back_loop(0, 8, 2)
    sum_a.step()
    sum_b.step()
    back_loop(8, 16, 2)
    sum_a.step()
    weight_grad(src_c, 2)
    sum_c.step()
    sum_e.step()
    sum_a.step()
    sum_b.step()

    sub = sub_iota((WA, 8, D))

    def project_back(at):
        for n in range(2):
            cols = slice(n * 256, (n + 1) * 256)
            dnf[:, cols] = dg(qkv[at : at + HALF, :], wqkv[cols, :], NT)

    def input_grad(at, lb):
        rows = pl.ds(pl.multiple_of(at + lb * WT, WT), WT)
        x = xw[rows, :].astype(F32)
        r = norm_scale(x)
        dng = dnf[window(lb), :] * gain
        mean = jnp.mean(dng * x, -1, keepdims=True)
        y = dhf[rows, :] + r * (dng - x * (r * r * mean))
        return y.reshape(18, 8, D)

    outs = []

    def second_windows(lo, hi, n):
        @pl.loop(lo, hi)
        def _(lb):
            y = input_grad(HALF, lb)
            mix = y[12:18]
            turned = pltpu.roll(mix, 4, 1)
            at = pl.ds(lb * WA, WA)
            for lev, m in enumerate((mix, turned)):
                main = y[lev * 6 : lev * 6 + 6]
                xv[lev, at] = jnp.concatenate([main, main, main], 1).astype(BF16)
                here = pl.ds(pl.multiple_of(lb * 96 + lev * 48, 16), 48)
                edge[here, :] = jnp.where(sub < 2, main, m).reshape(48, D).astype(BF16)

        rows = pl.ds(lo * 96, (hi - lo) * 96)
        outs.append(remote(
            edge.at[rows], arrive_ref.at[rows], hsems.at[2 + 2 * n], hsems.at[3 + 2 * n],
            device(lat, east),
        ))
        outs[-1].start()

    def first_windows(lo, hi, n):
        @pl.loop(lo, hi)
        def _(lb):
            y = input_grad(0, lb)
            mix = y[12:18]
            turned = pltpu.roll(mix, 4, 1)
            at = pl.ds(lb * WA, WA)
            for lev, m in enumerate((mix, turned)):
                main = y[lev * 6 : lev * 6 + 6]
                right = jnp.where(sub < 2, m, xv[lev, at].astype(F32)[:, 16:24])
                xv[lev, at] = jnp.concatenate([m, main, right], 1).astype(BF16)

        at = pl.ds(lo * WA, (hi - lo) * WA)
        outs.append(pltpu.make_async_copy(xv.at[:, at], gx_hbm.at[:, at], store_sem.at[n]))
        outs[-1].start()

    project_back(HALF)
    sum_c.step()
    second_windows(0, 4, 0)
    sum_b.step()
    sum_e.step()
    second_windows(4, 8, 1)
    sum_c.step()
    sum_b.step()
    project_back(0)
    sum_a.step()
    sum_c.step()
    first_windows(0, 4, 0)
    sum_c.step()
    sum_b.step()
    first_windows(4, 8, 1)
    sum_a.step()
    sum_c.step()
    sum_b.step()
    sum_c.step()
    finish(outs)


def place_kernel(
    gx_ref, arrive_ref, qa_ref, qb_ref, qc_ref, e_ref, edec_ref, wqkv_ref, gain_ref,
    out_ref, gqkv_ref, gout_ref, gdec_ref, ggain_ref,
):
    sub = sub_iota((WA, 8, D))
    for lb in range(2):
        for lev in range(2):
            at = slice(lb * WA, (lb + 1) * WA)
            x = gx_ref[lev, at].astype(F32)
            new = arrive_ref[lb * 96 + lev * 48 : lb * 96 + lev * 48 + 48].astype(F32)
            edge = jnp.where(sub < 6, new.reshape(WA, 8, D), x[:, 0:8])
            out_ref[lev, at] = jnp.concatenate([edge, x[:, 8:24]], 1).astype(BF16)
    acc = jnp.zeros((128, 128), F32)
    for (first, count), q_ref in zip(GROUPS, (qa_ref, qb_ref, qc_ref)):
        width = count * HD
        for n in range(3):
            cols = slice(n * D + first * HD, n * D + first * HD + width)
            part = q_ref[:, n * width : (n + 1) * width].astype(F32)
            gqkv_ref[:, cols] = part
            prod = part * wqkv_ref[:, cols].astype(F32)
            for k in range(0, width, 128):
                acc += prod[:, k : k + 128]
    ggain_ref[...] = jnp.sum(acc.T, axis=0, keepdims=True) / gain_ref[...]
    gout_ref[...] = e_ref[...].astype(F32)
    gdec_ref[...] = edec_ref[0:C].astype(F32)


VM = pl.BlockSpec(memory_space=pltpu.VMEM)
ANY = pl.BlockSpec(memory_space=pl.ANY)
SDS = jax.ShapeDtypeStruct
DMA = pltpu.SemaphoreType.DMA


SM = pl.BlockSpec(memory_space=pltpu.SMEM)


def sum_bufs(plan):
    rows, lanes, by_lanes, rp, lp, _ = plan
    rows, lanes = (rows, lanes // 2) if by_lanes else (rows // 2, lanes)
    band = rows // 8
    shapes = [(rows, lanes), (rows, lanes), (8, band, lanes), (band, lanes)]
    shapes.append((8, band // rp, lanes // lp))
    return [pltpu.VMEM(s, BF16) for s in shapes]


def fused_call(x, pts_t, slots, weights, counts, cells, gain, w_qkv, w_out, w_dec_t):
    def vm(*shape, dtype=BF16):
        return pltpu.VMEM(shape, dtype)

    return pl.pallas_call(
        fused_kernel,
        out_shape=(
            SDS(x.shape, BF16), SDS((768, D), BF16), SDS((D, 768), BF16), SDS((D, 384), BF16),
            SDS((D, 384), BF16), SDS((ER, D), BF16),
        ),
        in_specs=[ANY, VM, VM, VM, SM, VM, VM, ANY, ANY, VM],
        out_specs=(ANY, VM, VM, VM, VM, VM),
        scratch_shapes=[
            vm(2, 48, 24, D), vm(D, 3 * D), vm(D, D), DMA((3,)), DMA((3,)),
            vm(7, C, CAP), vm(BANDS, C, CAP), DMA((7,)), DMA((7,)),
            vm(768, D), vm(768, D), vm(768, D), DMA((8,)),
            vm(TOK, D), vm(TOK, D), vm(TOK, 3 * D),
            vm(TOK, 4 * WT), vm(TOK, 2 * WT), vm(TOK, 2 * WT), vm(TOK, D),
            vm(256, BANDS * CAP), vm(9 * C, BANDS * CAP), vm(C, TOK), vm(TOK, D, dtype=F32),
            vm(TOK, D), vm(TOK, D), vm(TOK, D), vm(HALF, D, dtype=F32),
            vm(D, 768), vm(D, 384), vm(D, 384), vm(ER, D),
            *sum_bufs(PLAN_4), *sum_bufs(PLAN_2), *sum_bufs(PLAN_2), *sum_bufs(PLAN_E),
            DMA((2, 26)), DMA((2, 26)), DMA((2, 26)), DMA((2, 26)),
        ],
        compiler_params=pltpu.CompilerParams(
            vmem_limit_bytes=62 << 20, collective_id=0, has_side_effects=True
        ),
        name="fused",
    )(x, pts_t, slots, weights, counts, cells, gain, w_qkv, w_out, w_dec_t)


def place_call(gx, arriving, qa, qb, qc, e, w_qkv, gain):
    def rows(lanes):
        return pl.BlockSpec((128, lanes), lambda i: (i, 0))

    grid_rows = pl.BlockSpec((2, 12, 24, D), lambda i: (0, i, 0, 0))
    across = pl.BlockSpec((1, 128), lambda i: (0, i))
    return pl.pallas_call(
        place_kernel,
        grid=(4,),
        out_shape=(
            SDS(gx.shape, BF16), SDS((D, 3 * D), F32), SDS((D, D), F32), SDS((C, D), F32),
            SDS((1, D), F32),
        ),
        in_specs=[
            grid_rows, pl.BlockSpec((192, D), lambda i: (i, 0)), rows(768), rows(384), rows(384),
            rows(D), pl.BlockSpec((128, D), lambda i: (4, 0)), rows(3 * D), across,
        ],
        out_specs=(grid_rows, rows(3 * D), rows(D), pl.BlockSpec((C, D), lambda i: (0, 0)), across),
        compiler_params=pltpu.CompilerParams(vmem_limit_bytes=60 << 20),
        name="place",
    )(gx, arriving, qa, qb, qc, e, e, w_qkv, gain)


def body(
    block_input, gain, w_qkv, w_out, w_dec, g_points, slot_point, slot_cell, slot_weight, pair_count
):
    parts = fused_call(
        block_input, g_points.T, slot_point, slot_weight, pair_count, slot_cell, gain[None],
        w_qkv, w_out, w_dec.T,
    )
    grad_x, g_qkv, g_out, g_dec, g_gain = place_call(*parts, w_qkv, gain[None])
    return (grad_x, g_qkv, g_out, g_dec.T, g_gain[0])


def solution(mesh):
    placed = (
        P(None, "lat", "lon", None),
        P(),
        P(),
        P(),
        P(),
        P(("lat", "lon"), None),
        P(("lat", "lon"), None),
        P(("lat", "lon"), None),
        P(("lat", "lon"), None),
        P(("lat", "lon")),
    )
    return jax.shard_map(
        body,
        mesh=mesh,
        in_specs=placed,
        out_specs=(P(None, "lat", "lon", None), P(), P(), P(), P()),
        check_vma=False,
    )
```
